32 devices in a mesh: dp: 8 (over z, y), blk: 4 (over x, core).
Axes of the slice: x: 2, y: 2, z: 4, core: 2. Of those that a mesh axis runs over, the one named last changes fastest.
Arguments:
- tokens: bfloat16 [8, 2048, 768], P('dp', 'blk'), may hold values from -6 to 6
- cotangent: bfloat16 [8, 2048, 768], P('dp', 'blk'), may hold values from -6 to 6
- segments: int32 [8, 2048], P('dp', 'blk'), may hold values from 0 to 3, as said below
- padding: int32 [8, 2048], P('dp', 'blk'), may hold values from 0 to 1, as said below
- drop_keep: int32 [2, 8, 4], P(None, 'dp'), may hold values 0 or 1
- ln1_gain: bfloat16 [768], replicated, may hold values from 0.5 to 1.5
- ln1_bias: bfloat16 [768], replicated, may hold values from -3 to 3
- qkv_weight: bfloat16 [768, 2304], replicated, may hold values from -0.3125 to 0.3125
- qv_bias: bfloat16 [1536], replicated, may hold values from -3 to 3
- proj_weight: bfloat16 [768, 768], replicated, may hold values from -0.625 to 0.625
- proj_bias: bfloat16 [768], replicated, may hold values from -3 to 3
- ln2_gain: bfloat16 [768], replicated, may hold values from 0.5 to 1.5
- ln2_bias: bfloat16 [768], replicated, may hold values from -3 to 3
- fc1_weight: bfloat16 [768, 3072], replicated, may hold values from -0.21875 to 0.21875
- fc1_bias: bfloat16 [3072], replicated, may hold values from -3 to 3
- fc2_weight: bfloat16 [3072, 768], replicated, may hold values from -0.109375 to 0.109375
- fc2_bias: bfloat16 [768], replicated, may hold values from -3 to 3
Outputs:
- layer_output: bfloat16 [8, 2048, 768], P('dp', 'blk')
- tokens_grad: bfloat16 [8, 2048, 768], P('dp', 'blk')
- ln1_gain_grad: float32 [768], P(('dp', 'blk'))
- ln1_bias_grad: float32 [768], P(('dp', 'blk'))
- qkv_weight_grad: float32 [768, 2304], P(('dp', 'blk'))
- qv_bias_grad: float32 [1536], P(('dp', 'blk'))
- proj_weight_grad: float32 [768, 768], P(('dp', 'blk'))
- proj_bias_grad: float32 [768], P(('dp', 'blk'))
- ln2_gain_grad: float32 [768], P(('dp', 'blk'))
- ln2_bias_grad: float32 [768], P(('dp', 'blk'))
- fc1_weight_grad: float32 [768, 3072], P(('dp', 'blk'))
- fc1_bias_grad: float32 [3072], P(('dp', 'blk'))
- fc2_weight_grad: float32 [3072, 768], P(('dp', 'blk'))
- fc2_bias_grad: float32 [768], P(('dp', 'blk'))
The draws below stay inside these ranges and needn't reach their ends.
Inputs may be any that keep to these rules, and one draw needn't show every extreme that they name: `segments`: each row holds 4 images numbered 0 to 3 in order of position; image 1 covers at least the positions 511 to 1536. `padding`: padding is a run of one or more positions at the end of each row; it carries segment 3, the number of the row's last image.
All inputs are finite; a program needn't handle non-finite values. No bound on the sum of `drop_keep` on one device may be relied on, other than what follows from the above.
Results may differ from the reference program's by a relative error of at most 0.015.
Values may be sent and summed in bfloat16 or wider, within the bound.
No kernel may reach another device: no remote copies, remote signals or barrier semaphores. Data moves between devices by JAX's collectives and lax.ppermute only.
A program may use at most 192 MiB of HBM per device.

```python
import jax
import jax.numpy as jnp
from jax import lax

D = 768
HEAD_DIM = 64
FF = 3072
BLK = 512
SEGS = 4
ROW_LEN = 2048
ROWS = 8
N_BLK = 4


def row_layout(key):
    first_key, second_key, third_key, fourth_key = jax.random.split(key, 4)
    least_span = (N_BLK - 2) * BLK + 2
    extra_len = jax.random.randint(first_key, (ROWS, 1), 0, BLK // 4 + 1)
    shift_len = jax.random.randint(second_key, (ROWS, 1), 0, extra_len + 1)
    begin_at = BLK - 1 - shift_len
    finish = begin_at + least_span + extra_len
    after_len = ROW_LEN - finish
    after_count = SEGS - 2
    spread_len = after_len // (4 * after_count)
    jitter = jax.random.randint(third_key, (ROWS, SEGS), -spread_len, spread_len + 1)
    places = jnp.arange(ROW_LEN, dtype=jnp.int32)[None, :]
    segments = (places >= begin_at).astype(jnp.int32) + (places >= finish).astype(jnp.int32)
    last_cut = finish
    for index in range(SEGS - 3):
        last_cut = finish + (index + 1) * after_len // after_count + jitter[:, index:index + 1]
        segments = segments + (places >= last_cut).astype(jnp.int32)
    last_len = ROW_LEN - last_cut
    tail_len = jax.random.randint(fourth_key, (ROWS, 1), 1, last_len // 2 + 1)
    padding = (places < ROW_LEN - tail_len).astype(jnp.int32)
    return (segments, padding)


def draw_segments(key, part):
    shared = row_layout(key)
    return shared[0]


def draw_padding(key, part):
    shared = row_layout(key)
    return shared[1]


def with_ends(values, stream_key, least, high):
    spot = [jax.random.randint(jax.random.fold_in(stream_key, axis), (), 0, length) for axis, length in enumerate(values.shape)]
    main_axis = values.shape.index(max(values.shape))
    beside = spot[:main_axis] + [(spot[main_axis] + 1) % values.shape[main_axis]] + spot[main_axis + 1:]
    return values.at[tuple(spot)].set(least).at[tuple(beside)].set(high)


def shard_levels(rng, dims, shards, least, high):
    factor_of = 1.0
    for dim, parts in shards:
        draws = jax.random.uniform(jax.random.fold_in(jax.random.fold_in(rng, 6), dim), (parts,), jnp.float32, least / len(shards), high / len(shards))
        factor_of = factor_of * jnp.repeat(jnp.exp(draws), dims[dim] // parts).reshape((-1,) + (1,) * (len(dims) - 1 - dim))
    return factor_of


def scatter_about(key, dims, deviation, reach, shards=(), kind=jnp.bfloat16):
    factor_of = shard_levels(key, dims, shards, -0.22, 0.18) if shards else 1.0
    array = jax.random.normal(key, dims, jnp.float32) * deviation * factor_of
    return jnp.minimum(jnp.maximum(array, -reach), reach).astype(kind)


def setup_inputs(seed: int = 0) -> dict:
    keys = jax.random.split(jax.random.key(seed), 18)
    return {
        "tokens": scatter_about(keys[0], (ROWS, ROW_LEN, D), 1.0, 6.0, ((0, 8), (1, 4))),
        "cotangent": scatter_about(keys[1], (ROWS, ROW_LEN, D), 1.0, 6.0, ((0, 8), (1, 4))),
        "segments": draw_segments(jax.random.fold_in(keys[17], 71), 0),
        "padding": draw_padding(jax.random.fold_in(keys[17], 71), 0),
        "drop_keep": with_ends((jax.random.randint(keys[4], (2, ROWS, SEGS), 0, 10) < 9).astype(jnp.int32), jax.random.fold_in(keys[4], 1), 0, 1),
        "ln1_gain": jnp.clip(1.0 + 0.1 * jax.random.normal(keys[5], (D,), jnp.float32), 0.5, 1.5).astype(jnp.bfloat16),
        "ln1_bias": scatter_about(keys[6], (D,), 0.5, 3.0),
        "qkv_weight": scatter_about(keys[7], (D, 3 * D), (D // 2) ** -0.5, 0.3125),
        "qv_bias": scatter_about(keys[8], (2 * D,), 0.5, 3.0),
        "proj_weight": scatter_about(keys[9], (D, D), (D // 8) ** -0.5, 0.625),
        "proj_bias": scatter_about(keys[10], (D,), 0.5, 3.0),
        "ln2_gain": jnp.clip(1.0 + 0.1 * jax.random.normal(keys[11], (D,), jnp.float32), 0.5, 1.5).astype(jnp.bfloat16),
        "ln2_bias": scatter_about(keys[12], (D,), 0.5, 3.0),
        "fc1_weight": scatter_about(keys[13], (D, FF), D ** -0.5, 0.21875),
        "fc1_bias": scatter_about(keys[14], (FF,), 0.5, 3.0),
        "fc2_weight": scatter_about(keys[15], (FF, D), FF ** -0.5, 0.109375),
        "fc2_bias": scatter_about(keys[16], (D,), 0.5, 3.0),
    }


@jax.custom_vjp
def low(v):
    return lax.optimization_barrier(v.astype(jnp.bfloat16)).astype(jnp.float32)

@jax.custom_vjp
def low_back(v):
    return v

def low_keep(v):
    return (low(v), None)

def low_pass(kept, grad):
    return (grad,)

def back_keep(v):
    return (v, None)

def back_low(kept, grad):
    return (low(grad),)
low.defvjp(low_keep, low_pass)
low_back.defvjp(back_keep, back_low)
highest = lax.Precision.HIGHEST
epsilon = 1e-06
keep_rate = 0.9
attn_scale = 0.125
negative = -1e+30
row_group = 1

def normalize(values, ln_gain, ln_bias):
    center = values - lax.optimization_barrier(jnp.mean(values, -1, keepdims=True))
    spread = lax.optimization_barrier(jnp.mean(center * center, -1, keepdims=True))
    return center * lax.rsqrt(spread + epsilon) * ln_gain + ln_bias

def smooth(values):
    return jax.nn.gelu(values, approximate=False)

def token_keep(drop_keep, segments):
    levels = jnp.arange(drop_keep.shape[2], dtype=jnp.int32)
    matches = (segments[None, :, :, None] == levels).astype(jnp.float32)
    flags = drop_keep.astype(jnp.float32)[:, :, None, :]
    return lax.optimization_barrier(jnp.sum(matches * flags, -1)) / keep_rate

def forward_rows(source, segments, padding, keep_attn, keep_mlp, weights):
    gain_one, bias_one, qkv_w, qv_b, proj_w, proj_b, gain_two, bias_two, up_w, up_b, down_w, down_b = weights
    batch_rows, length, model_dim = source.shape
    head_count = model_dim // HEAD_DIM
    head_shape = (batch_rows, length, head_count, HEAD_DIM)
    normed = low(normalize(source, gain_one, bias_one))
    full_bias = jnp.concatenate([qv_b[:model_dim], jnp.zeros((model_dim,), jnp.float32), qv_b[model_dim:]])
    packed = low(low_back(jnp.einsum('gld,de->gle', normed, qkv_w, precision=highest) + full_bias))
    queries = packed[..., :model_dim].reshape(head_shape)
    key_heads = packed[..., model_dim:2 * model_dim].reshape(head_shape)
    value_heads = packed[..., 2 * model_dim:].reshape(head_shape)
    raw_scores = jnp.einsum('gqhe,gkhe->ghqk', queries, key_heads, precision=highest)
    allowed = (segments[:, :, None] == segments[:, None, :]) & ((padding[:, None, :] == 1) | (padding[:, :, None] == 0))
    scores = low_back(jnp.where(allowed[:, None], raw_scores * attn_scale, negative))
    probs = low(jax.nn.softmax(scores, -1))
    mixture = jnp.einsum('ghqk,gkhe->gqhe', probs, value_heads, precision=highest).reshape(batch_rows, length, model_dim)
    mixture = low(low_back(mixture))
    branch = low_back(jnp.einsum('gld,de->gle', mixture, proj_w, precision=highest) + proj_b)
    middle = source + keep_attn[..., None] * branch
    normed_two = low(normalize(middle, gain_two, bias_two))
    hidden = low_back(jnp.einsum('gld,df->glf', normed_two, up_w, precision=highest) + up_b)
    active = low(smooth(hidden))
    output = low_back(jnp.einsum('glf,fd->gld', active, down_w, precision=highest) + down_b)
    return middle + keep_mlp[..., None] * output

def reference(tokens, cotangent, segments, padding, drop_keep, ln1_gain, ln1_bias, qkv_weight, qv_bias, proj_weight, proj_bias, ln2_gain, ln2_bias, fc1_weight, fc1_bias, fc2_weight, fc2_bias):
    weights = tuple((operand.astype(jnp.float32) for operand in (ln1_gain, ln1_bias, qkv_weight, qv_bias, proj_weight, proj_bias, ln2_gain, ln2_bias, fc1_weight, fc1_bias, fc2_weight, fc2_bias)))
    keep_both = token_keep(drop_keep, segments)
    step_count = tokens.shape[0] // row_group

    def grouped(operand):
        return operand.reshape((step_count, row_group) + operand.shape[1:])
    scanned = (grouped(tokens), grouped(cotangent), grouped(segments), grouped(padding), grouped(keep_both[0]), grouped(keep_both[1]))

    def advance(totals, members):
        block_x, block_cot, block_seg, block_pad, block_attn, block_mlp = members

        def forward(source, params):
            return forward_rows(source, block_seg, block_pad, block_attn, block_mlp, params)
        result, pullback = jax.vjp(forward, block_x.astype(jnp.float32), weights)
        grad_x, grad_w = pullback(block_cot.astype(jnp.float32))
        totals = jax.tree.map(lambda left, right: left + right, totals, grad_w)
        return (totals, (result.astype(jnp.bfloat16), grad_x.astype(jnp.bfloat16)))
    initial = jax.tree.map(jnp.zeros_like, weights)
    totals, (outputs, grads_x) = lax.scan(advance, initial, scanned)
    layer_output = outputs.reshape(tokens.shape)
    tokens_grad = grads_x.reshape(tokens.shape)
    return (layer_output, tokens_grad, totals[0], totals[1], totals[2], totals[3], totals[4], totals[5], totals[6], totals[7], totals[8], totals[9], totals[10], totals[11])
```

```python
from functools import partial

import jax
import jax.numpy as jnp
from jax import lax
from jax.experimental import pallas as pl
from jax.experimental.pallas import tpu as pltpu
from jax.sharding import PartitionSpec as P

HEAD_DIM = 64
F32 = jnp.float32
BF16 = jnp.bfloat16
epsilon = 1e-06
keep_rate = 0.9
attn_scale = 0.125
negative = -1e30
PAD_CLASS = 4
TILE = 256
NN = ((1,), (0,))
NT = ((1,), (1,))
TN = ((0,), (0,))


def mm(left, right, dims=NN):
    return lax.dot_general(left, right, (dims, ((), ())), preferred_element_type=F32)


def pair_rows(head):
    return slice(head * HEAD_DIM, (head + 1) * HEAD_DIM)


def pair_lanes(pair):
    return slice(pair * 128, (pair + 1) * 128)


def load_masked(k_ref, q_ref, kmask_ref, qmask_ref, kx, qx, qt, heads):
    lane = lax.broadcasted_iota(jnp.int32, (k_ref.shape[0], 128), 1)
    low = kmask_ref[:, :128]
    high = kmask_ref[:, 128:]
    for pair in range(heads // 2):
        keys = k_ref[:, pair_lanes(pair)]
        kx[2 * pair] = jnp.where(lane < HEAD_DIM, keys, high)
        kx[2 * pair + 1] = jnp.where(lane < HEAD_DIM, low, keys)
        turned = (q_ref[:, pair_lanes(pair)].astype(F32) * attn_scale).T.astype(BF16)
        if qt is not None:
            qt[pair_lanes(pair), :] = turned
        qx[2 * pair, :HEAD_DIM, :] = turned[:HEAD_DIM]
        qx[2 * pair, HEAD_DIM:, :] = qmask_ref[...]
        qx[2 * pair + 1, :HEAD_DIM, :] = qmask_ref[...]
        qx[2 * pair + 1, HEAD_DIM:, :] = turned[HEAD_DIM:]


def forward_kernel(
    act_ref, q_ref, k_ref, v_ref, kmask_ref, qmask_ref, o_ref, ot_ref, lse_ref, kx, qx, vt, top, total, acc, *, heads
):
    queries, keys = q_ref.shape[0], k_ref.shape[0]
    load_masked(k_ref, q_ref, kmask_ref, qmask_ref, kx, qx, None, heads)
    for pair in range(heads // 2):
        vt[pair_lanes(pair), :] = v_ref[:, pair_lanes(pair)].astype(F32).T.astype(BF16)
    for q_tile in range(queries // TILE):
        top[...] = jnp.full_like(top, -1e29)
        total[...] = jnp.zeros_like(total)
        acc[...] = jnp.zeros_like(acc)
        at = slice(q_tile * TILE, (q_tile + 1) * TILE)

        def body(k_tile, carry):
            @pl.when(act_ref[q_tile, k_tile] > 0)
            def _():
                span = pl.ds(pl.multiple_of(k_tile * TILE, TILE), TILE)
                scores = [mm(kx[h, span, :], qx[h, :, at]) for h in range(heads)]
                old = [top[h : h + 1, :] for h in range(heads)]
                new = [jnp.maximum(old[h], jnp.max(scores[h], 0, keepdims=True)) for h in range(heads)]
                decay = [jnp.exp(old[h] - new[h]) for h in range(heads)]
                weights = [jnp.exp(scores[h] - new[h]) for h in range(heads)]
                added = [mm(vt[pair_rows(h), span], weights[h].astype(BF16)) for h in range(heads)]
                for h in range(heads):
                    top[h : h + 1, :] = new[h]
                    total[h : h + 1, :] = decay[h] * total[h : h + 1, :] + jnp.sum(weights[h], 0, keepdims=True)
                    acc[pair_rows(h), :] = decay[h] * acc[pair_rows(h), :] + added[h]

            return carry

        lax.fori_loop(0, keys // TILE, body, 0)
        for h in range(heads):
            acc[pair_rows(h), :] = acc[pair_rows(h), :] / total[h : h + 1, :]
            lse_ref[h : h + 1, at] = top[h : h + 1, :] + jnp.log(total[h : h + 1, :])
        ot_ref[:, at] = acc[...].astype(BF16)
        for pair in range(heads // 2):
            o_ref[at, pair_lanes(pair)] = acc[pair_lanes(pair), :].T.astype(BF16)


def attend(act, q, k, v, kmask, qmask):
    queries, width = q.shape
    keys = k.shape[0]
    heads = width // HEAD_DIM
    vm = pl.BlockSpec(memory_space=pltpu.VMEM)
    return pl.pallas_call(
        partial(forward_kernel, heads=heads),
        out_shape=(
            jax.ShapeDtypeStruct((queries, width), BF16),
            jax.ShapeDtypeStruct((width, queries), BF16),
            jax.ShapeDtypeStruct((8, queries), F32),
        ),
        in_specs=[pl.BlockSpec(memory_space=pltpu.SMEM)] + [vm] * 5,
        out_specs=(vm, vm, vm),
        scratch_shapes=[
            pltpu.VMEM((heads, keys, 128), BF16),
            pltpu.VMEM((heads, 128, queries), BF16),
            pltpu.VMEM((width, keys), BF16),
            pltpu.VMEM((8, TILE), F32),
            pltpu.VMEM((8, TILE), F32),
            pltpu.VMEM((width, TILE), F32),
        ],
        compiler_params=pltpu.CompilerParams(vmem_limit_bytes=40 * 2**20),
        cost_estimate=pl.CostEstimate(flops=9 * 10**9, bytes_accessed=10**7, transcendentals=8 * 10**6),
        name="attention_forward",
    )(act, q, k, v, kmask, qmask)


def backward_kernel(
    act_ref,
    q_ref,
    k_ref,
    v_ref,
    kmask_ref,
    qmask_ref,
    ot_ref,
    lse_ref,
    do_ref,
    dq_ref,
    dk_ref,
    dv_ref,
    kx,
    qx,
    kt,
    qt,
    dox,
    dot,
    delta,
    dq_sum,
    dk_sum,
    dv_sum,
    *,
    heads,
):
    queries, keys = q_ref.shape[0], k_ref.shape[0]
    load_masked(k_ref, q_ref, kmask_ref, qmask_ref, kx, qx, qt, heads)
    zero = jnp.zeros((HEAD_DIM, queries), BF16)
    for pair in range(heads // 2):
        lanes = pair_lanes(pair)
        kt[lanes, :] = k_ref[:, lanes].astype(F32).T.astype(BF16)
        turned = do_ref[:, lanes].astype(F32).T
        product = turned * ot_ref[lanes, :].astype(F32)
        delta[2 * pair : 2 * pair + 1, :] = jnp.sum(product[:HEAD_DIM], 0, keepdims=True)
        delta[2 * pair + 1 : 2 * pair + 2, :] = jnp.sum(product[HEAD_DIM:], 0, keepdims=True)
        turned = turned.astype(BF16)
        dot[lanes, :] = turned
        dox[2 * pair, :HEAD_DIM, :] = turned[:HEAD_DIM]
        dox[2 * pair, HEAD_DIM:, :] = zero
        dox[2 * pair + 1, :HEAD_DIM, :] = zero
        dox[2 * pair + 1, HEAD_DIM:, :] = turned[HEAD_DIM:]
    dq_sum[...] = jnp.zeros_like(dq_sum)
    dk_sum[...] = jnp.zeros_like(dk_sum)
    dv_sum[...] = jnp.zeros_like(dv_sum)
    group = 3 if heads % 3 == 0 else 2
    for q_tile in range(queries // TILE):
        at = slice(q_tile * TILE, (q_tile + 1) * TILE)

        def body(k_tile, carry):
            @pl.when(act_ref[q_tile, k_tile] > 0)
            def _():
                span = pl.ds(pl.multiple_of(k_tile * TILE, TILE), TILE)
                for first in range(0, heads, group):
                    hs = range(first, first + group)
                    scores = {h: mm(kx[h, span, :], qx[h, :, at]) for h in hs}
                    dp = {h: mm(v_ref[span, pair_lanes(h // 2)], dox[h, :, at]) for h in hs}
                    probs = {h: jnp.exp(scores[h] - lse_ref[h : h + 1, at]) for h in hs}
                    rounded = {h: probs[h].astype(BF16) for h in hs}
                    ds = {h: (probs[h] * (dp[h] - delta[h : h + 1, at])).astype(BF16) for h in hs}
                    dv = {h: mm(dot[pair_rows(h), at], rounded[h], NT) for h in hs}
                    dk = {h: mm(qt[pair_rows(h), at], ds[h], NT) for h in hs}
                    dq = {h: mm(kt[pair_rows(h), span], ds[h]) for h in hs}
                    for h in hs:
                        dv_sum[pair_rows(h), span] += dv[h]
                        dk_sum[pair_rows(h), span] += dk[h]
                        dq_sum[pair_rows(h), at] += dq[h]

            return carry

        lax.fori_loop(0, keys // TILE, body, 0)
    for pair in range(heads // 2):
        lanes = pair_lanes(pair)
        dq_ref[:, lanes] = (dq_sum[lanes, :] * attn_scale).T.astype(BF16)
        dk_ref[:, lanes] = dk_sum[lanes, :].T.astype(BF16)
        dv_ref[:, lanes] = dv_sum[lanes, :].T.astype(BF16)


def attend_back(act, q, k, v, kmask, qmask, ot, lse, do):
    queries, width = q.shape
    keys = k.shape[0]
    heads = width // HEAD_DIM
    vm = pl.BlockSpec(memory_space=pltpu.VMEM)
    return pl.pallas_call(
        partial(backward_kernel, heads=heads),
        out_shape=(
            jax.ShapeDtypeStruct((queries, width), BF16),
            jax.ShapeDtypeStruct((keys, width), BF16),
            jax.ShapeDtypeStruct((keys, width), BF16),
        ),
        in_specs=[pl.BlockSpec(memory_space=pltpu.SMEM)] + [vm] * 8,
        out_specs=(vm, vm, vm),
        scratch_shapes=[
            pltpu.VMEM((heads, keys, 128), BF16),
            pltpu.VMEM((heads, 128, queries), BF16),
            pltpu.VMEM((width, keys), BF16),
            pltpu.VMEM((width, queries), BF16),
            pltpu.VMEM((heads, 128, queries), BF16),
            pltpu.VMEM((width, queries), BF16),
            pltpu.VMEM((8, queries), F32),
            pltpu.VMEM((width, queries), F32),
            pltpu.VMEM((width, keys), F32),
            pltpu.VMEM((width, keys), F32),
        ],
        compiler_params=pltpu.CompilerParams(vmem_limit_bytes=48 * 2**20),
        cost_estimate=pl.CostEstimate(flops=23 * 10**9, bytes_accessed=2 * 10**7, transcendentals=8 * 10**6),
        name="attention_backward",
    )(act, q, k, v, kmask, qmask, ot, lse, do)


def masks_of(query_code, key_code):
    keys = key_code.shape[0]
    classes = jnp.arange(HEAD_DIM, dtype=jnp.int32)
    one_hot = (key_code[:, None] == classes[None, :]).astype(BF16)
    kmask = jnp.concatenate([one_hot, jnp.zeros((keys, 128), BF16), one_hot], 1)
    code, kind = query_code[None, :], classes[:, None]
    seen = (code == kind) | ((code == PAD_CLASS) & (kind == PAD_CLASS - 1)) | (kind > PAD_CLASS)
    qmask = jnp.where(seen, 0.0, negative).astype(BF16)
    seg_q = jnp.minimum(query_code, PAD_CLASS - 1).reshape(-1, TILE)
    seg_k = jnp.minimum(key_code, PAD_CLASS - 1).reshape(-1, TILE)
    meets = (seg_q.min(1)[:, None] <= seg_k.max(1)[None, :]) & (seg_q.max(1)[:, None] >= seg_k.min(1)[None, :])
    return kmask, qmask, meets.astype(jnp.int32)


def centre(values):
    shifted = values - jnp.mean(values, -1, keepdims=True)
    spread = jnp.mean(shifted * shifted, -1, keepdims=True)
    scale = lax.rsqrt(spread + epsilon)
    return shifted * scale, scale


def norm_back(unit, scale, grad):
    return (grad - jnp.mean(grad, -1, keepdims=True) - unit * jnp.mean(grad * unit, -1, keepdims=True)) * scale


def swap_halves(rows):
    half = rows.shape[0] // 2
    return jnp.concatenate([rows[half:], rows[:half]], 0)


def pick(array, index, dim):
    return lax.dynamic_index_in_dim(array, index, dim, keepdims=False)


class Links:
    def __init__(self, mesh):
        self.dp, self.blk = mesh.shape["dp"], mesh.shape["blk"]
        self.bits = self.dp.bit_length() - 1

    def core(self, value):
        return lax.ppermute(value, "blk", [(i, i ^ 1) for i in range(self.blk)])

    def side(self, value):
        return lax.ppermute(value, "blk", [(i, i ^ 2) for i in range(self.blk)])

    def cross(self, value, step):
        if step == "x":
            return self.side(value)
        return lax.ppermute(value, "dp", [(i, i ^ (1 << step)) for i in range(self.dp)])

    def bit(self, step):
        if step == "x":
            return lax.axis_index("blk") // 2
        return (lax.axis_index("dp") >> step) & 1

    def scatter(self, array, dims, order):
        dims = list(dims)
        for count, step in enumerate(order):
            place = dims.index(step)
            mine = self.bit(step)
            arrived = self.cross(pick(array, 1 - mine, place), step)
            array = pick(array, mine, place).astype(F32) + arrived.astype(F32)
            if count < len(order) - 1:
                array = array.astype(BF16)
            dims.pop(place)
        return array

    def swap(self, value):
        top = self.dp // 2
        pairs = []
        for d in range(self.dp):
            for b in range(self.blk):
                high, core = d // top, b % 2
                pairs.append((d * self.blk + b, (d % top + core * top) * self.blk + (b - core + high)))
        return lax.ppermute(value, ("dp", "blk"), pairs)


def local(
    links,
    tokens,
    cotangent,
    segments,
    padding,
    drop_keep,
    ln1_gain,
    ln1_bias,
    qkv_weight,
    qv_bias,
    proj_weight,
    proj_bias,
    ln2_gain,
    ln2_bias,
    fc1_weight,
    fc1_bias,
    fc2_weight,
    fc2_bias,
):
    _, block_len, width = tokens.shape
    half = width // 2
    hidden_half = fc1_weight.shape[1] // 2
    core = lax.axis_index("blk") % 2
    me = lax.axis_index("blk")
    n = links.dp
    owners = n * links.blk

    mine = tokens[0]
    far = links.side(mine)
    other = links.core(mine)
    far_other = links.core(far)
    near_tokens = jnp.concatenate([mine, other], 0)
    far_tokens = jnp.concatenate([far, far_other], 0)
    grad_mine = cotangent[0]
    grad_out = jnp.concatenate([grad_mine, links.core(grad_mine)], 0).astype(F32)
    code = jnp.where(padding == 1, segments, PAD_CLASS).reshape(1, block_len)
    codes = lax.all_gather(code, "blk", axis=0, tiled=True)
    key_code = jnp.concatenate([pick(codes, me ^ i, 0) for i in range(links.blk)], 0)
    query_code = key_code[: 2 * block_len]
    kmask, qmask, act = masks_of(query_code, key_code)

    flags = drop_keep[:, 0, :].astype(F32)
    matches = (jnp.minimum(query_code, PAD_CLASS - 1)[:, None] == jnp.arange(flags.shape[1])).astype(F32)
    keep_attn = jnp.sum(matches * flags[0], 1, keepdims=True) / keep_rate
    keep_mlp = jnp.sum(matches * flags[1], 1, keepdims=True) / keep_rate

    w_qkv = pick(qkv_weight.reshape(width, 3, 2, half), core, 2).reshape(width, 3 * half)
    qv = pick(qv_bias.astype(F32).reshape(2, 2, half), core, 1)
    b_qkv = jnp.concatenate([qv[0], jnp.zeros((half,), F32), qv[1]])
    w_proj = proj_weight.reshape(2, half, width)
    w_proj = jnp.concatenate([pick(w_proj, core, 0), pick(w_proj, 1 - core, 0)], 0)
    w_up = pick(fc1_weight.reshape(width, 2, hidden_half), core, 1)
    b_up = pick(fc1_bias.astype(F32).reshape(2, hidden_half), core, 0)
    w_down = pick(fc2_weight.reshape(2, hidden_half, width), core, 0)

    gain_one, bias_one = ln1_gain.astype(F32), ln1_bias.astype(F32)
    gain_two, bias_two = ln2_gain.astype(F32), ln2_bias.astype(F32)

    source = near_tokens.astype(F32)
    near_normed = (centre(source)[0] * gain_one + bias_one).astype(BF16)
    near_packed = (mm(near_normed, w_qkv) + b_qkv).astype(BF16)
    far_normed = (centre(far_tokens.astype(F32))[0] * gain_one + bias_one).astype(BF16)
    far_packed = (mm(far_normed, w_qkv[:, half:]) + b_qkv[half:]).astype(BF16)
    q = near_packed[:, :half]
    k = jnp.concatenate([near_packed[:, half : 2 * half], far_packed[:, :half]], 0)
    v = jnp.concatenate([near_packed[:, 2 * half :], far_packed[:, half:]], 0)
    mixture, mixture_t, lse = attend(act, q, k, v, kmask, qmask)

    whole = jnp.concatenate([mixture, swap_halves(links.core(mixture))], 1)
    middle = source + keep_attn * (mm(whole, w_proj) + proj_bias.astype(F32))
    unit_two, scale_two = centre(middle)
    normed_two = (unit_two * gain_two + bias_two).astype(BF16)
    hidden = mm(normed_two, w_up) + b_up
    bell = 0.5 * (1.0 + lax.erf(hidden * (0.5**0.5)))
    active = (hidden * bell).astype(BF16)
    slope = bell + hidden * jnp.exp(-0.5 * hidden * hidden) * 0.3989422804014327
    down = mm(active, w_down)
    down_other = links.core(down[block_len:].astype(BF16)).astype(F32)
    result = middle[:block_len] + keep_mlp[:block_len] * (down[:block_len] + down_other + fc2_bias.astype(F32))
    layer_output = result.astype(BF16).reshape(tokens.shape)

    grad_down = (keep_mlp * grad_out).astype(BF16)
    d_down = mm(active, grad_down, TN).astype(BF16)
    grad_hidden = (mm(grad_down, w_down, NT) * slope).astype(BF16)
    d_up = mm(normed_two, grad_hidden, TN).astype(BF16)
    part = mm(grad_hidden, w_up, NT).astype(BF16)
    grad_normed_two = part.astype(F32) + swap_halves(links.core(part)).astype(F32)
    grad_middle = grad_out + norm_back(unit_two, scale_two, grad_normed_two * gain_two)
    grad_proj = (keep_attn * grad_middle).astype(BF16)
    d_proj = mm(mixture, grad_proj, TN).astype(BF16)
    grad_mixture = mm(grad_proj, w_proj[:half], NT).astype(BF16)
    dq, dk, dv = attend_back(act, q, k, v, kmask, qmask, mixture_t, lse, grad_mixture)

    rows = 2 * block_len
    near_grad = jnp.concatenate([dq, dk[:rows], dv[:rows]], 1)
    far_grad = jnp.concatenate([dk[rows:], dv[rows:]], 1)
    far_dx = mm(far_grad, w_qkv[:, half:], NT)
    near_dx = mm(near_grad, w_qkv, NT)
    far_sum = far_dx[:block_len] + links.core(far_dx[block_len:].astype(BF16)).astype(F32)
    across = links.side(far_sum.astype(BF16)).astype(F32)
    beside = links.core(near_dx[block_len:].astype(BF16)).astype(F32)
    grad_normed_one = near_dx[:block_len] + beside + across
    unit_one, scale_one = centre(source[:block_len])
    grad_source = norm_back(unit_one, scale_one, grad_normed_one * gain_one)
    tokens_grad = (grad_middle[:block_len] + grad_source).astype(BF16).reshape(tokens.shape)

    d_q = mm(near_normed, dq, TN).astype(BF16)
    both_normed = jnp.concatenate([near_normed, far_normed], 0)
    d_k = mm(both_normed, dk, TN).astype(BF16)
    d_v = mm(both_normed, dv, TN).astype(BF16)

    def ln_sums(weight, grad_weight, sums, gain, bias):
        weight = weight.astype(F32)
        each = weight * (grad_weight.astype(F32) - bias[:, None] * sums[None, :])
        return jnp.sum(each, 1) / gain, jnp.sum(weight * sums[None, :], 1)

    up_sums = jnp.sum(grad_hidden, 0, dtype=F32)
    q_sums = jnp.sum(dq, 0, dtype=F32)
    k_sums = jnp.sum(dk, 0, dtype=F32)
    v_sums = jnp.sum(dv, 0, dtype=F32)
    gain_two_grad, bias_two_grad = ln_sums(w_up, d_up, up_sums, gain_two, bias_two)
    gain_one_grad, bias_one_grad = ln_sums(
        w_qkv,
        jnp.concatenate([d_q, d_k, d_v], 1),
        jnp.concatenate([q_sums, k_sums, v_sums]),
        gain_one,
        bias_one,
    )

    def spread(value, parts=1):
        value = value.reshape(parts, -1)
        empty = jnp.zeros_like(value)
        first = jnp.where(core == 0, value, empty)
        last = jnp.where(core == 0, empty, value)
        return jnp.concatenate([first, last], 1).reshape(-1)

    smalls = (
        gain_one_grad,
        bias_one_grad,
        spread(jnp.concatenate([q_sums, v_sums]), 2),
        jnp.sum(grad_proj[:block_len], 0, dtype=F32),
        gain_two_grad,
        bias_two_grad,
        spread(up_sums),
        jnp.sum(grad_down[:block_len], 0, dtype=F32),
    )
    sizes = [value.shape[0] // owners for value in smalls]
    small = jnp.concatenate([value.reshape(owners, -1) for value in smalls], 1)
    small = small.reshape((2,) * links.bits + (2, 2, -1)).astype(BF16)

    bits = links.bits
    low = [bits - 1 - i for i in range(bits)]
    chip = low + ["x"]
    by_core = low[1:] + ["x", low[0]]
    tail = [s for s in low if s > 1][::-1]

    def across_rows(array, order):
        view = array.reshape((2,) * (bits + 1) + (-1, width))
        return links.swap(links.scatter(view, by_core, order))

    def across_columns(array, order):
        view = array.reshape((2,) * (bits + 1) + (2, width // owners, -1))
        kept = links.scatter(view, chip, order)
        sent = links.core(pick(kept, 1 - core, 0))
        kept = pick(kept, core, 0)
        return jnp.where(core == 0, jnp.concatenate([kept, sent], 1), jnp.concatenate([sent, kept], 1))

    down_grad = across_rows(d_down, ["x", 0, 1] + tail)
    up_grad = across_columns(d_up, [0, 1, "x"] + tail)
    proj_grad = across_rows(d_proj, [1, "x", 0] + tail)
    q_grad = across_columns(d_q, [0, 1, "x"] + tail)
    k_grad = across_columns(d_k, [1, "x", 0] + tail)
    v_grad = across_columns(d_v, ["x", 0, 1] + tail)
    kept = links.scatter(small, chip, [0, 1, "x"] + tail)
    small = pick(kept, core, 0) + links.core(pick(kept, 1 - core, 0))
    ends = [sum(sizes[: i + 1]) for i in range(len(sizes))]
    g1, b1, qvb, pb, g2, b2, u1, d2 = (small[end - size : end] for end, size in zip(ends, sizes))
    qkv_grad = jnp.concatenate([q_grad, k_grad, v_grad], 1)
    return (layer_output, tokens_grad, g1, b1, qkv_grad, qvb, proj_grad, pb, g2, b2, up_grad, u1, down_grad, d2)


def solution(mesh):
    both = P(("dp", "blk"))
    rows = P(("dp", "blk"), None)
    token = P("dp", "blk", None)
    whole = P()
    placed = (token, token, P("dp", "blk"), P("dp", "blk"), P(None, "dp", None)) + (whole,) * 12
    return jax.shard_map(
        partial(local, Links(mesh)),
        mesh=mesh,
        in_specs=placed,
        out_specs=(token, token, both, both, rows, both, rows, both, both, both, rows, both, rows, both),
        check_vma=False,
    )
```

```python
from functools import partial

import jax
import jax.numpy as jnp
from jax import lax
from jax.experimental import pallas as pl
from jax.experimental.pallas import tpu as pltpu
from jax.sharding import PartitionSpec as P

HEAD_DIM = 64
F32 = jnp.float32
BF16 = jnp.bfloat16
epsilon = 1e-06
keep_rate = 0.9
attn_scale = 0.125
negative = -1e30
PAD_CLASS = 4
TILE = 256
MIB = 2**20
FLOPS_PER_US = 1.0 * 10**9
BUDGET = {
    "near_forward": (28, 17),
    "far_forward": (28, 13),
    "mlp": (36, 21),
    "down_weight": (16, 5),
    "up_weight": (20, 5),
    "middle_backward": (16, 5),
    "proj_weight": (12, 1),
    "far_backward": (36, 16),
    "near_backward": (36, 20),
    "qkv_weight": (24, 8),
    "sum_half": (8, 2),
    "sum_last": (8, 1),
    "add_blocks": (8, 2),
    "token_gradient": (12, 2),
    "layer_output": (12, 2),
}
NN = ((1,), (0,))
NT = ((1,), (1,))
TN = ((0,), (0,))
VMEM = pl.BlockSpec(memory_space=pltpu.VMEM)
SMEM = pl.BlockSpec(memory_space=pltpu.SMEM)


def mm(left, right, dims=NN):
    return lax.dot_general(left, right, (dims, ((), ())), preferred_element_type=F32)


def rows_of(head):
    return slice(head * HEAD_DIM, (head + 1) * HEAD_DIM)


def lanes_of(pair):
    return slice(pair * 128, (pair + 1) * 128)


def centre(values):
    shifted = values - jnp.mean(values, -1, keepdims=True)
    spread = jnp.mean(shifted * shifted, -1, keepdims=True)
    scale = lax.rsqrt(spread + epsilon)
    return shifted * scale, scale


def norm_back(unit, scale, grad):
    return (grad - jnp.mean(grad, -1, keepdims=True) - unit * jnp.mean(grad * unit, -1, keepdims=True)) * scale


def call(kernel, name, outs, scratch, specs, out_specs=None, grid=None, prefetch=0, after=()):
    limit, cost = BUDGET[name]
    first = prefetch + len(specs)

    def ordered(*refs):
        kernel(*refs[:first], *refs[first + len(after) :])

    spec = pltpu.PrefetchScalarGridSpec(
        num_scalar_prefetch=prefetch,
        grid=grid or (1,),
        in_specs=list(specs) + [pl.BlockSpec(memory_space=pl.ANY)] * len(after),
        out_specs=out_specs or tuple(VMEM for _ in outs),
        scratch_shapes=scratch,
    )
    run = pl.pallas_call(
        ordered,
        out_shape=tuple(jax.ShapeDtypeStruct(shape, kind) for shape, kind in outs),
        grid_spec=spec,
        compiler_params=pltpu.CompilerParams(vmem_limit_bytes=limit * MIB),
        cost_estimate=pl.CostEstimate(flops=int(cost * FLOPS_PER_US), bytes_accessed=1, transcendentals=0),
        name=name,
    )
    return lambda *args: run(*args, *after)


def query_mask(code):
    kind = lax.broadcasted_iota(jnp.int32, (HEAD_DIM, code.shape[1]), 0).astype(F32)
    seen = (code == kind) | ((code == PAD_CLASS) & (kind == PAD_CLASS - 1)) | (kind > PAD_CLASS)
    return jnp.where(seen, 0.0, negative).astype(BF16)


def load_queries(qt_ref, code, qx, heads):
    mask = query_mask(code)
    for h in range(heads):
        own = slice(0, HEAD_DIM) if h % 2 == 0 else slice(HEAD_DIM, 128)
        rest = slice(HEAD_DIM, 128) if h % 2 == 0 else slice(0, HEAD_DIM)
        qx[h, own, :] = qt_ref[rows_of(h), :]
        qx[h, rest, :] = mask


def load_keys(k_ref, first, code, kx, heads):
    keys = k_ref.shape[0]
    kind = lax.broadcasted_iota(jnp.int32, (128, keys), 0).astype(F32)
    low = (kind == code).astype(F32).T.astype(BF16)
    high = (kind - HEAD_DIM == code).astype(F32).T.astype(BF16)
    lane = lax.broadcasted_iota(jnp.int32, (keys, 128), 1)
    for pair in range(heads // 2):
        slab = k_ref[:, first + pair * 128 : first + (pair + 1) * 128]
        kx[2 * pair] = jnp.where(lane < HEAD_DIM, slab, high)
        kx[2 * pair + 1] = jnp.where(lane < HEAD_DIM, low, slab)


def tile_ranges(code):
    image = jnp.minimum(code, float(PAD_CLASS - 1))
    cuts = [image[:, i : i + TILE] for i in range(0, code.shape[1], TILE)]
    return [(jnp.min(c), jnp.max(c)) for c in cuts]


def note_tiles(q_code, k_code, act):
    q_ranges, k_ranges = tile_ranges(q_code), tile_ranges(k_code)
    for i, (q_low, q_high) in enumerate(q_ranges):
        for j, (k_low, k_high) in enumerate(k_ranges):
            act[i, j] = ((q_low <= k_high) & (q_high >= k_low)).astype(jnp.int32)


def each_tile(act, queries, keys, body):
    for q_tile in range(queries // TILE):
        at = slice(q_tile * TILE, (q_tile + 1) * TILE)

        def step(k_tile, carry):
            @pl.when(act[q_tile, k_tile] > 0)
            def _():
                body(at, pl.ds(pl.multiple_of(k_tile * TILE, TILE), TILE))

            return carry

        lax.fori_loop(0, keys // TILE, step, 0)


def fold_keys(act, kx, qx, vt, top, total, acc, heads):
    def body(at, span):
        hs = range(heads)
        scores = [mm(kx[h, span, :], qx[h, :, at]) for h in hs]
        old = [top[h : h + 1, at] for h in hs]
        new = [jnp.maximum(old[h], jnp.max(scores[h], 0, keepdims=True)) for h in hs]
        decay = [jnp.exp(old[h] - new[h]) for h in hs]
        weights = [jnp.exp(scores[h] - new[h]) for h in hs]
        added = [mm(vt[rows_of(h), span], weights[h].astype(BF16)) for h in hs]
        for h in hs:
            top[h : h + 1, at] = new[h]
            total[h : h + 1, at] = decay[h] * total[h : h + 1, at] + jnp.sum(weights[h], 0, keepdims=True)
            acc[rows_of(h), at] = decay[h] * acc[rows_of(h), at] + added[h]

    each_tile(act, qx.shape[2], kx.shape[1], body)


def normed_rows(ref, at, gain, bias):
    return (centre(ref[at, :].astype(F32))[0] * gain + bias).astype(BF16)


def near_kernel(
    core_ref,
    mine_ref,
    other_ref,
    gain_ref,
    bias_ref,
    wq_ref,
    wk_ref,
    wv_ref,
    bq_ref,
    bv_ref,
    x_ref,
    normed_ref,
    w_ref,
    qt_ref,
    kv_ref,
    code_ref,
    top,
    total,
    acc,
    act,
    kx,
    qx,
    vt,
    *,
    heads,
):
    half = heads * HEAD_DIM
    block = mine_ref.shape[0] - 16
    gain, bias = gain_ref[...].astype(F32), bias_ref[...].astype(F32)
    bq, bv = bq_ref[...].astype(F32), bv_ref[...].astype(F32)
    w_ref[:, :half] = wq_ref[...]
    w_ref[:, half : 2 * half] = wk_ref[...]
    w_ref[:, 2 * half :] = wv_ref[...]
    for index, ref in enumerate((mine_ref, other_ref)):
        code_ref[:, index * block : (index + 1) * block] = jnp.broadcast_to(
            ref[block : block + 16, :block].astype(F32)[:1], (8, block)
        )
        for start in range(0, block, TILE):
            at = slice(index * block + start, index * block + start + TILE)
            x_ref[at, :] = ref[start : start + TILE, :]
            normed = normed_rows(ref, slice(start, start + TILE), gain, bias)
            normed_ref[at, :] = normed
            q = (mm(normed, wq_ref[...]) + bq).astype(BF16).astype(F32) * attn_scale
            qt_ref[:, at] = q.T.astype(BF16)
            kv_ref[at, :half] = mm(normed, wk_ref[...]).astype(BF16)
            v = (mm(normed, wv_ref[...]) + bv).astype(BF16)
            kv_ref[at, half:] = v
            vt[:, at] = v.astype(F32).T.astype(BF16)
    code = code_ref[0:1, :]
    note_tiles(code, code, act)
    load_queries(qt_ref, code, qx, heads)
    load_keys(kv_ref, 0, code, kx, heads)
    top[...] = jnp.full_like(top, -1e29)
    total[...] = jnp.zeros_like(total)
    acc[...] = jnp.zeros_like(acc)
    fold_keys(act, kx, qx, vt, top, total, acc, heads)


def forward_near(core, mine, other, gain, bias, qkv_weight, qv_bias):
    padded, width = mine.shape
    half = width // 2
    heads = half // HEAD_DIM
    rows = 2 * (padded - 16)
    specs = [VMEM] * 4 + [
        pl.BlockSpec((width, half), lambda i, c: (0, c[0])),
        pl.BlockSpec((width, half), lambda i, c: (0, 2 + c[0])),
        pl.BlockSpec((width, half), lambda i, c: (0, 4 + c[0])),
        pl.BlockSpec((1, half), lambda i, c: (0, c[0])),
        pl.BlockSpec((1, half), lambda i, c: (0, 2 + c[0])),
    ]
    outs = (
        ((rows, width), BF16),
        ((rows, width), BF16),
        ((width, 3 * half), BF16),
        ((half, rows), BF16),
        ((rows, width), BF16),
        ((8, rows), F32),
        ((8, rows), F32),
        ((8, rows), F32),
        ((half, rows), F32),
    )
    scratch = [
        pltpu.SMEM((rows // TILE, rows // TILE), jnp.int32),
        pltpu.VMEM((heads, rows, 128), BF16),
        pltpu.VMEM((heads, 128, rows), BF16),
        pltpu.VMEM((half, rows), BF16),
    ]
    run = call(partial(near_kernel, heads=heads), "near_forward", outs, scratch, specs, prefetch=1)
    return run(core, mine, other, gain, bias, qkv_weight, qkv_weight, qkv_weight, qv_bias, qv_bias)


def far_kernel(
    core_ref,
    far_ref,
    other_ref,
    gain_ref,
    bias_ref,
    wk_ref,
    wv_ref,
    bv_ref,
    qt_ref,
    code_ref,
    top_ref,
    total_ref,
    acc_ref,
    normed_ref,
    kv_ref,
    far_code_ref,
    o_ref,
    ot_ref,
    lse_ref,
    act,
    kx,
    qx,
    vt,
    top,
    total,
    acc,
    *,
    heads,
):
    half = heads * HEAD_DIM
    block = far_ref.shape[0] - 16
    gain, bias = gain_ref[...].astype(F32), bias_ref[...].astype(F32)
    bv = bv_ref[...].astype(F32)
    for index, ref in enumerate((far_ref, other_ref)):
        far_code_ref[:, index * block : (index + 1) * block] = jnp.broadcast_to(
            ref[block : block + 16, :block].astype(F32)[:1], (8, block)
        )
        for start in range(0, block, TILE):
            at = slice(index * block + start, index * block + start + TILE)
            normed = normed_rows(ref, slice(start, start + TILE), gain, bias)
            normed_ref[at, :] = normed
            kv_ref[at, :half] = mm(normed, wk_ref[...]).astype(BF16)
            v = (mm(normed, wv_ref[...]) + bv).astype(BF16)
            kv_ref[at, half:] = v
            vt[:, at] = v.astype(F32).T.astype(BF16)
    code, far_code = code_ref[0:1, :], far_code_ref[0:1, :]
    note_tiles(code, far_code, act)
    load_queries(qt_ref, code, qx, heads)
    load_keys(kv_ref, 0, far_code, kx, heads)
    top[...] = top_ref[...]
    total[...] = total_ref[...]
    acc[...] = acc_ref[...]
    fold_keys(act, kx, qx, vt, top, total, acc, heads)
    lse_ref[...] = top[...] + jnp.log(jnp.maximum(total[...], 1e-30))
    for h in range(heads):
        acc[rows_of(h), :] = acc[rows_of(h), :] / total[h : h + 1, :]
    ot_ref[...] = acc[...].astype(BF16)
    for pair in range(heads // 2):
        o_ref[:, lanes_of(pair)] = acc[lanes_of(pair), :].T.astype(BF16)


def forward_far(core, far, other, gain, bias, qkv_weight, qv_bias, qt, code, top, total, acc):
    padded, width = far.shape
    half = width // 2
    heads = half // HEAD_DIM
    rows = 2 * (padded - 16)
    specs = (
        [VMEM] * 4
        + [
            pl.BlockSpec((width, half), lambda i, c: (0, 2 + c[0])),
            pl.BlockSpec((width, half), lambda i, c: (0, 4 + c[0])),
            pl.BlockSpec((1, half), lambda i, c: (0, 2 + c[0])),
        ]
        + [VMEM] * 5
    )
    outs = (
        ((rows, width), BF16),
        ((rows, width), BF16),
        ((8, rows), F32),
        ((rows, half), BF16),
        ((half, rows), BF16),
        ((8, rows), F32),
    )
    scratch = [
        pltpu.SMEM((rows // TILE, rows // TILE), jnp.int32),
        pltpu.VMEM((heads, rows, 128), BF16),
        pltpu.VMEM((heads, 128, rows), BF16),
        pltpu.VMEM((half, rows), BF16),
        pltpu.VMEM((8, rows), F32),
        pltpu.VMEM((8, rows), F32),
        pltpu.VMEM((half, rows), F32),
    ]
    run = call(partial(far_kernel, heads=heads), "far_forward", outs, scratch, specs, prefetch=1)
    return run(core, far, other, gain, bias, qkv_weight, qkv_weight, qv_bias, qt, code, top, total, acc)


def back_kernel(*refs, heads, near):
    qt_ref, q_code_ref, k_code_ref, kv_ref, ot_ref, lse_ref, do_ref, w_ref = refs[:8]
    if near:
        dq_ref, out_ref, dx_ref, send_ref, act, kx, qx, kt, dox, delta, dq_sum, dk_sum, dv_sum = refs[8:]
    else:
        out_ref, dx_ref, send_ref, dq_sum, act, kx, qx, kt, dox, delta, dk_sum, dv_sum = refs[8:]
    queries, keys = qt_ref.shape[1], kv_ref.shape[0]
    half = heads * HEAD_DIM
    q_code, k_code = q_code_ref[0:1, :], k_code_ref[0:1, :]
    note_tiles(q_code, k_code, act)
    load_queries(qt_ref, q_code, qx, heads)
    load_keys(kv_ref, 0, k_code, kx, heads)
    zero = jnp.zeros((HEAD_DIM, queries), BF16)
    for h in range(heads):
        own = slice(0, HEAD_DIM) if h % 2 == 0 else slice(HEAD_DIM, 128)
        rest = slice(HEAD_DIM, 128) if h % 2 == 0 else slice(0, HEAD_DIM)
        grad = do_ref[rows_of(h), :]
        dox[h, own, :] = grad
        dox[h, rest, :] = zero
        delta[h : h + 1, :] = jnp.sum(grad.astype(F32) * ot_ref[rows_of(h), :].astype(F32), 0, keepdims=True)
    for pair in range(heads // 2):
        kt[lanes_of(pair), :] = kv_ref[:, lanes_of(pair)].astype(F32).T.astype(BF16)
    dq_sum[...] = dq_ref[...] if near else jnp.zeros_like(dq_sum)
    dk_sum[...] = jnp.zeros_like(dk_sum)
    dv_sum[...] = jnp.zeros_like(dv_sum)
    group = 3 if heads % 3 == 0 else 2

    def body(at, span):
        for first in range(0, heads, group):
            hs = range(first, first + group)
            scores = {h: mm(kx[h, span, :], qx[h, :, at]) for h in hs}
            dp = {h: mm(kv_ref[span, half + (h // 2) * 128 : half + (h // 2 + 1) * 128], dox[h, :, at]) for h in hs}
            probs = {h: jnp.exp(scores[h] - lse_ref[h : h + 1, at]) for h in hs}
            rounded = {h: probs[h].astype(BF16) for h in hs}
            ds = {h: (probs[h] * (dp[h] - delta[h : h + 1, at])).astype(BF16) for h in hs}
            dv = {h: mm(do_ref[rows_of(h), at], rounded[h], NT) for h in hs}
            dk = {h: mm(qt_ref[rows_of(h), at], ds[h], NT) for h in hs}
            dq = {h: mm(kt[rows_of(h), span], ds[h]) for h in hs}
            for h in hs:
                dv_sum[rows_of(h), span] += dv[h]
                dk_sum[rows_of(h), span] += dk[h]
                dq_sum[rows_of(h), at] += dq[h]

    each_tile(act, queries, keys, body)
    base = half if near else 0
    for pair in range(heads // 2):
        lanes = lanes_of(pair)
        if near:
            out_ref[:, lanes] = (dq_sum[lanes, :] * attn_scale).T.astype(BF16)
        out_ref[:, base + pair * 128 : base + (pair + 1) * 128] = dk_sum[lanes, :].T.astype(BF16)
        out_ref[:, base + half + pair * 128 : base + half + (pair + 1) * 128] = dv_sum[lanes, :].T.astype(BF16)
    block = keys // 2
    weights = w_ref[...] if near else w_ref[:, half:]
    for start in range(0, block, TILE):
        at = slice(start, start + TILE)
        send_ref[at, :] = mm(out_ref[block + start : block + start + TILE, :], weights, NT).astype(BF16)
        dx_ref[at, :] = mm(out_ref[at, :], weights, NT)


def attend_back(after, qt, q_code, k_code, kv, ot, lse, do, w, dq=None):
    half, queries = qt.shape
    keys = kv.shape[0]
    heads = half // HEAD_DIM
    near = dq is not None
    moved = (((keys // 2, 2 * half), F32), ((keys // 2, 2 * half), BF16))
    outs = (((keys, (3 if near else 2) * half), BF16),) + moved
    if not near:
        outs += (((half, queries), F32),)
    scratch = [
        pltpu.SMEM((queries // TILE, keys // TILE), jnp.int32),
        pltpu.VMEM((heads, keys, 128), BF16),
        pltpu.VMEM((heads, 128, queries), BF16),
        pltpu.VMEM((half, keys), BF16),
        pltpu.VMEM((heads, 128, queries), BF16),
        pltpu.VMEM((8, queries), F32),
    ]
    if near:
        scratch.append(pltpu.VMEM((half, queries), F32))
    scratch += [pltpu.VMEM((half, keys), F32), pltpu.VMEM((half, keys), F32)]
    name = "near_backward" if near else "far_backward"
    args = (qt, q_code, k_code, kv, ot, lse, do, w) + ((dq,) if near else ())
    run = call(partial(back_kernel, heads=heads, near=near), name, outs, scratch, [VMEM] * len(args), after=after)
    return run(*args)


def keep_column(code_ref, flags_ref, branch, images):
    code = jnp.minimum(code_ref[0:1, :], float(PAD_CLASS - 1))
    kept = jnp.zeros_like(code)
    for image in range(images):
        kept = kept + jnp.where(code == image, flags_ref[branch, image].astype(F32), 0.0)
    return jnp.broadcast_to(kept / keep_rate, (128, code.shape[1])).T[:, :1]


def gelu_both(hidden):
    size = jnp.abs(hidden)
    bell = jnp.exp(-0.5 * hidden * hidden)
    t = 1.0 / (1.0 + 0.23164189 * size)
    tail = ((((0.5307027145 * t - 0.7265760135) * t + 0.7107068705) * t - 0.142248368) * t + 0.127414796) * t * bell
    cdf = jnp.where(hidden >= 0, 1.0 - tail, tail)
    return hidden * cdf, cdf + hidden * (bell * 0.3989422804014327)


def mlp_kernel(
    core_ref,
    flags_ref,
    code_ref,
    x_ref,
    own_ref,
    got_ref,
    cot_ref,
    w_own_ref,
    w_got_ref,
    b_proj_ref,
    gain_ref,
    bias_ref,
    w_up_ref,
    b_up_ref,
    w_down_ref,
    middle_ref,
    normed_ref,
    active_ref,
    grad_hidden_ref,
    grad_down_ref,
    part_ref,
    down_ref,
    up_sums_ref,
    down_sums_ref,
    *,
    images,
):
    step = pl.program_id(0)
    keep_attn = keep_column(code_ref, flags_ref, 0, images)
    keep_mlp = keep_column(code_ref, flags_ref, 1, images)
    branch = mm(own_ref[...], w_own_ref[...]) + mm(got_ref[...], w_got_ref[...]) + b_proj_ref[...].astype(F32)
    middle = x_ref[...].astype(F32) + keep_attn * branch
    middle_ref[...] = middle
    normed = (centre(middle)[0] * gain_ref[...].astype(F32) + bias_ref[...].astype(F32)).astype(BF16)
    normed_ref[...] = normed
    grad_down = (keep_mlp * cot_ref[...].astype(F32)).astype(BF16)
    grad_down_ref[...] = grad_down

    @pl.when(step == 0)
    def _():
        up_sums_ref[...] = jnp.zeros_like(up_sums_ref)
        down_sums_ref[...] = jnp.zeros_like(down_sums_ref)

    @pl.when(step < pl.num_programs(0) // 2)
    def _():
        down_sums_ref[...] += jnp.sum(grad_down.astype(F32), 0, keepdims=True)

    units = w_up_ref.shape[1]
    chunk = 512
    for start in range(0, units, chunk):
        cols = slice(start, start + chunk)
        hidden = mm(normed, w_up_ref[:, cols]) + b_up_ref[:, cols].astype(F32)
        active, slope = gelu_both(hidden)
        active_ref[:, cols] = active.astype(BF16)
        grad_hidden = (mm(grad_down, w_down_ref[cols, :], NT) * slope).astype(BF16)
        grad_hidden_ref[:, cols] = grad_hidden
        up_sums_ref[:, cols] += jnp.sum(grad_hidden.astype(F32), 0, keepdims=True)
    down_ref[...] = mm(active_ref[...], w_down_ref[...]).astype(BF16)
    part_ref[...] = mm(grad_hidden_ref[...], w_up_ref[...], NT).astype(BF16)


def mlp(after, core, flags, code, x, own, got, cot, proj_weight, proj_bias, gain, bias, fc1_weight, fc1_bias, fc2_weight):
    rows, width = x.shape
    half, units = width // 2, fc1_weight.shape[1] // 2
    steps = rows // TILE

    def tile(cols, shift=0):
        return pl.BlockSpec((TILE, cols), lambda i, c: ((i + shift) % steps, 0))

    one = pl.BlockSpec((1, width), lambda i, c: (0, 0))
    specs = [
        SMEM,
        pl.BlockSpec((8, TILE), lambda i, c: (0, i)),
        tile(width),
        tile(half),
        tile(half, steps // 2),
        tile(width),
        pl.BlockSpec((half, width), lambda i, c: (c[0], 0)),
        pl.BlockSpec((half, width), lambda i, c: (1 - c[0], 0)),
        one,
        one,
        one,
        pl.BlockSpec((width, units), lambda i, c: (0, c[0])),
        pl.BlockSpec((1, units), lambda i, c: (0, c[0])),
        pl.BlockSpec((units, width), lambda i, c: (c[0], 0)),
    ]
    outs = (
        ((rows, width), F32),
        ((rows, width), BF16),
        ((rows, units), BF16),
        ((rows, units), BF16),
        ((rows, width), BF16),
        ((rows, width), BF16),
        ((rows, width), BF16),
        ((1, units), F32),
        ((1, width), F32),
    )
    out_specs = (
        tile(width),
        tile(width),
        tile(units),
        tile(units),
        tile(width),
        tile(width),
        tile(width),
        pl.BlockSpec((1, units), lambda i, c: (0, 0)),
        one,
    )
    kernel = partial(mlp_kernel, images=flags.shape[1])
    run = call(kernel, "mlp", outs, [], specs, out_specs, (steps,), prefetch=1, after=after)
    return run(
        core, flags, code, x, own, got, cot, proj_weight, proj_weight, proj_bias, gain, bias, fc1_weight, fc1_bias, fc2_weight
    )


def middle_kernel(
    core_ref,
    flags_ref,
    code_ref,
    part_ref,
    got_ref,
    middle_ref,
    cot_ref,
    gain_ref,
    w_ref,
    grad_middle_ref,
    grad_half_ref,
    do_ref,
    sums_ref,
    *,
    images,
):
    step = pl.program_id(0)
    keep_attn = keep_column(code_ref, flags_ref, 0, images)
    unit, scale = centre(middle_ref[...])
    grad = (part_ref[...].astype(F32) + got_ref[...].astype(F32)) * gain_ref[...].astype(F32)
    grad_middle = cot_ref[...].astype(F32) + norm_back(unit, scale, grad)
    grad_middle_ref[...] = grad_middle
    grad_proj = (keep_attn * grad_middle).astype(BF16)
    half = w_ref.shape[0]
    grad_half_ref[...] = jnp.where(core_ref[0] == 0, grad_proj[:, :half], grad_proj[:, half:])
    do_ref[...] = mm(w_ref[...], grad_proj, NT).astype(BF16)

    @pl.when(step == 0)
    def _():
        sums_ref[...] = jnp.zeros_like(sums_ref)

    @pl.when(step >= pl.num_programs(0) // 2)
    def _():
        sums_ref[...] += jnp.sum(grad_proj.astype(F32), 0, keepdims=True)


def middle_back(after, core, flags, code, part, got, middle, cot, gain, proj_weight):
    rows, width = part.shape
    half = width // 2
    steps = rows // TILE
    late = steps // 2

    def tile(cols, shift=late):
        return pl.BlockSpec((TILE, cols), lambda i, c: ((i + shift) % steps, 0))

    one = pl.BlockSpec((1, width), lambda i, c: (0, 0))
    specs = [
        SMEM,
        pl.BlockSpec((8, TILE), lambda i, c: (0, (i + late) % steps)),
        tile(width),
        tile(width, 0),
        tile(width),
        tile(width),
        one,
        pl.BlockSpec((half, width), lambda i, c: (c[0], 0)),
    ]
    outs = (((rows // 2, width), F32), ((rows, half), BF16), ((half, rows), BF16), ((1, width), F32))
    out_specs = (
        pl.BlockSpec((TILE, width), lambda i, c: (jnp.maximum(i - late, 0), 0)),
        tile(half),
        pl.BlockSpec((half, TILE), lambda i, c: (0, (i + late) % steps)),
        one,
    )
    kernel = partial(middle_kernel, images=flags.shape[1])
    run = call(kernel, "middle_backward", outs, [], specs, out_specs, (steps,), prefetch=1, after=after)
    return run(core, flags, code, part, got, middle, cot, gain, proj_weight)


def turned_kernel(left_ref, right_ref, out_ref):
    out_ref[...] = mm(left_ref[...], right_ref[...], TN).astype(BF16)


def turned_product(after, name, left, right):
    rows, height = left.shape
    width = right.shape[1]
    step = TILE if height % TILE == 0 else 128
    specs = [pl.BlockSpec((rows, step), lambda i: (0, i)), pl.BlockSpec((rows, width), lambda i: (0, 0))]
    out_specs = (pl.BlockSpec((step, width), lambda i: (i, 0)),)
    run = call(turned_kernel, name, (((height, width), BF16),), [], specs, out_specs, (height // step,), after=after)
    return run(left, right)[0]


def up_kernel(core_ref, normed_ref, grad_ref, w_ref, sums_ref, gain_ref, bias_ref, out_ref, small_ref):
    out = mm(normed_ref[...], grad_ref[...], TN)
    out_ref[...] = out.astype(BF16)
    small_ref[...] = ln_columns(out, w_ref[...].astype(F32), sums_ref[...], gain_ref, bias_ref)


def ln_columns(grad, weight, sums, gain_ref, bias_ref):
    gain, bias = gain_ref[...].astype(F32), bias_ref[...].astype(F32)
    first = jnp.sum(weight * grad, 1, keepdims=True)
    second = jnp.sum(weight * sums, 1, keepdims=True)
    lane = lax.broadcasted_iota(jnp.int32, (weight.shape[0], 128), 1)
    return jnp.where(lane == 0, (first - bias * second) / gain, jnp.where(lane == 1, second, 0.0))


def up_product(after, core, normed, grad, weight, sums, gain, bias):
    rows, width = normed.shape
    units = grad.shape[1]
    column = pl.BlockSpec((TILE, 1), lambda i, c: (i, 0))
    specs = [
        pl.BlockSpec((rows, TILE), lambda i, c: (0, i)),
        pl.BlockSpec((rows, units), lambda i, c: (0, 0)),
        pl.BlockSpec((TILE, units), lambda i, c: (i, c[0])),
        pl.BlockSpec((1, units), lambda i, c: (0, 0)),
        column,
        column,
    ]
    outs = (((width, units), BF16), ((width, 128), F32))
    out_specs = (pl.BlockSpec((TILE, units), lambda i, c: (i, 0)), pl.BlockSpec((TILE, 128), lambda i, c: (i, 0)))
    run = call(up_kernel, "up_weight", outs, [], specs, out_specs, (width // TILE,), prefetch=1, after=after)
    return run(core, normed, grad, weight, sums, gain, bias)


def qkv_kernel(near_ref, far_ref, near_grad_ref, far_grad_ref, w_ref, gain_ref, bias_ref, out_ref, small_ref, sums_ref):
    half = far_grad_ref.shape[1] // 2

    @pl.when(pl.program_id(0) == 0)
    def _():
        near = jnp.sum(near_grad_ref[...].astype(F32), 0, keepdims=True)
        far = jnp.sum(far_grad_ref[...].astype(F32), 0, keepdims=True)
        sums_ref[:, :half] = near[:, :half]
        sums_ref[:, half:] = near[:, half:] + far

    out_q = mm(near_ref[...], near_grad_ref[:, :half], TN)
    out_kv = mm(near_ref[...], near_grad_ref[:, half:], TN) + mm(far_ref[...], far_grad_ref[...], TN)
    out = jnp.concatenate([out_q, out_kv], 1)
    out_ref[...] = out.astype(BF16)
    small_ref[...] = ln_columns(out, w_ref[...].astype(F32), sums_ref[...], gain_ref, bias_ref)


def qkv_product(after, near, far, near_grad, far_grad, w, gain, bias):
    rows, width = near.shape
    wide, far_wide = near_grad.shape[1], far_grad.shape[1]
    column = pl.BlockSpec((TILE, 1), lambda i: (i, 0))
    specs = [
        pl.BlockSpec((rows, TILE), lambda i: (0, i)),
        pl.BlockSpec((rows, TILE), lambda i: (0, i)),
        pl.BlockSpec((rows, wide), lambda i: (0, 0)),
        pl.BlockSpec((rows, far_wide), lambda i: (0, 0)),
        pl.BlockSpec((TILE, wide), lambda i: (i, 0)),
        column,
        column,
    ]
    outs = (((width, wide), BF16), ((width, 128), F32), ((1, wide), F32))
    out_specs = (
        pl.BlockSpec((TILE, wide), lambda i: (i, 0)),
        pl.BlockSpec((TILE, 128), lambda i: (i, 0)),
        pl.BlockSpec((1, wide), lambda i: (0, 0)),
    )
    run = call(qkv_kernel, "qkv_weight", outs, [], specs, out_specs, (width // TILE,), after=after)
    return run(near, far, near_grad, far_grad, w, gain, bias)


def sum_kernel(bits_ref, kept_ref, arrived_ref, *out_refs):
    if len(out_refs) == 1:
        out_refs[0][...] = kept_ref[...][:, 0].astype(F32) + arrived_ref[...].astype(F32)
        return
    mine = bits_ref[1]
    for out_ref, at in zip(out_refs, (1 - mine, mine)):
        out_ref[...] = (kept_ref[:, 0, :, at].astype(F32) + arrived_ref[:, :, at].astype(F32)).astype(BF16)


def add_kernel(left_ref, right_ref, out_ref):
    out_ref[...] = (left_ref[...].astype(F32) + right_ref[...].astype(F32)).astype(out_ref.dtype)


def add(after, left, right):
    run = call(add_kernel, "add_blocks", ((left.shape, BF16),), [], [VMEM, VMEM], after=after)
    return run(left, right)[0]


def finish_kernel(x_ref, dx_ref, beside_ref, across_ref, gain_ref, middle_ref, out_ref):
    unit, scale = centre(x_ref[...].astype(F32))
    grad = dx_ref[...] + beside_ref[...].astype(F32) + across_ref[...].astype(F32)
    out_ref[...] = (middle_ref[...] + norm_back(unit, scale, grad * gain_ref[...].astype(F32))).astype(BF16)


def finish(after, x, dx, beside, across, gain, middle):
    rows, width = x.shape
    tile = pl.BlockSpec((TILE, width), lambda i: (i, 0))
    one = pl.BlockSpec((1, width), lambda i: (0, 0))
    specs = [tile, tile, tile, tile, one, tile]
    run = call(finish_kernel, "token_gradient", ((x.shape, BF16),), [], specs, (tile,), (rows // TILE,), after=after)
    return run(x, dx, beside, across, gain, middle)[0]


def output_kernel(flags_ref, code_ref, middle_ref, down_ref, got_ref, bias_ref, out_ref, *, images):
    kept = keep_column(code_ref, flags_ref, 1, images)
    branch = down_ref[...].astype(F32) + got_ref[...].astype(F32) + bias_ref[...].astype(F32)
    out_ref[...] = (middle_ref[...] + kept * branch).astype(BF16)


def layer_out(after, flags, code, middle, down, got, bias):
    rows, width = got.shape
    tile = pl.BlockSpec((TILE, width), lambda i: (i, 0))
    one = pl.BlockSpec((1, width), lambda i: (0, 0))
    specs = [SMEM, pl.BlockSpec((8, TILE), lambda i: (0, i)), tile, tile, tile, one]
    kernel = partial(output_kernel, images=flags.shape[1])
    run = call(kernel, "layer_output", ((got.shape, BF16),), [], specs, (tile,), (rows // TILE,), after=after)
    return run(flags, code, middle, down, got, bias)[0]


def swap_halves(rows):
    half = rows.shape[0] // 2
    return jnp.concatenate([rows[half:], rows[:half]], 0)


def pick(array, index, dim):
    return lax.dynamic_index_in_dim(array, index, dim, keepdims=False)


class Links:
    def __init__(self, mesh):
        self.dp, self.blk = mesh.shape["dp"], mesh.shape["blk"]
        self.bits = self.dp.bit_length() - 1

    def core(self, value):
        return lax.ppermute(value, "blk", [(i, i ^ 1) for i in range(self.blk)])

    def side(self, value):
        return lax.ppermute(value, "blk", [(i, i ^ 2) for i in range(self.blk)])

    def cross(self, value, step):
        if step == "x":
            return self.side(value)
        return lax.ppermute(value, "dp", [(i, i ^ (1 << step)) for i in range(self.dp)])

    def bit(self, step):
        if step == "x":
            return lax.axis_index("blk") // 2
        return (lax.axis_index("dp") >> step) & 1

    def swap(self, value):
        top = self.dp // 2
        pairs = []
        for d in range(self.dp):
            for b in range(self.blk):
                high, core = d // top, b % 2
                pairs.append((d * self.blk + b, (d % top + core * top) * self.blk + (b - core + high)))
        return lax.ppermute(value, ("dp", "blk"), pairs)


class Portion:
    def __init__(self, links, array, dims, order):
        self.links, self.order = links, list(order)
        self.dims = list(dims)
        self.tail = array.shape[1:]
        step = self.order[0]
        view = self.split(array, step)
        self.kept = view
        self.arrived = links.cross(pick(view, 1 - links.bit(step), 1), step)
        self.sent_once = False

    def split(self, array, step):
        place = self.dims.index(step)
        return array.reshape((2**place, 2, 2 ** (len(self.dims) - place - 1)) + self.tail)

    def advance(self, after):
        links, step = self.links, self.order.pop(0)
        place = self.dims.index(step)
        bit = links.bit(step)
        before, behind = 2**place, 2 ** (len(self.dims) - place - 1)
        self.dims.pop(place)
        count = len(self.tail)
        whole = (0,) * (count + 4)
        if not self.order:
            kept = self.kept if self.kept.ndim == count + 3 else self.kept.reshape((before, 1, behind) + self.tail)
            shape = (before, behind) + self.tail
            first = kept.shape[1] == 2
            block = pl.BlockSpec((before, 1, behind) + self.tail, lambda i, b: (0, b[0] if first else 0) + (0,) * (count + 1))
            run = call(sum_kernel, "sum_last", ((shape, F32),), [], [block, VMEM], prefetch=1, after=after)
            bits = jnp.stack([bit, bit]).astype(jnp.int32)
            self.total = run(bits, kept, self.arrived.reshape(shape))[0].reshape(self.tail)
            return self.total
        follow = self.order[0]
        spot = self.dims.index(follow)
        outer, inner = 2**spot, 2 ** (len(self.dims) - spot - 1)
        first = self.kept.ndim == count + 3 and self.kept.shape[1] == 2 and not self.sent_once
        if first and spot < place:
            between = before // (2 * outer)
            kept = self.kept.reshape((outer, 2, between, 2, behind) + self.tail)
            block = (outer, 2, between, 1, behind) + self.tail
            index = lambda i, b: (0, 0, 0, b[0], 0) + (0,) * count
            arrived = self.arrived.reshape((outer, 2, between, 1, behind) + self.tail)
            at = lambda ref, where: ref[:, where]
            shape = (outer, between, 1, behind) + self.tail
        elif first:
            between = outer // before
            kept = self.kept.reshape((before, 2, between, 2, inner) + self.tail)
            block = (before, 1, between, 2, inner) + self.tail
            index = lambda i, b: (0, b[0], 0, 0, 0) + (0,) * count
            arrived = self.arrived.reshape((before, 1, between, 2, inner) + self.tail)
            at = lambda ref, where: ref[:, :, :, where]
            shape = (before, 1, between, inner) + self.tail
        else:
            kept = self.kept.reshape((outer, 2, inner) + self.tail)
            block = (outer, 2, inner) + self.tail
            index = lambda i, b: (0, 0, 0) + (0,) * count
            arrived = self.arrived.reshape((outer, 2, inner) + self.tail)
            at = lambda ref, where: ref[:, where]
            shape = (outer, inner) + self.tail

        def kernel(bits_ref, kept_ref, arrived_ref, send_ref, keep_ref):
            mine = bits_ref[1]
            for out_ref, where in ((send_ref, 1 - mine), (keep_ref, mine)):
                out_ref[...] = (at(kept_ref, where).astype(F32) + at(arrived_ref, where).astype(F32)).astype(BF16)

        specs = [pl.BlockSpec(block, index), VMEM]
        bits = jnp.stack([bit, links.bit(follow)]).astype(jnp.int32)
        run = call(kernel, "sum_half", ((shape, BF16), (shape, BF16)), [], specs, prefetch=1, after=after)
        send, keep = run(bits, kept, arrived)
        self.sent_once = True
        self.kept = keep
        self.arrived = links.cross(send, follow)
        return keep


def local(
    links,
    tokens,
    cotangent,
    segments,
    padding,
    drop_keep,
    ln1_gain,
    ln1_bias,
    qkv_weight,
    qv_bias,
    proj_weight,
    proj_bias,
    ln2_gain,
    ln2_bias,
    fc1_weight,
    fc1_bias,
    fc2_weight,
    fc2_bias,
):
    _, block, width = tokens.shape
    half = width // 2
    units = fc1_weight.shape[1] // 2
    core = lax.axis_index("blk") % 2
    core_arg = core.reshape(1).astype(jnp.int32)
    owners = links.dp * links.blk
    rows = 2 * block

    code = jnp.where(padding == 1, segments, PAD_CLASS).astype(BF16)
    mine = jnp.concatenate([tokens[0], jnp.pad(code, ((0, 15), (0, width - block)))], 0)
    far = links.side(mine)
    other = links.core(mine)
    cot = jnp.concatenate([cotangent[0], links.core(cotangent[0])], 0)
    flags = drop_keep[:, 0, :]

    gain_one, bias_one = ln1_gain.reshape(1, -1), ln1_bias.reshape(1, -1)
    gain_two, bias_two = ln2_gain.reshape(1, -1), ln2_bias.reshape(1, -1)
    bias_qv = qv_bias.reshape(1, -1)
    x, near_normed, w_qkv, qt, near_kv, near_code, top, total, acc = forward_near(
        core_arg, mine, other, gain_one, bias_one, qkv_weight, bias_qv
    )
    far = lax.dynamic_update_slice(far, near_normed[:8, :128], (block + 8, 0))
    far_other = links.core(far)
    far_normed, far_kv, far_code, own, ot, lse = forward_far(
        core_arg, far, far_other, gain_one, bias_one, qkv_weight, bias_qv, qt, near_code, top, total, acc
    )
    got = links.core(own)
    middle, normed_two, active, grad_hidden, grad_down, part, down, up_sums, down_sums = mlp(
        (),
        core_arg,
        flags,
        near_code,
        x,
        own,
        got,
        cot,
        proj_weight,
        proj_bias.reshape(1, -1),
        gain_two,
        bias_two,
        fc1_weight,
        fc1_bias.reshape(1, -1),
        fc2_weight,
    )
    got_part = links.core(part)
    down_other = links.core(down[block:])

    bits = links.bits
    low = [bits - 1 - i for i in range(bits)]
    chip = low + ["x"]
    by_core = low[1:] + ["x", low[0]]
    tail = [s for s in low if s > 1][::-1]
    groups = 2 * links.dp

    d_down = turned_product((part,), "down_weight", active, grad_down)
    down_portion = Portion(links, d_down.reshape(groups, -1, width), by_core, ["x", 0, 1] + tail)
    d_up, up_small = up_product(
        (d_down,), core_arg, normed_two, grad_hidden, fc1_weight, up_sums, ln2_gain.reshape(-1, 1), ln2_bias.reshape(-1, 1)
    )
    up_portion = Portion(links, d_up.reshape(groups, -1, units), chip, [0, 1, "x"] + tail)
    grad_middle, grad_half, do, proj_sums = middle_back(
        (d_up,), core_arg, flags, near_code, part, got_part, middle, cot, gain_two, proj_weight
    )
    d_own = turned_product((do,), "proj_weight", own, grad_half)
    d_got = turned_product((d_own,), "proj_weight", got, swap_halves(grad_half))
    d_proj = jnp.where(core == 0, jnp.concatenate([d_own, d_got], 0), jnp.concatenate([d_got, d_own], 0))

    far_grad, far_dx, far_send, dq = attend_back((d_got,), qt, near_code, far_code, far_kv, ot, lse, do, w_qkv)
    last = down_portion.advance((far_grad,))
    last = up_portion.advance((last,))
    far_sum = add((last,), far_dx, links.core(far_send))
    across = links.side(far_sum)
    near_grad, near_dx, near_send = attend_back((far_sum,), qt, near_code, near_code, near_kv, ot, lse, do, w_qkv, dq)
    last = down_portion.advance((near_grad,))
    last = up_portion.advance((last,))
    d_qkv, qkv_small, qkv_sums = qkv_product(
        (last,), near_normed, far_normed, near_grad, far_grad, w_qkv, ln1_gain.reshape(-1, 1), ln1_bias.reshape(-1, 1)
    )

    def spread(value, parts):
        value = value.reshape(parts, -1)
        empty = jnp.zeros_like(value)
        first = jnp.where(core == 0, value, empty)
        last = jnp.where(core == 0, empty, value)
        return jnp.concatenate([first, last], 1).reshape(width, -1)

    smalls = (
        qkv_small[:, :2],
        up_small[:, :2],
        proj_sums.reshape(width, 1),
        down_sums.reshape(width, 1),
        spread(jnp.concatenate([qkv_sums[:, :half], qkv_sums[:, 2 * half :]], 1), 2),
        spread(up_sums, 1),
    )
    small = jnp.concatenate(smalls, 1)
    extra = small.shape[1]
    small = jnp.pad(small, ((0, 0), (0, 128 - extra))).astype(BF16)
    cut = (4 * half // 128 + 1) // 2 * 128
    one = jnp.concatenate([d_qkv[:, cut:], d_proj, small], 1)
    two = d_qkv[:, :cut]
    one_portion = Portion(links, one.reshape(groups, -1, one.shape[1]), chip, [0, "x", 1] + tail)
    two_portion = Portion(links, two.reshape(groups, -1, two.shape[1]), chip, [1, 0, "x"] + tail)
    last = down_portion.advance((d_qkv,))
    last = up_portion.advance((last,))
    layer_output = layer_out((last,), flags, near_code, middle, down, down_other, fc2_bias.reshape(1, -1))
    last = layer_output
    for _ in tail:
        last = one_portion.advance((last,))
        last = two_portion.advance((last,))
        last = down_portion.advance((last,))
        last = up_portion.advance((last,))
    down_part, up_part = down_portion.total, up_portion.total
    tokens_grad = finish((last,), tokens[0], near_dx, links.core(near_send), across, gain_one, grad_middle)
    last = tokens_grad
    while one_portion.order:
        last = one_portion.advance((last,))
        last = two_portion.advance((last,))
    one_part, two_part = one_portion.total, two_portion.total

    def split(array):
        array = array.reshape(2, width // owners, -1)
        return pick(array, core, 0), links.core(pick(array, 1 - core, 0))

    def join(kept, arrived):
        return jnp.where(core == 0, jnp.concatenate([kept, arrived], 1), jnp.concatenate([arrived, kept], 1))

    down_grad = links.swap(down_part)
    kept, arrived = split(up_part)
    up_grad = join(kept, arrived)
    kept, arrived = split(jnp.concatenate([two_part, one_part], 1))
    parts = [join(kept[:, i * half : (i + 1) * half], arrived[:, i * half : (i + 1) * half]) for i in range(4)]
    qkv_grad, proj_grad = jnp.concatenate(parts[:3], 1), parts[3]
    small = kept[:, 4 * half : 4 * half + extra] + arrived[:, 4 * half : 4 * half + extra]
    g1, b1, g2, b2, pb, d2 = (small[:, i] for i in range(6))
    qvb, u1 = small[:, 6:8].reshape(-1), small[:, 8:12].reshape(-1)
    shape = tokens.shape
    return (
        layer_output.reshape(shape),
        tokens_grad.reshape(shape),
        g1,
        b1,
        qkv_grad,
        qvb,
        proj_grad,
        pb,
        g2,
        b2,
        up_grad,
        u1,
        down_grad,
        d2,
    )


def solution(mesh):
    both = P(("dp", "blk"))
    rows = P(("dp", "blk"), None)
    token = P("dp", "blk", None)
    placed = (token, token, P("dp", "blk"), P("dp", "blk"), P(None, "dp", None)) + (P(),) * 12
    return jax.shard_map(
        partial(local, Links(mesh)),
        mesh=mesh,
        in_specs=placed,
        out_specs=(token, token, both, both, rows, both, rows, both, both, both, rows, both, rows, both),
        check_vma=False,
    )
```

```python
from functools import partial

import jax
import jax.numpy as jnp
from jax import lax
from jax.experimental import pallas as pl
from jax.experimental.pallas import tpu as pltpu
from jax.sharding import PartitionSpec as P

HEAD_DIM = 64
F32 = jnp.float32
BF16 = jnp.bfloat16
epsilon = 1e-06
keep_rate = 0.9
attn_scale = 0.125
negative = -1e30
PAD_CLASS = 4
TILE = 256
MIB = 2**20
FLOPS_PER_US = 1.0 * 10**9
BUDGET = {
    "near_forward": (28, 15),
    "far_forward": (28, 12),
    "mlp": (36, 21),
    "down_weight": (16, 1),
    "up_weight": (24, 1),
    "middle_backward": (16, 5),
    "far_backward": (32, 14),
    "near_backward": (48, 22),
    "sum_half": (8, 2),
    "sum_last": (8, 1),
    "add_blocks": (8, 2),
    "token_gradient": (12, 2),
    "layer_output": (12, 2),
}
NN = ((1,), (0,))
NT = ((1,), (1,))
TN = ((0,), (0,))
VMEM = pl.BlockSpec(memory_space=pltpu.VMEM)
SMEM = pl.BlockSpec(memory_space=pltpu.SMEM)
HBM = pl.BlockSpec(memory_space=pltpu.HBM)
ROW_STEP = 384


def mm(left, right, dims=NN):
    return lax.dot_general(left, right, (dims, ((), ())), preferred_element_type=F32)


def rows_of(head):
    return slice(head * HEAD_DIM, (head + 1) * HEAD_DIM)


def lanes_of(pair):
    return slice(pair * 128, (pair + 1) * 128)


def centre(values):
    shifted = values - jnp.mean(values, -1, keepdims=True)
    spread = jnp.mean(shifted * shifted, -1, keepdims=True)
    scale = lax.rsqrt(spread + epsilon)
    return shifted * scale, scale


def norm_back(unit, scale, grad):
    return (grad - jnp.mean(grad, -1, keepdims=True) - unit * jnp.mean(grad * unit, -1, keepdims=True)) * scale


def call(kernel, name, outs, scratch, specs, out_specs=None, grid=None, prefetch=0, after=(), pin=(), hold=()):
    limit, cost = BUDGET[name]
    out_specs = out_specs or tuple(VMEM for _ in outs)
    first = prefetch + len(specs)

    def ordered(*refs):
        kernel(*refs[:first], *refs[first + len(after) :])

    spec = pltpu.PrefetchScalarGridSpec(
        num_scalar_prefetch=prefetch,
        grid=grid or (1,),
        in_specs=list(specs) + [pl.BlockSpec(memory_space=pl.ANY)] * len(after),
        out_specs=out_specs,
        scratch_shapes=scratch,
    )
    run = pl.pallas_call(
        ordered,
        out_shape=tuple(
            (pltpu.HBM if pinned else jax.ShapeDtypeStruct)(shape, kind)
            for (shape, kind), pinned in zip(outs, hold if hold else [spec is HBM for spec in out_specs])
        ),
        grid_spec=spec,
        compiler_params=pltpu.CompilerParams(vmem_limit_bytes=limit * MIB),
        cost_estimate=pl.CostEstimate(flops=int(cost * FLOPS_PER_US), bytes_accessed=1, transcendentals=0),
        name=name,
    )

    def place(*args):
        held = list(args)
        for i, spec in enumerate(specs):
            if spec is HBM or i in pin:
                held[prefetch + i] = pltpu.with_memory_space_constraint(held[prefetch + i], pltpu.HBM)
        return run(*held, *after)

    return place


def query_mask(code):
    kind = lax.broadcasted_iota(jnp.int32, (HEAD_DIM, code.shape[1]), 0).astype(F32)
    seen = (code == kind) | ((code == PAD_CLASS) & (kind == PAD_CLASS - 1)) | (kind > PAD_CLASS)
    return jnp.where(seen, 0.0, negative).astype(BF16)


def load_queries(qt_ref, code, qx, heads):
    mask = query_mask(code)
    for h in range(heads):
        own = slice(0, HEAD_DIM) if h % 2 == 0 else slice(HEAD_DIM, 128)
        rest = slice(HEAD_DIM, 128) if h % 2 == 0 else slice(0, HEAD_DIM)
        qx[h, own, :] = qt_ref[rows_of(h), :]
        qx[h, rest, :] = mask


def load_keys(k_ref, first, code, kx, heads):
    keys = k_ref.shape[0]
    kind = lax.broadcasted_iota(jnp.int32, (128, keys), 0).astype(F32)
    low = (kind == code).astype(F32).T.astype(BF16)
    high = (kind - HEAD_DIM == code).astype(F32).T.astype(BF16)
    lane = lax.broadcasted_iota(jnp.int32, (keys, 128), 1)
    for pair in range(heads // 2):
        slab = k_ref[:, first + pair * 128 : first + (pair + 1) * 128]
        kx[2 * pair] = jnp.where(lane < HEAD_DIM, slab, high)
        kx[2 * pair + 1] = jnp.where(lane < HEAD_DIM, low, slab)


def tile_ranges(code):
    image = jnp.minimum(code, float(PAD_CLASS - 1))
    cuts = [image[:, i : i + TILE] for i in range(0, code.shape[1], TILE)]
    return [(jnp.min(c), jnp.max(c)) for c in cuts]


def note_tiles(q_code, k_code, act):
    q_ranges, k_ranges = tile_ranges(q_code), tile_ranges(k_code)
    for i, (q_low, q_high) in enumerate(q_ranges):
        for j, (k_low, k_high) in enumerate(k_ranges):
            act[i, j] = ((q_low <= k_high) & (q_high >= k_low)).astype(jnp.int32)


def each_tile(act, queries, keys, body):
    for q_tile in range(queries // TILE):
        at = slice(q_tile * TILE, (q_tile + 1) * TILE)

        def step(k_tile, carry):
            @pl.when(act[q_tile, k_tile] > 0)
            def _():
                body(at, pl.ds(pl.multiple_of(k_tile * TILE, TILE), TILE))

            return carry

        lax.fori_loop(0, keys // TILE, step, 0)


def fold_keys(act, kx, qx, vt, top, total, acc, heads):
    def body(at, span):
        hs = range(heads)
        scores = [mm(kx[h, span, :], qx[h, :, at]) for h in hs]
        old = [top[h : h + 1, at] for h in hs]
        new = [jnp.maximum(old[h], jnp.max(scores[h], 0, keepdims=True)) for h in hs]
        decay = [jnp.exp(old[h] - new[h]) for h in hs]
        weights = [jnp.exp(scores[h] - new[h]) for h in hs]
        added = [mm(vt[rows_of(h), span], weights[h].astype(BF16)) for h in hs]
        for h in hs:
            top[h : h + 1, at] = new[h]
            total[h : h + 1, at] = decay[h] * total[h : h + 1, at] + jnp.sum(weights[h], 0, keepdims=True)
            acc[rows_of(h), at] = decay[h] * acc[rows_of(h), at] + added[h]

    each_tile(act, qx.shape[2], kx.shape[1], body)


def normed_rows(ref, at, gain, bias):
    return (centre(ref[at, :].astype(F32))[0] * gain + bias).astype(BF16)


def begin(sems, index, source, target):
    copy = pltpu.make_async_copy(source, target, sems.at[index])
    copy.start()
    return copy


def load_tokens(refs, code_ref):
    block = refs[0].shape[0] - 16
    for index, ref in enumerate(refs):
        row = ref[block : block + 16, :block].astype(F32)[:1]
        code_ref[:, index * block : (index + 1) * block] = jnp.broadcast_to(row, (8, block))
        for start in range(0, block, TILE):
            at = slice(index * block + start, index * block + start + TILE)
            yield at, ref[start : start + TILE, :]


def turn(array):
    return array.astype(F32).T.astype(BF16)


def near_kernel(
    core_ref,
    mine_ref,
    other_ref,
    gain_ref,
    bias_ref,
    bq_ref,
    bv_ref,
    weight_hbm,
    code_ref,
    top,
    total,
    acc,
    normed_hbm,
    w_hbm,
    qt_hbm,
    kv_hbm,
    act,
    kx,
    qx,
    vt,
    normed_v,
    w_v,
    qt_v,
    kv_v,
    sems,
    *,
    heads,
):
    half = heads * HEAD_DIM
    first = pl.multiple_of(core_ref[0] * half, 128)
    loads = [
        begin(sems, i, weight_hbm.at[:, pl.ds(2 * i * half + first, half)], w_v.at[:, i * half : (i + 1) * half])
        for i in range(3)
    ]
    gain, bias = gain_ref[...].astype(F32), bias_ref[...].astype(F32)
    bq, bv = bq_ref[...].astype(F32), bv_ref[...].astype(F32)
    for at, tokens in load_tokens((mine_ref, other_ref), code_ref):
        normed = (centre(tokens.astype(F32))[0] * gain + bias).astype(BF16)
        normed_v[:, at] = turn(normed)
        for load in loads:
            load.wait()
        loads = []
        q = (mm(normed, w_v[:, :half]) + bq).astype(BF16).astype(F32) * attn_scale
        qt_v[:, at] = q.T.astype(BF16)
        kv_v[at, :half] = mm(normed, w_v[:, half : 2 * half]).astype(BF16)
        v = (mm(normed, w_v[:, 2 * half :]) + bv).astype(BF16)
        kv_v[at, half:] = v
        vt[:, at] = turn(v)
    pairs = ((normed_v, normed_hbm), (w_v, w_hbm), (qt_v, qt_hbm), (kv_v, kv_hbm))
    stores = [begin(sems, 3 + i, source, target) for i, (source, target) in enumerate(pairs)]
    code = code_ref[0:1, :]
    note_tiles(code, code, act)
    load_queries(qt_v, code, qx, heads)
    load_keys(kv_v, 0, code, kx, heads)
    top[...] = jnp.full_like(top, -1e29)
    total[...] = jnp.zeros_like(total)
    acc[...] = jnp.zeros_like(acc)
    fold_keys(act, kx, qx, vt, top, total, acc, heads)
    for store in stores:
        store.wait()


def forward_near(core, mine, other, gain, bias, qkv_weight, qv_bias):
    padded, width = mine.shape
    half = width // 2
    heads = half // HEAD_DIM
    rows = 2 * (padded - 16)
    specs = [VMEM] * 4 + [
        pl.BlockSpec((1, half), lambda i, c: (0, c[0])),
        pl.BlockSpec((1, half), lambda i, c: (0, 2 + c[0])),
        HBM,
    ]
    kept = (((width, rows), BF16), ((width, 3 * half), BF16), ((half, rows), BF16), ((rows, width), BF16))
    outs = (((8, rows), F32), ((8, rows), F32), ((8, rows), F32), ((half, rows), F32)) + kept
    scratch = [
        pltpu.SMEM((rows // TILE, rows // TILE), jnp.int32),
        pltpu.VMEM((heads, rows, 128), BF16),
        pltpu.VMEM((heads, 128, rows), BF16),
        pltpu.VMEM((half, rows), BF16),
    ]
    scratch += [pltpu.VMEM(shape, kind) for shape, kind in kept] + [pltpu.SemaphoreType.DMA((7,))]
    run = call(
        partial(near_kernel, heads=heads), "near_forward", outs, scratch, specs, (VMEM,) * 4 + (HBM,) * 4, prefetch=1
    )
    return run(core, mine, other, gain, bias, qv_bias, qv_bias, qkv_weight)


def far_kernel(
    far_ref,
    other_ref,
    gain_ref,
    bias_ref,
    bv_ref,
    code_ref,
    top_ref,
    total_ref,
    acc_ref,
    w_hbm,
    qt_hbm,
    far_code_ref,
    o_ref,
    lse_ref,
    normed_hbm,
    kv_hbm,
    ot_hbm,
    act,
    kx,
    qx,
    vt,
    top,
    total,
    acc,
    w_v,
    qt_v,
    normed_v,
    kv_v,
    ot_v,
    sems,
    *,
    heads,
):
    half = heads * HEAD_DIM
    loads = [begin(sems, 0, w_hbm.at[:, half:], w_v), begin(sems, 1, qt_hbm, qt_v)]
    gain, bias = gain_ref[...].astype(F32), bias_ref[...].astype(F32)
    bv = bv_ref[...].astype(F32)
    for at, tokens in load_tokens((far_ref, other_ref), far_code_ref):
        normed = (centre(tokens.astype(F32))[0] * gain + bias).astype(BF16)
        normed_v[:, at] = turn(normed)
        for load in loads:
            load.wait()
        loads = []
        kv_v[at, :half] = mm(normed, w_v[:, :half]).astype(BF16)
        v = (mm(normed, w_v[:, half:]) + bv).astype(BF16)
        kv_v[at, half:] = v
        vt[:, at] = turn(v)
    stores = [begin(sems, 2, normed_v, normed_hbm), begin(sems, 3, kv_v, kv_hbm)]
    code, far_code = code_ref[0:1, :], far_code_ref[0:1, :]
    note_tiles(code, far_code, act)
    load_queries(qt_v, code, qx, heads)
    load_keys(kv_v, 0, far_code, kx, heads)
    top[...] = top_ref[...]
    total[...] = total_ref[...]
    acc[...] = acc_ref[...]
    fold_keys(act, kx, qx, vt, top, total, acc, heads)
    lse_ref[...] = top[...] + jnp.log(jnp.maximum(total[...], 1e-30))
    for h in range(heads):
        acc[rows_of(h), :] = acc[rows_of(h), :] / total[h : h + 1, :]
    ot_v[...] = acc[...].astype(BF16)
    stores.append(begin(sems, 4, ot_v, ot_hbm))
    for pair in range(heads // 2):
        o_ref[:, lanes_of(pair)] = acc[lanes_of(pair), :].T.astype(BF16)
    for store in stores:
        store.wait()


def forward_far(far, other, gain, bias, w, qv_bias, qt, code, top, total, acc):
    padded, width = far.shape
    half = width // 2
    heads = half // HEAD_DIM
    rows = 2 * (padded - 16)
    specs = [VMEM] * 9 + [HBM] * 2
    kept = (((width, rows), BF16), ((rows, width), BF16), ((half, rows), BF16))
    outs = (((8, rows), F32), ((rows, half), BF16), ((8, rows), F32)) + kept
    scratch = [
        pltpu.SMEM((rows // TILE, rows // TILE), jnp.int32),
        pltpu.VMEM((heads, rows, 128), BF16),
        pltpu.VMEM((heads, 128, rows), BF16),
        pltpu.VMEM((half, rows), BF16),
        pltpu.VMEM((8, rows), F32),
        pltpu.VMEM((8, rows), F32),
        pltpu.VMEM((half, rows), F32),
        pltpu.VMEM((width, width), BF16),
        pltpu.VMEM((half, rows), BF16),
    ]
    scratch += [pltpu.VMEM(shape, kind) for shape, kind in kept] + [pltpu.SemaphoreType.DMA((5,))]
    run = call(partial(far_kernel, heads=heads), "far_forward", outs, scratch, specs, (VMEM,) * 3 + (HBM,) * 3)
    return run(far, other, gain, bias, qv_bias, code, top, total, acc, w, qt)


def back_kernel(*refs, heads, near, unit):
    half = heads * HEAD_DIM
    if near:
        (bits_ref, q_code_ref, k_code_ref, lse_ref, do_ref, dq_ref, far_sums_ref, far_v_ref, gain_ref, bias_ref) = refs[:10]
        early_ref, qt_hbm, kv_hbm, ot_hbm, w_hbm, *more = refs[10:20]
        send_ref, send_one, keep_one, send_two, keep_two, dx_hbm = refs[20:26]
        act, kx, qx, kt, dox, delta, qt_ref, kv_ref, ot_ref, w_ref, dk_sum, dv_sum, sems, dx_v, dq_sum = refs[26:41]
        out_ref, normed_v, far_normed_v, far_grad_v, got_v, grad_half_v, small_v = refs[41:]
        stored = (dx_v, dx_hbm)
        pairs = tuple(zip(more, (normed_v, far_normed_v, far_grad_v, got_v, grad_half_v)))
        later = [begin(sems, 5 + i, source, target) for i, (source, target) in enumerate(pairs)]
    else:
        q_code_ref, k_code_ref, lse_ref, do_ref, qt_hbm, kv_hbm, ot_hbm, w_hbm = refs[:8]
        dx_ref, send_ref, dq_sum, sums_ref, v_ref, out_hbm = refs[8:14]
        act, kx, qx, kt, dox, delta, qt_ref, kv_ref, ot_ref, w_ref, dk_sum, dv_sum, sems, out_ref = refs[14:]
        stored = (out_ref, out_hbm)
    held = w_hbm if near else w_hbm.at[:, half:]
    pairs = ((qt_hbm, qt_ref), (kv_hbm, kv_ref), (ot_hbm, ot_ref), (held, w_ref))
    loads = [begin(sems, i, source, target) for i, (source, target) in enumerate(pairs)]
    queries, keys = qt_ref.shape[1], kv_ref.shape[0]
    for load in loads[:3]:
        load.wait()
    q_code, k_code = q_code_ref[0:1, :], k_code_ref[0:1, :]
    note_tiles(q_code, k_code, act)
    load_queries(qt_ref, q_code, qx, heads)
    load_keys(kv_ref, 0, k_code, kx, heads)
    zero = jnp.zeros((HEAD_DIM, queries), BF16)
    for h in range(heads):
        own = slice(0, HEAD_DIM) if h % 2 == 0 else slice(HEAD_DIM, 128)
        rest = slice(HEAD_DIM, 128) if h % 2 == 0 else slice(0, HEAD_DIM)
        grad = do_ref[rows_of(h), :]
        dox[h, own, :] = grad
        dox[h, rest, :] = zero
        delta[h : h + 1, :] = jnp.sum(grad.astype(F32) * ot_ref[rows_of(h), :].astype(F32), 0, keepdims=True)
    for pair in range(heads // 2):
        kt[lanes_of(pair), :] = kv_ref[:, lanes_of(pair)].astype(F32).T.astype(BF16)
    dq_sum[...] = dq_ref[...] if near else jnp.zeros_like(dq_sum)
    dk_sum[...] = jnp.zeros_like(dk_sum)
    dv_sum[...] = jnp.zeros_like(dv_sum)
    loads[3].wait()
    group = 3 if heads % 3 == 0 else 2

    def body(at, span):
        for first in range(0, heads, group):
            hs = range(first, first + group)
            scores = {h: mm(kx[h, span, :], qx[h, :, at]) for h in hs}
            dp = {h: mm(kv_ref[span, half + (h // 2) * 128 : half + (h // 2 + 1) * 128], dox[h, :, at]) for h in hs}
            probs = {h: jnp.exp(scores[h] - lse_ref[h : h + 1, at]) for h in hs}
            rounded = {h: probs[h].astype(BF16) for h in hs}
            ds = {h: (probs[h] * (dp[h] - delta[h : h + 1, at])).astype(BF16) for h in hs}
            dv = {h: mm(do_ref[rows_of(h), at], rounded[h], NT) for h in hs}
            dk = {h: mm(qt_ref[rows_of(h), at], ds[h], NT) for h in hs}
            dq = {h: mm(kt[rows_of(h), span], ds[h]) for h in hs}
            for h in hs:
                dv_sum[rows_of(h), span] += dv[h]
                dk_sum[rows_of(h), span] += dk[h]
                dq_sum[rows_of(h), at] += dq[h]

    each_tile(act, queries, keys, body)
    base = half if near else 0
    for pair in range(heads // 2):
        lanes = lanes_of(pair)
        if near:
            out_ref[:, lanes] = (dq_sum[lanes, :] * attn_scale).T.astype(BF16)
        out_ref[:, base + pair * 128 : base + (pair + 1) * 128] = dk_sum[lanes, :].T.astype(BF16)
        out_ref[:, base + half + pair * 128 : base + half + (pair + 1) * 128] = dv_sum[lanes, :].T.astype(BF16)
    sums = jnp.sum(out_ref[...].astype(F32), 0, keepdims=True)
    block = keys // 2
    stores = [] if near else [begin(sems, 4, *stored)]
    for start in range(0, block, TILE):
        at = slice(start, start + TILE)
        send_ref[at, :] = mm(out_ref[block + start : block + start + TILE, :], w_ref[...], NT).astype(BF16)
    for start in range(0, block, TILE):
        at = slice(start, start + TILE)
        part = mm(out_ref[at, :], w_ref[...], NT)
        if near:
            dx_v[at, :] = part
        else:
            dx_ref[at, :] = part
    v_column = jnp.sum(dv_sum[...], 1, keepdims=True)
    if not near:
        sums_ref[...] = jnp.broadcast_to(sums, sums_ref.shape)
        v_ref[...] = jnp.broadcast_to(v_column, v_ref.shape)
        stores[0].wait()
        return
    stores = [begin(sems, 4, *stored)]
    for load in later:
        load.wait()
    small_v[...] = early_ref[...]
    core = bits_ref[2]
    lane = lane_of((half // 2, 128))
    q_column = jnp.sum(dq_sum[...], 1, keepdims=True) * attn_scale
    for base, column in ((0, q_column), (half, v_column + far_v_ref[:, :1])):
        mine = pl.ds(pl.multiple_of(base + core * (half // 2), 8), half // 2)
        for j, piece in enumerate(interleaved(column, unit, 2)):
            small_v[mine, :] += jnp.where(lane == 10 + j, piece, 0.0)
    sums = jnp.concatenate([sums[:, :half], sums[:, half:] + far_sums_ref[0:1, :]], 1)
    gain, bias = gain_ref[...].astype(F32), bias_ref[...].astype(F32)
    cut = send_two.shape[2]
    for step in range(2 * half // ROW_STEP):
        at = slice(step * ROW_STEP, (step + 1) * ROW_STEP)
        out_q = mm(normed_v[at, :], out_ref[:, :half])
        out_kv = mm(normed_v[at, :], out_ref[:, half:]) + mm(far_normed_v[at, :], far_grad_v[...])
        out = jnp.concatenate([out_q, out_kv], 1)
        columns = small_v[at, :] + ln_columns(out, w_ref[at, :].astype(F32), sums, gain[:, at], bias[:, at], 0)
        deal_part(bits_ref[3], out[:, :cut], send_two, keep_two, step)

        def rest(proj):
            deal_part(bits_ref[1], jnp.concatenate([out[:, cut:], proj, columns], 1), send_one, keep_one, step)

        low, high = grad_half_v[:block, :], grad_half_v[block:, :]

        @pl.when(core == step)
        def _():
            rest(mm(ot_ref[:, :block], low) + mm(ot_ref[:, block:], high))

        @pl.when(core != step)
        def _():
            rest(mm(got_v[:block, :], high, TN) + mm(got_v[block:, :], low, TN))

    stores[0].wait()


def attend_back(after, unit, qt, q_code, k_code, kv, ot, lse, do, w, dq=None, bits=None, smalls=(), moved=()):
    half, queries = qt.shape
    keys = kv.shape[0]
    heads = half // HEAD_DIM
    width = 2 * half
    near = dq is not None
    wide = 3 * half if near else width
    grad, passed = ((keys, wide), BF16), ((keys // 2, width), BF16)
    dx, dq_shape = ((keys // 2, width), F32), ((half, queries), F32)
    if near:
        cut = (4 * half // 128 + 1) // 2 * 128
        one, two = dealt(width, 4 * unit, wide - cut + half + 128)[0], dealt(width, 8 * unit, cut)[0]
        outs = (passed, *one, *two, dx)
    else:
        outs = (dx, passed, dq_shape, ((8, wide), F32), ((half, 128), F32), grad)
    out_specs = (VMEM,) * (len(outs) - 1) + (HBM,)
    scratch = [
        pltpu.SMEM((queries // TILE, keys // TILE), jnp.int32),
        pltpu.VMEM((heads, keys, 128), BF16),
        pltpu.VMEM((heads, 128, queries), BF16),
        pltpu.VMEM((half, keys), BF16),
        pltpu.VMEM((heads, 128, queries), BF16),
        pltpu.VMEM((8, queries), F32),
        pltpu.VMEM((half, queries), BF16),
        pltpu.VMEM((keys, width), BF16),
        pltpu.VMEM((half, queries), BF16),
        pltpu.VMEM((width, wide), BF16),
        pltpu.VMEM((half, keys), F32),
        pltpu.VMEM((half, keys), F32),
        pltpu.SemaphoreType.DMA((10,)),
        pltpu.VMEM(*outs[-1]),
    ]
    small, held, prefetch = [q_code, k_code, lse, do], [qt, kv, ot, w], ()
    if near:
        scratch += [pltpu.VMEM((half, queries), F32), pltpu.VMEM(*grad)]
        scratch += [pltpu.VMEM(array.shape, array.dtype) for array in moved] + [pltpu.VMEM((width, 128), F32)]
        small, held, prefetch = small + [dq, *smalls], held + list(moved), (bits,)
    name = "near_backward" if near else "far_backward"
    specs = [VMEM] * len(small) + [HBM] * len(held)
    kernel = partial(back_kernel, heads=heads, near=near, unit=unit)
    run = call(kernel, name, outs, scratch, specs, out_specs, prefetch=len(prefetch), after=after)
    return run(*prefetch, *small, *held)


def keep_column(code_ref, flags_ref, branch, images):
    code = jnp.minimum(code_ref[0:1, :], float(PAD_CLASS - 1))
    kept = jnp.zeros_like(code)
    for image in range(images):
        kept = kept + jnp.where(code == image, flags_ref[branch, image].astype(F32), 0.0)
    return jnp.broadcast_to(kept / keep_rate, (128, code.shape[1])).T[:, :1]


def gelu_both(hidden):
    size = jnp.abs(hidden)
    bell = jnp.exp(-0.5 * hidden * hidden)
    t = 1.0 / (1.0 + 0.23164189 * size)
    tail = ((((0.5307027145 * t - 0.7265760135) * t + 0.7107068705) * t - 0.142248368) * t + 0.127414796) * t * bell
    cdf = jnp.where(hidden >= 0, 1.0 - tail, tail)
    return hidden * cdf, cdf + hidden * (bell * 0.3989422804014327)


def mlp_kernel(
    core_ref,
    flags_ref,
    code_ref,
    mine_ref,
    other_ref,
    own_ref,
    got_ref,
    cot_mine_ref,
    cot_other_ref,
    w_own_ref,
    w_got_ref,
    b_proj_ref,
    gain_ref,
    bias_ref,
    w_up_ref,
    b_up_ref,
    w_down_ref,
    middle_ref,
    normed_ref,
    active_ref,
    grad_hidden_ref,
    grad_down_ref,
    part_ref,
    down_ref,
    up_sums_ref,
    small_ref,
    down_sums_ref,
    *,
    images,
    unit,
):
    step = pl.program_id(0)
    keep_attn = keep_column(code_ref, flags_ref, 0, images)
    keep_mlp = keep_column(code_ref, flags_ref, 1, images)
    branch = mm(own_ref[...], w_own_ref[...]) + mm(got_ref[...], w_got_ref[...]) + b_proj_ref[...].astype(F32)
    early = step < pl.num_programs(0) // 2
    middle = jnp.where(early, mine_ref[...], other_ref[...]).astype(F32) + keep_attn * branch
    middle_ref[...] = middle
    normed = (centre(middle)[0] * gain_ref[...].astype(F32) + bias_ref[...].astype(F32)).astype(BF16)
    normed_ref[...] = normed
    cot = jnp.where(early, cot_mine_ref[...], cot_other_ref[...])
    grad_down = (keep_mlp * cot.astype(F32)).astype(BF16)
    grad_down_ref[...] = grad_down

    @pl.when(step == 0)
    def _():
        up_sums_ref[...] = jnp.zeros_like(up_sums_ref)
        down_sums_ref[...] = jnp.zeros_like(down_sums_ref)

    @pl.when(step < pl.num_programs(0) // 2)
    def _():
        down_sums_ref[...] += jnp.sum(grad_down.astype(F32), 0, keepdims=True)

    units = w_up_ref.shape[1]
    chunk = 512
    for start in range(0, units, chunk):
        cols = slice(start, start + chunk)
        hidden = mm(normed, w_up_ref[:, cols]) + b_up_ref[:, cols].astype(F32)
        active, slope = gelu_both(hidden)
        active_ref[:, cols] = active.astype(BF16)
        grad_hidden = (mm(grad_down, w_down_ref[cols, :], NT) * slope).astype(BF16)
        grad_hidden_ref[:, cols] = grad_hidden
        up_sums_ref[:, cols] += jnp.sum(grad_hidden.astype(F32), 0, keepdims=True)
    down_ref[...] = mm(active_ref[...], w_down_ref[...]).astype(BF16)
    part_ref[...] = mm(grad_hidden_ref[...], w_up_ref[...], NT).astype(BF16)

    @pl.when(step == pl.num_programs(0) - 1)
    def _():
        lane = lane_of(small_ref.shape)
        small_ref[...] = jnp.where(lane == 5, upright(down_sums_ref[...]), 0.0)
        half = w_own_ref.shape[0]
        mine = pl.ds(pl.multiple_of(core_ref[0] * half, 8), half)
        lane = lane_of((half, 128))
        for j, column in enumerate(interleaved(upright(up_sums_ref[...]), unit, units // half)):
            small_ref[mine, :] += jnp.where(lane == 6 + j, column, 0.0)


def mlp(after, unit, core, flags, code, mine, other, own, got, cot_mine, cot_other, proj_weight, proj_bias, gain, bias, fc1_weight, fc1_bias, fc2_weight):
    rows, width = 2 * cot_mine.shape[0], cot_mine.shape[1]
    half, units = width // 2, fc1_weight.shape[1] // 2
    steps = rows // TILE

    def tile(cols, shift=0):
        return pl.BlockSpec((TILE, cols), lambda i, c: ((i + shift) % steps, 0))

    one = pl.BlockSpec((1, width), lambda i, c: (0, 0))
    late = steps // 2
    first = pl.BlockSpec((TILE, width), lambda i, c: (jnp.minimum(i, late - 1), 0))
    second = pl.BlockSpec((TILE, width), lambda i, c: (jnp.maximum(i - late, 0), 0))
    specs = [
        SMEM,
        pl.BlockSpec((8, TILE), lambda i, c: (0, i)),
        first,
        second,
        tile(half),
        tile(half, late),
        first,
        second,
        pl.BlockSpec((half, width), lambda i, c: (c[0], 0)),
        pl.BlockSpec((half, width), lambda i, c: (1 - c[0], 0)),
        one,
        one,
        one,
        pl.BlockSpec((width, units), lambda i, c: (0, c[0])),
        pl.BlockSpec((1, units), lambda i, c: (0, c[0])),
        pl.BlockSpec((units, width), lambda i, c: (c[0], 0)),
    ]
    outs = (
        ((rows, width), F32),
        ((rows, width), BF16),
        ((rows, units), BF16),
        ((rows, units), BF16),
        ((rows, width), BF16),
        ((rows, width), BF16),
        ((rows, width), BF16),
        ((1, units), F32),
        ((width, 128), F32),
    )
    out_specs = (
        tile(width),
        tile(width),
        tile(units),
        tile(units),
        tile(width),
        tile(width),
        tile(width),
        pl.BlockSpec((1, units), lambda i, c: (0, 0)),
        pl.BlockSpec((width, 128), lambda i, c: (0, 0)),
    )
    kernel = partial(mlp_kernel, images=flags.shape[1], unit=unit)
    scratch = [pltpu.VMEM((1, width), F32)]
    hold = (True, False, False, False, False, False, True, False, False)
    run = call(
        kernel,
        "mlp",
        outs,
        scratch,
        specs,
        out_specs,
        (steps,),
        prefetch=1,
        after=after,
        pin=(2, 3, 6, 7, 8, 9, 13, 15),
        hold=hold,
    )
    return run(
        core,
        flags,
        code,
        mine,
        other,
        own,
        got,
        cot_mine,
        cot_other,
        proj_weight,
        proj_weight,
        proj_bias,
        gain,
        bias,
        fc1_weight,
        fc1_bias,
        fc2_weight,
    )


def middle_kernel(
    core_ref,
    flags_ref,
    code_ref,
    part_ref,
    got_ref,
    middle_ref,
    cot_mine_ref,
    cot_other_ref,
    gain_ref,
    w_ref,
    early_ref,
    grad_middle_ref,
    grad_half_ref,
    do_ref,
    small_ref,
    sums_ref,
    *,
    images,
):
    step = pl.program_id(0)
    keep_attn = keep_column(code_ref, flags_ref, 0, images)
    unit, scale = centre(middle_ref[...])
    grad = (part_ref[...].astype(F32) + got_ref[...].astype(F32)) * gain_ref[...].astype(F32)
    early = step < pl.num_programs(0) // 2
    cot = jnp.where(early, cot_other_ref[...], cot_mine_ref[...]).astype(F32)
    grad_middle = cot + norm_back(unit, scale, grad)
    grad_middle_ref[...] = grad_middle
    grad_proj = (keep_attn * grad_middle).astype(BF16)
    half = w_ref.shape[0]
    grad_half_ref[...] = jnp.where(core_ref[0] == 0, grad_proj[:, :half], grad_proj[:, half:])
    do_ref[...] = mm(w_ref[...], grad_proj, NT).astype(BF16)

    @pl.when(step == 0)
    def _():
        sums_ref[...] = jnp.zeros_like(sums_ref)

    @pl.when(step >= pl.num_programs(0) // 2)
    def _():
        sums_ref[...] += jnp.sum(grad_proj.astype(F32), 0, keepdims=True)

    @pl.when(step == pl.num_programs(0) - 1)
    def _():
        lane = lane_of(small_ref.shape)
        small_ref[...] = early_ref[...] + jnp.where(lane == 4, upright(sums_ref[...]), 0.0)


def middle_back(after, core, flags, code, part, got, middle, cot_mine, cot_other, gain, proj_weight, early):
    rows, width = part.shape
    half = width // 2
    steps = rows // TILE
    late = steps // 2

    def tile(cols, shift=late):
        return pl.BlockSpec((TILE, cols), lambda i, c: ((i + shift) % steps, 0))

    one = pl.BlockSpec((1, width), lambda i, c: (0, 0))
    specs = [
        SMEM,
        pl.BlockSpec((8, TILE), lambda i, c: (0, (i + late) % steps)),
        tile(width),
        tile(width, 0),
        tile(width),
        pl.BlockSpec((TILE, width), lambda i, c: (jnp.maximum(i - late, 0), 0)),
        pl.BlockSpec((TILE, width), lambda i, c: (jnp.minimum(i, late - 1), 0)),
        one,
        pl.BlockSpec((half, width), lambda i, c: (c[0], 0)),
        pl.BlockSpec((width, 128), lambda i, c: (0, 0)),
    ]
    outs = (((rows // 2, width), F32), ((rows, half), BF16), ((half, rows), BF16), ((width, 128), F32))
    out_specs = (
        pl.BlockSpec((TILE, width), lambda i, c: (jnp.maximum(i - late, 0), 0)),
        tile(half),
        pl.BlockSpec((half, TILE), lambda i, c: (0, (i + late) % steps)),
        pl.BlockSpec((width, 128), lambda i, c: (0, 0)),
    )
    kernel = partial(middle_kernel, images=flags.shape[1])
    run = call(
        kernel,
        "middle_backward",
        outs,
        [pltpu.VMEM((1, width), F32)],
        specs,
        out_specs,
        (steps,),
        prefetch=1,
        after=after,
        pin=(4, 5, 6, 8),
        hold=(True, True, False, False),
    )
    return run(core, flags, code, part, got, middle, cot_mine, cot_other, gain, proj_weight, early)


def deal(bit, rows, send_ref, keep_ref):
    run = send_ref.shape[1]
    for i in range(send_ref.shape[0]):
        low, high = rows[2 * i * run : (2 * i + 1) * run], rows[(2 * i + 1) * run : (2 * i + 2) * run]
        send_ref[i] = jnp.where(bit == 0, high, low).astype(BF16)
        keep_ref[i] = jnp.where(bit == 0, low, high).astype(BF16)


def deal_part(bit, rows, send_ref, keep_ref, step):
    count = rows.shape[0] // (2 * send_ref.shape[1])
    part = pl.ds(step * count, count)
    deal(bit, rows, send_ref.at[part], keep_ref.at[part])


def dealt(height, run, width):
    shape = (height // (2 * run), run, width)
    count = ROW_STEP // (2 * run)
    return [(shape, BF16)] * 2, [pl.BlockSpec((count, run, width), lambda i, *_: (i, 0, 0))] * 2


def down_kernel(bits_ref, left_ref, right_ref, send_ref, keep_ref):
    deal(bits_ref[0], mm(left_ref[...], right_ref[...], TN), send_ref, keep_ref)


def down_product(after, bits, left, right, run):
    rows, height = left.shape
    width = right.shape[1]
    specs = [pl.BlockSpec((rows, ROW_STEP), lambda i, b: (0, i)), pl.BlockSpec((rows, width), lambda i, b: (0, 0))]
    outs, out_specs = dealt(height, run, width)
    grid = (height // ROW_STEP,)
    return call(down_kernel, "down_weight", outs, [], specs, out_specs, grid, prefetch=1, after=after)(bits, left, right)


def up_kernel(
    bits_ref, normed_ref, grad_ref, w_ref, sums_ref, gain_ref, bias_ref, early_ref, send_ref, keep_ref, small_ref
):
    out = mm(normed_ref[...], grad_ref[...], TN)
    deal(bits_ref[1], out, send_ref, keep_ref)
    gain, bias = gain_ref[...].astype(F32), bias_ref[...].astype(F32)
    small_ref[...] = early_ref[...] + ln_columns(out, w_ref[...].astype(F32), sums_ref[...], gain, bias, 2)


def upright(row):
    return jnp.broadcast_to(row, (128, row.shape[1])).T


def lane_of(shape):
    return lax.broadcasted_iota(jnp.int32, shape, 1)


def interleaved(column, unit, parts):
    blocks = column.shape[0] // (unit * parts)
    out = []
    for j in range(parts):
        pieces = [column[(k * parts + j) * unit : (k * parts + j + 1) * unit] for k in range(blocks)]
        out.append(jnp.concatenate(pieces, 0))
    return out


def ln_columns(grad, weight, sums, gain_ref, bias_ref, place):
    first = jnp.sum(weight * grad, 1, keepdims=True)
    second = jnp.sum(weight * sums, 1, keepdims=True)
    lane = lane_of((weight.shape[0], 128))
    scaled = (first - upright(bias_ref) * second) / upright(gain_ref)
    return jnp.where(lane == place, scaled, jnp.where(lane == place + 1, second, 0.0))


def up_product(after, bits, normed, grad, weight, sums, gain, bias, early, run):
    rows, width = normed.shape
    units = grad.shape[1]
    part = pl.BlockSpec((1, ROW_STEP), lambda i, b: (0, i))
    specs = [
        pl.BlockSpec((rows, ROW_STEP), lambda i, b: (0, i)),
        pl.BlockSpec((rows, units), lambda i, b: (0, 0)),
        pl.BlockSpec((ROW_STEP, units), lambda i, b: (i, b[2])),
        pl.BlockSpec((1, units), lambda i, b: (0, 0)),
        part,
        part,
        pl.BlockSpec((ROW_STEP, 128), lambda i, b: (i, 0)),
    ]
    outs, out_specs = dealt(width, run, units)
    outs, out_specs = outs + [((width, 128), F32)], out_specs + [pl.BlockSpec((ROW_STEP, 128), lambda i, b: (i, 0))]
    grid = (width // ROW_STEP,)
    call_up = call(up_kernel, "up_weight", outs, [], specs, out_specs, grid, prefetch=1, after=after, pin=(2,))
    return call_up(bits, normed, grad, weight, sums, gain, bias, early)


def add_kernel(left_ref, right_ref, out_ref):
    out_ref[...] = (left_ref[...].astype(F32) + right_ref[...].astype(F32)).astype(out_ref.dtype)


def add(after, left, right):
    run = call(add_kernel, "add_blocks", ((left.shape, BF16),), [], [VMEM, VMEM], after=after)
    return run(left, right)[0]


def finish_kernel(x_ref, dx_ref, beside_ref, across_ref, gain_ref, middle_ref, out_ref):
    unit, scale = centre(x_ref[...].astype(F32))
    grad = dx_ref[...] + beside_ref[...].astype(F32) + across_ref[...].astype(F32)
    out_ref[...] = (middle_ref[...] + norm_back(unit, scale, grad * gain_ref[...].astype(F32))).astype(BF16)


def finish(after, x, dx, beside, across, gain, middle):
    rows, width = x.shape
    tile = pl.BlockSpec((TILE, width), lambda i: (i, 0))
    one = pl.BlockSpec((1, width), lambda i: (0, 0))
    specs = [tile, tile, tile, tile, one, tile]
    run = call(finish_kernel, "token_gradient", ((x.shape, BF16),), [], specs, (tile,), (rows // TILE,), after=after)
    return run(x, dx, beside, across, gain, middle)[0]


def output_kernel(flags_ref, code_ref, middle_ref, down_ref, got_ref, bias_ref, out_ref, *, images):
    kept = keep_column(code_ref, flags_ref, 1, images)
    branch = down_ref[...].astype(F32) + got_ref[...].astype(F32) + bias_ref[...].astype(F32)
    out_ref[...] = (middle_ref[...] + kept * branch).astype(BF16)


def layer_out(after, flags, code, middle, down, got, bias):
    rows, width = got.shape
    tile = pl.BlockSpec((TILE, width), lambda i: (i, 0))
    one = pl.BlockSpec((1, width), lambda i: (0, 0))
    specs = [SMEM, pl.BlockSpec((8, TILE), lambda i: (0, i)), tile, tile, tile, one]
    kernel = partial(output_kernel, images=flags.shape[1])
    run = call(kernel, "layer_output", ((got.shape, BF16),), [], specs, (tile,), (rows // TILE,), after=after)
    return run(flags, code, middle, down, got, bias)[0]


def swap_halves(rows):
    half = rows.shape[0] // 2
    return jnp.concatenate([rows[half:], rows[:half]], 0)


def pick(array, index, dim):
    return lax.dynamic_index_in_dim(array, index, dim, keepdims=False)


class Links:
    def __init__(self, mesh):
        self.dp, self.blk = mesh.shape["dp"], mesh.shape["blk"]
        self.bits = self.dp.bit_length() - 1

    def core(self, value):
        return lax.ppermute(value, "blk", [(i, i ^ 1) for i in range(self.blk)])

    def side(self, value):
        return lax.ppermute(value, "blk", [(i, i ^ 2) for i in range(self.blk)])

    def cross(self, value, step):
        if step == "x":
            return self.side(value)
        return lax.ppermute(value, "dp", [(i, i ^ (1 << step)) for i in range(self.dp)])

    def bit(self, step):
        if step == "x":
            return lax.axis_index("blk") // 2
        return (lax.axis_index("dp") >> step) & 1

    def swap(self, value):
        top = self.dp // 2
        pairs = []
        for d in range(self.dp):
            for b in range(self.blk):
                high, core = d // top, b % 2
                pairs.append((d * self.blk + b, (d % top + core * top) * self.blk + (b - core + high)))
        return lax.ppermute(value, ("dp", "blk"), pairs)


class Portion:
    def __init__(self, links, send, keep, dims, order):
        self.links, self.order = links, list(order)
        self.dims = [dim for dim in dims if dim != order[0]]
        self.tail = (send.shape[0] * send.shape[1] // 2 ** len(self.dims), send.shape[2])
        self.kept = keep
        self.arrived = links.cross(send, order[0])

    def advance(self, after):
        links = self.links
        self.order.pop(0)
        if not self.order:
            kept, arrived = self.kept.reshape(self.tail), self.arrived.reshape(self.tail)
            self.total = call(add_kernel, "sum_last", ((self.tail, F32),), [], [VMEM] * 2, after=after)(kept, arrived)[0]
            return self.total
        follow = self.order[0]
        spot = self.dims.index(follow)
        self.dims.pop(spot)
        outer, inner = 2**spot, 2 ** (len(self.dims) - spot)
        shape = (outer, inner) + self.tail
        view = (outer, 2, inner) + self.tail

        def kernel(bit_ref, kept_ref, arrived_ref, send_ref, keep_ref):
            for out_ref, where in ((send_ref, 1 - bit_ref[0]), (keep_ref, bit_ref[0])):
                out_ref[...] = (kept_ref[:, where].astype(F32) + arrived_ref[:, where].astype(F32)).astype(BF16)

        run = call(kernel, "sum_half", ((shape, BF16), (shape, BF16)), [], [VMEM] * 2, prefetch=1, after=after)
        send, keep = run(links.bit(follow).reshape(1).astype(jnp.int32), self.kept.reshape(view), self.arrived.reshape(view))
        self.kept = keep
        self.arrived = links.cross(send, follow)
        return keep


def local(
    links,
    tokens,
    cotangent,
    segments,
    padding,
    drop_keep,
    ln1_gain,
    ln1_bias,
    qkv_weight,
    qv_bias,
    proj_weight,
    proj_bias,
    ln2_gain,
    ln2_bias,
    fc1_weight,
    fc1_bias,
    fc2_weight,
    fc2_bias,
):
    _, block, width = tokens.shape
    half = width // 2
    units = fc1_weight.shape[1] // 2
    core = lax.axis_index("blk") % 2
    core_arg = core.reshape(1).astype(jnp.int32)
    owners = links.dp * links.blk
    rows = 2 * block

    code = jnp.where(padding == 1, segments, PAD_CLASS).astype(BF16)
    mine = jnp.concatenate([tokens[0], jnp.pad(code, ((0, 15), (0, width - block)))], 0)
    far = links.side(mine)
    other = links.core(mine)
    cot_mine = cotangent[0]
    cot_other = links.core(cot_mine)
    flags = drop_keep[:, 0, :]
    bits = links.bits
    low = [bits - 1 - i for i in range(bits)]
    chip = low + ["x"]
    by_core = low[1:] + ["x", low[0]]
    tail = [s for s in low if s > 1][::-1]
    side_bits = jnp.stack([links.bit("x"), links.bit(0), core, links.bit(1)]).astype(jnp.int32)
    unit = width // owners

    gain_one, bias_one = ln1_gain.reshape(1, -1), ln1_bias.reshape(1, -1)
    gain_two, bias_two = ln2_gain.reshape(1, -1), ln2_bias.reshape(1, -1)
    bias_qv = qv_bias.reshape(1, -1)
    near_code, top, total, acc, near_normed, w_qkv, qt, near_kv = forward_near(
        core_arg, mine, other, gain_one, bias_one, qkv_weight, bias_qv
    )
    far = lax.dynamic_update_slice(far, near_code[:, :128].astype(BF16), (block + 8, 0))
    far_other = links.core(far)
    bias_v = lax.dynamic_slice(bias_qv, (0, width + core * half), (1, half))
    far_code, own, lse, far_normed, far_kv, ot = forward_far(
        far, far_other, gain_one, bias_one, w_qkv, bias_v, qt, near_code, top, total, acc
    )
    got = links.core(own)
    middle, normed_two, active, grad_hidden, grad_down, part, down, up_sums, small = mlp(
        (),
        unit,
        core_arg,
        flags,
        near_code,
        tokens[0],
        other,
        own,
        got,
        cot_mine,
        cot_other,
        proj_weight,
        proj_bias.reshape(1, -1),
        gain_two,
        bias_two,
        fc1_weight,
        fc1_bias.reshape(1, -1),
        fc2_weight,
    )
    got_part = links.core(part)
    down_other = links.core(down[block:])

    send, keep = down_product((part,), side_bits, active, grad_down, 2 * fc2_weight.shape[0] // owners)
    down_portion = Portion(links, send, keep, by_core, ["x", 0, 1] + tail)
    send, keep, small = up_product(
        (keep,),
        side_bits,
        normed_two,
        grad_hidden,
        fc1_weight,
        up_sums,
        gain_two,
        bias_two,
        small,
        4 * unit,
    )
    up_portion = Portion(links, send, keep, chip, [0, 1, "x"] + tail)
    grad_middle, grad_half, do, small = middle_back(
        (keep,), core_arg, flags, near_code, part, got_part, middle, cot_mine, cot_other, gain_two, proj_weight, small
    )
    far_dx, far_send, dq, far_sums, far_v, far_grad = attend_back(
        (), unit, qt, near_code, far_code, far_kv, ot, lse, do, w_qkv
    )
    last = down_portion.advance((far_grad,))
    last = up_portion.advance((last,))
    far_sum = add((last,), far_dx, links.core(far_send))
    across = links.side(far_sum)
    near_send, send_one, keep_one, send_two, keep_two, near_dx = attend_back(
        (far_sum,),
        unit,
        qt,
        near_code,
        near_code,
        near_kv,
        ot,
        lse,
        do,
        w_qkv,
        dq,
        side_bits,
        (far_sums, far_v, gain_one, bias_one, small),
        (near_normed, far_normed, far_grad, got, grad_half),
    )
    last = down_portion.advance((near_dx,))
    last = up_portion.advance((last,))
    one_portion = Portion(links, send_one, keep_one, chip, [0, "x", 1] + tail)
    two_portion = Portion(links, send_two, keep_two, chip, [1, 0, "x"] + tail)
    last = down_portion.advance((last,))
    last = up_portion.advance((last,))
    layer_output = layer_out((last,), flags, near_code, middle, down, down_other, fc2_bias.reshape(1, -1))
    last = layer_output
    for _ in tail:
        last = one_portion.advance((last,))
        last = two_portion.advance((last,))
        last = down_portion.advance((last,))
        last = up_portion.advance((last,))
    down_part, up_part = down_portion.total, up_portion.total
    tokens_grad = finish((last,), tokens[0], near_dx, links.core(near_send), across, gain_one, grad_middle)
    last = tokens_grad
    while one_portion.order:
        last = one_portion.advance((last,))
        last = two_portion.advance((last,))
    one_part, two_part = one_portion.total, two_portion.total

    def split(array):
        array = array.reshape(2, width // owners, -1)
        return pick(array, core, 0), links.core(pick(array, 1 - core, 0))

    def join(kept, arrived):
        return jnp.where(core == 0, jnp.concatenate([kept, arrived], 1), jnp.concatenate([arrived, kept], 1))

    down_grad = links.swap(down_part)
    kept, arrived = split(up_part)
    up_grad = join(kept, arrived)
    kept, arrived = split(jnp.concatenate([two_part, one_part], 1))
    parts = [join(kept[:, i * half : (i + 1) * half], arrived[:, i * half : (i + 1) * half]) for i in range(4)]
    qkv_grad, proj_grad = jnp.concatenate(parts[:3], 1), parts[3]
    small = kept[:, 4 * half :] + arrived[:, 4 * half :]
    g1, b1, g2, b2, pb, d2 = (small[:, i] for i in range(6))
    u1, qvb = small[:, 6:10].T.reshape(-1), small[:, 10:12].T.reshape(-1)
    shape = tokens.shape
    return (
        layer_output.reshape(shape),
        tokens_grad.reshape(shape),
        g1,
        b1,
        qkv_grad,
        qvb,
        proj_grad,
        pb,
        g2,
        b2,
        up_grad,
        u1,
        down_grad,
        d2,
    )


def solution(mesh):
    both = P(("dp", "blk"))
    rows = P(("dp", "blk"), None)
    token = P("dp", "blk", None)
    placed = (token, token, P("dp", "blk"), P("dp", "blk"), P(None, "dp", None)) + (P(),) * 12
    return jax.shard_map(
        partial(local, Links(mesh)),
        mesh=mesh,
        in_specs=placed,
        out_specs=(token, token, both, both, rows, both, rows, both, both, both, rows, both, rows, both),
        check_vma=False,
    )
```

```python
from functools import partial

import jax
import jax.numpy as jnp
from jax import lax
from jax.experimental import pallas as pl
from jax.experimental.pallas import tpu as pltpu
from jax.sharding import PartitionSpec as P

HEAD_DIM = 64
F32 = jnp.float32
BF16 = jnp.bfloat16
epsilon = 1e-06
keep_rate = 0.9
attn_scale = 0.125
negative = -1e30
PAD_CLASS = 4
TILE = 256
MIB = 2**20
FLOPS_PER_US = 1.0 * 10**9
BUDGET = {
    "near_forward": (28, 15),
    "far_forward": (28, 12),
    "mlp": (52, 30),
    "far_backward": (48, 20),
    "near_backward_first": (48, 16),
    "near_backward_last": (48, 15),
    "join_up": (8, 1),
    "join_all": (8, 1),
    "sum_half": (8, 2),
    "sum_last": (8, 1),
    "add_blocks": (8, 2),
    "token_gradient": (12, 2),
    "layer_output": (12, 2),
}
NN = ((1,), (0,))
NT = ((1,), (1,))
TN = ((0,), (0,))
VMEM = pl.BlockSpec(memory_space=pltpu.VMEM)
SMEM = pl.BlockSpec(memory_space=pltpu.SMEM)
HBM = pl.BlockSpec(memory_space=pltpu.HBM)
ROW_STEP = 384


def mm(left, right, dims=NN):
    return lax.dot_general(left, right, (dims, ((), ())), preferred_element_type=F32)


def rows_of(head):
    return slice(head * HEAD_DIM, (head + 1) * HEAD_DIM)


def lanes_of(pair):
    return slice(pair * 128, (pair + 1) * 128)


def centre(values):
    shifted = values - jnp.mean(values, -1, keepdims=True)
    spread = jnp.mean(shifted * shifted, -1, keepdims=True)
    scale = lax.rsqrt(spread + epsilon)
    return shifted * scale, scale


def norm_back(unit, scale, grad):
    return (grad - jnp.mean(grad, -1, keepdims=True) - unit * jnp.mean(grad * unit, -1, keepdims=True)) * scale


def call(kernel, name, outs, scratch, specs, out_specs=None, grid=None, prefetch=0, after=(), pin=(), hold=()):
    limit, cost = BUDGET[name]
    out_specs = out_specs or tuple(VMEM for _ in outs)
    first = prefetch + len(specs)

    def ordered(*refs):
        kernel(*refs[:first], *refs[first + len(after) :])

    spec = pltpu.PrefetchScalarGridSpec(
        num_scalar_prefetch=prefetch,
        grid=grid or (1,),
        in_specs=list(specs) + [pl.BlockSpec(memory_space=pl.ANY)] * len(after),
        out_specs=out_specs,
        scratch_shapes=scratch,
    )
    run = pl.pallas_call(
        ordered,
        out_shape=tuple(
            (pltpu.HBM if pinned else jax.ShapeDtypeStruct)(shape, kind)
            for (shape, kind), pinned in zip(outs, hold if hold else [spec is HBM for spec in out_specs])
        ),
        grid_spec=spec,
        compiler_params=pltpu.CompilerParams(vmem_limit_bytes=limit * MIB),
        cost_estimate=pl.CostEstimate(flops=int(cost * FLOPS_PER_US), bytes_accessed=1, transcendentals=0),
        name=name,
    )

    def place(*args):
        held = list(args)
        for i, spec in enumerate(specs):
            if spec is HBM or i in pin:
                held[prefetch + i] = pltpu.with_memory_space_constraint(held[prefetch + i], pltpu.HBM)
        return run(*held, *after)

    return place


def query_mask(code):
    kind = lax.broadcasted_iota(jnp.int32, (HEAD_DIM, code.shape[1]), 0).astype(F32)
    seen = (code == kind) | ((code == PAD_CLASS) & (kind == PAD_CLASS - 1)) | (kind > PAD_CLASS)
    return jnp.where(seen, 0.0, negative).astype(BF16)


def load_queries(qt_ref, code, qx, heads):
    mask = query_mask(code)
    for h in range(heads):
        own = slice(0, HEAD_DIM) if h % 2 == 0 else slice(HEAD_DIM, 128)
        rest = slice(HEAD_DIM, 128) if h % 2 == 0 else slice(0, HEAD_DIM)
        qx[h, own, :] = qt_ref[rows_of(h), :]
        qx[h, rest, :] = mask


def load_keys(k_ref, first, code, kx, heads):
    keys = k_ref.shape[0]
    kind = lax.broadcasted_iota(jnp.int32, (128, keys), 0).astype(F32)
    low = (kind == code).astype(F32).T.astype(BF16)
    high = (kind - HEAD_DIM == code).astype(F32).T.astype(BF16)
    lane = lax.broadcasted_iota(jnp.int32, (keys, 128), 1)
    for pair in range(heads // 2):
        slab = k_ref[:, first + pair * 128 : first + (pair + 1) * 128]
        kx[2 * pair] = jnp.where(lane < HEAD_DIM, slab, high)
        kx[2 * pair + 1] = jnp.where(lane < HEAD_DIM, low, slab)


def tile_ranges(code):
    image = jnp.minimum(code, float(PAD_CLASS - 1))
    cuts = [image[:, i : i + TILE] for i in range(0, code.shape[1], TILE)]
    return [(jnp.min(c), jnp.max(c)) for c in cuts]


def note_tiles(q_code, k_code, act):
    q_ranges, k_ranges = tile_ranges(q_code), tile_ranges(k_code)
    for i, (q_low, q_high) in enumerate(q_ranges):
        for j, (k_low, k_high) in enumerate(k_ranges):
            act[i, j] = ((q_low <= k_high) & (q_high >= k_low)).astype(jnp.int32)


def each_tile(act, queries, keys, body):
    for q_tile in range(queries // TILE):
        at = slice(q_tile * TILE, (q_tile + 1) * TILE)

        def step(k_tile, carry):
            @pl.when(act[q_tile, k_tile] > 0)
            def _():
                body(at, pl.ds(pl.multiple_of(k_tile * TILE, TILE), TILE))

            return carry

        lax.fori_loop(0, keys // TILE, step, 0)


def fold_keys(act, kx, qx, vt, top, total, acc, heads):
    def body(at, span):
        hs = range(heads)
        scores = [mm(kx[h, span, :], qx[h, :, at]) for h in hs]
        old = [top[h : h + 1, at] for h in hs]
        new = [jnp.maximum(old[h], jnp.max(scores[h], 0, keepdims=True)) for h in hs]
        decay = [jnp.exp(old[h] - new[h]) for h in hs]
        weights = [jnp.exp(scores[h] - new[h]) for h in hs]
        added = [mm(vt[rows_of(h), span], weights[h].astype(BF16)) for h in hs]
        for h in hs:
            top[h : h + 1, at] = new[h]
            total[h : h + 1, at] = decay[h] * total[h : h + 1, at] + jnp.sum(weights[h], 0, keepdims=True)
            acc[rows_of(h), at] = decay[h] * acc[rows_of(h), at] + added[h]

    each_tile(act, qx.shape[2], kx.shape[1], body)


def normed_rows(ref, at, gain, bias):
    return (centre(ref[at, :].astype(F32))[0] * gain + bias).astype(BF16)


def begin(sems, index, source, target):
    copy = pltpu.make_async_copy(source, target, sems.at[index])
    copy.start()
    return copy


def load_tokens(refs, code_ref):
    block = refs[0].shape[0] - 16
    for index, ref in enumerate(refs):
        row = ref[block : block + 16, :block].astype(F32)[:1]
        code_ref[:, index * block : (index + 1) * block] = jnp.broadcast_to(row, (8, block))
        for start in range(0, block, TILE):
            at = slice(index * block + start, index * block + start + TILE)
            yield at, ref[start : start + TILE, :]


def turn(array):
    return array.astype(F32).T.astype(BF16)


def near_kernel(
    core_ref,
    mine_ref,
    other_ref,
    gain_ref,
    bias_ref,
    bq_ref,
    bv_ref,
    weight_hbm,
    code_ref,
    top,
    total,
    normed_hbm,
    w_hbm,
    qt_hbm,
    kv_hbm,
    acc_hbm,
    act,
    kx,
    qx,
    vt,
    normed_v,
    w_v,
    qt_v,
    kv_v,
    acc,
    sems,
    *,
    heads,
):
    half = heads * HEAD_DIM
    first = pl.multiple_of(core_ref[0] * half, 128)
    loads = [
        begin(sems, i, weight_hbm.at[:, pl.ds(2 * i * half + first, half)], w_v.at[:, i * half : (i + 1) * half])
        for i in range(3)
    ]
    gain, bias = gain_ref[...].astype(F32), bias_ref[...].astype(F32)
    bq, bv = bq_ref[...].astype(F32), bv_ref[...].astype(F32)
    for at, tokens in load_tokens((mine_ref, other_ref), code_ref):
        normed = (centre(tokens.astype(F32))[0] * gain + bias).astype(BF16)
        normed_v[:, at] = turn(normed)
        for load in loads:
            load.wait()
        loads = []
        q = (mm(normed, w_v[:, :half]) + bq).astype(BF16).astype(F32) * attn_scale
        qt_v[:, at] = q.T.astype(BF16)
        kv_v[at, :half] = mm(normed, w_v[:, half : 2 * half]).astype(BF16)
        v = (mm(normed, w_v[:, 2 * half :]) + bv).astype(BF16)
        kv_v[at, half:] = v
        vt[:, at] = turn(v)
    pairs = ((normed_v, normed_hbm), (w_v, w_hbm), (qt_v, qt_hbm), (kv_v, kv_hbm))
    stores = [begin(sems, 3 + i, source, target) for i, (source, target) in enumerate(pairs)]
    code = code_ref[0:1, :]
    note_tiles(code, code, act)
    load_queries(qt_v, code, qx, heads)
    load_keys(kv_v, 0, code, kx, heads)
    top[...] = jnp.full_like(top, -1e29)
    total[...] = jnp.zeros_like(total)
    acc[...] = jnp.zeros_like(acc)
    fold_keys(act, kx, qx, vt, top, total, acc, heads)
    stores.append(begin(sems, 7, acc, acc_hbm))
    for store in stores:
        store.wait()


def forward_near(core, mine, other, gain, bias, qkv_weight, qv_bias):
    padded, width = mine.shape
    half = width // 2
    heads = half // HEAD_DIM
    rows = 2 * (padded - 16)
    specs = [VMEM] * 4 + [
        pl.BlockSpec((1, half), lambda i, c: (0, c[0])),
        pl.BlockSpec((1, half), lambda i, c: (0, 2 + c[0])),
        HBM,
    ]
    kept = (((width, rows), BF16), ((width, 3 * half), BF16), ((half, rows), BF16), ((rows, width), BF16))
    kept += (((half, rows), F32),)
    outs = (((8, rows), F32), ((8, rows), F32), ((8, rows), F32)) + kept
    scratch = [
        pltpu.SMEM((rows // TILE, rows // TILE), jnp.int32),
        pltpu.VMEM((heads, rows, 128), BF16),
        pltpu.VMEM((heads, 128, rows), BF16),
        pltpu.VMEM((half, rows), BF16),
    ]
    scratch += [pltpu.VMEM(shape, kind) for shape, kind in kept] + [pltpu.SemaphoreType.DMA((8,))]
    run = call(
        partial(near_kernel, heads=heads),
        "near_forward",
        outs,
        scratch,
        specs,
        (VMEM,) * 3 + (HBM,) * 5,
        prefetch=1,
        hold=(True,) * 8,
    )
    return run(core, mine, other, gain, bias, qv_bias, qv_bias, qkv_weight)


def far_kernel(
    far_ref,
    other_ref,
    gain_ref,
    bias_ref,
    bv_ref,
    code_ref,
    top_ref,
    total_ref,
    w_hbm,
    qt_hbm,
    acc_hbm,
    far_code_ref,
    o_ref,
    lse_ref,
    normed_hbm,
    kv_hbm,
    ot_hbm,
    act,
    kx,
    qx,
    vt,
    top,
    total,
    acc,
    w_v,
    qt_v,
    normed_v,
    kv_v,
    ot_v,
    sems,
    *,
    heads,
):
    half = heads * HEAD_DIM
    loads = [begin(sems, 0, w_hbm.at[:, half:], w_v), begin(sems, 1, qt_hbm, qt_v), begin(sems, 5, acc_hbm, acc)]
    gain, bias = gain_ref[...].astype(F32), bias_ref[...].astype(F32)
    bv = bv_ref[...].astype(F32)
    for at, tokens in load_tokens((far_ref, other_ref), far_code_ref):
        normed = (centre(tokens.astype(F32))[0] * gain + bias).astype(BF16)
        normed_v[:, at] = turn(normed)
        for load in loads:
            load.wait()
        loads = []
        kv_v[at, :half] = mm(normed, w_v[:, :half]).astype(BF16)
        v = (mm(normed, w_v[:, half:]) + bv).astype(BF16)
        kv_v[at, half:] = v
        vt[:, at] = turn(v)
    stores = [begin(sems, 2, normed_v, normed_hbm), begin(sems, 3, kv_v, kv_hbm)]
    code, far_code = code_ref[0:1, :], far_code_ref[0:1, :]
    note_tiles(code, far_code, act)
    load_queries(qt_v, code, qx, heads)
    load_keys(kv_v, 0, far_code, kx, heads)
    top[...] = top_ref[...]
    total[...] = total_ref[...]
    fold_keys(act, kx, qx, vt, top, total, acc, heads)
    lse_ref[...] = top[...] + jnp.log(jnp.maximum(total[...], 1e-30))
    for h in range(heads):
        acc[rows_of(h), :] = acc[rows_of(h), :] / total[h : h + 1, :]
    ot_v[...] = acc[...].astype(BF16)
    stores.append(begin(sems, 4, ot_v, ot_hbm))
    for pair in range(heads // 2):
        o_ref[:, lanes_of(pair)] = acc[lanes_of(pair), :].T.astype(BF16)
    for store in stores:
        store.wait()


def forward_far(far, other, gain, bias, w, qv_bias, qt, code, top, total, acc):
    padded, width = far.shape
    half = width // 2
    heads = half // HEAD_DIM
    rows = 2 * (padded - 16)
    specs = [VMEM] * 8 + [HBM] * 3
    kept = (((width, rows), BF16), ((rows, width), BF16), ((half, rows), BF16))
    outs = (((8, rows), F32), ((rows, half), BF16), ((8, rows), F32)) + kept
    scratch = [
        pltpu.SMEM((rows // TILE, rows // TILE), jnp.int32),
        pltpu.VMEM((heads, rows, 128), BF16),
        pltpu.VMEM((heads, 128, rows), BF16),
        pltpu.VMEM((half, rows), BF16),
        pltpu.VMEM((8, rows), F32),
        pltpu.VMEM((8, rows), F32),
        pltpu.VMEM((half, rows), F32),
        pltpu.VMEM((width, width), BF16),
        pltpu.VMEM((half, rows), BF16),
    ]
    scratch += [pltpu.VMEM(shape, kind) for shape, kind in kept] + [pltpu.SemaphoreType.DMA((6,))]
    run = call(partial(far_kernel, heads=heads), "far_forward", outs, scratch, specs, (VMEM,) * 3 + (HBM,) * 3, hold=(True, False, True) + (True,) * 3)
    return run(far, other, gain, bias, qv_bias, code, top, total, w, qt, acc)


def back_tiles(act, kx, qx, kt, dox, delta, qt_ref, kv_ref, do, lse, dq_sum, dk_sum, dv_sum, heads, group):
    half = heads * HEAD_DIM

    def body(at, span):
        for first in range(0, heads, group):
            hs = range(first, first + group)
            scores = {h: mm(kx[h, span, :], qx[h, :, at]) for h in hs}
            dp = {h: mm(kv_ref[span, half + (h // 2) * 128 : half + (h // 2 + 1) * 128], dox[h, :, at]) for h in hs}
            probs = {h: jnp.exp(scores[h] - lse(h, at)) for h in hs}
            rounded = {h: probs[h].astype(BF16) for h in hs}
            ds = {h: (probs[h] * (dp[h] - delta[h : h + 1, at])).astype(BF16) for h in hs}
            dv = {h: mm(do(h, at), rounded[h], NT) for h in hs}
            dk = {h: mm(qt_ref[rows_of(h), at], ds[h], NT) for h in hs}
            dq = {h: mm(kt[rows_of(h), span], ds[h]) for h in hs}
            for h in hs:
                dv_sum[rows_of(h), span] += dv[h]
                dk_sum[rows_of(h), span] += dk[h]
                dq_sum[rows_of(h), at] += dq[h]

    each_tile(act, qx.shape[2], kx.shape[1], body)


def back_ready(act, kx, qx, kt, dox, delta, qt_ref, kv_ref, ot_ref, do, q_code, k_code, heads):
    queries = qt_ref.shape[1]
    note_tiles(q_code, k_code, act)
    load_queries(qt_ref, q_code, qx, heads)
    load_keys(kv_ref, 0, k_code, kx, heads)
    zero = jnp.zeros((HEAD_DIM, queries), BF16)
    for h in range(heads):
        own = slice(0, HEAD_DIM) if h % 2 == 0 else slice(HEAD_DIM, 128)
        rest = slice(HEAD_DIM, 128) if h % 2 == 0 else slice(0, HEAD_DIM)
        grad = do(h, slice(0, queries))
        dox[h, own, :] = grad
        dox[h, rest, :] = zero
        delta[h : h + 1, :] = jnp.sum(grad.astype(F32) * ot_ref[rows_of(h), :].astype(F32), 0, keepdims=True)
    for pair in range(heads // 2):
        kt[lanes_of(pair), :] = turn(kv_ref[:, lanes_of(pair)])


def back_scratch(heads, queries, keys):
    half = heads * HEAD_DIM
    return [
        pltpu.SMEM((queries // TILE, keys // TILE), jnp.int32),
        pltpu.VMEM((heads, keys, 128), BF16),
        pltpu.VMEM((heads, 128, queries), BF16),
        pltpu.VMEM((half, keys), BF16),
        pltpu.VMEM((heads, 128, queries), BF16),
        pltpu.VMEM((8, queries), F32),
        pltpu.VMEM((half, queries), BF16),
        pltpu.VMEM((keys, 2 * half), BF16),
        pltpu.VMEM((half, queries), BF16),
        pltpu.VMEM((half, keys), F32),
        pltpu.VMEM((half, keys), F32),
    ]


def far_back_kernel(
    core_ref,
    flags_ref,
    q_code_ref,
    k_code_ref,
    lse_ref,
    part_ref,
    got_ref,
    gain_ref,
    early_ref,
    middle_hbm,
    cot_mine_hbm,
    cot_other_hbm,
    w_proj_hbm,
    qt_hbm,
    kv_hbm,
    ot_hbm,
    w_hbm,
    dx_ref,
    send_ref,
    sums_hbm,
    small_hbm,
    do_hbm,
    grad_half_hbm,
    grad_middle_hbm,
    dq_hbm,
    out_hbm,
    act,
    kx,
    qx,
    kt,
    dox,
    delta,
    qt_ref,
    kv_ref,
    ot_ref,
    dk_sum,
    dv_sum,
    w_ref,
    dq_sum,
    out_ref,
    middle_v,
    cot_v,
    w_proj_v,
    do_v,
    grad_half_v,
    grad_middle_v,
    sums_v,
    small_v,
    sems,
    *,
    heads,
    images,
):
    half = heads * HEAD_DIM
    rows = middle_v.shape[0]
    block = rows // 2
    pairs = (
        (middle_hbm, middle_v),
        (cot_mine_hbm, cot_v.at[:block, :]),
        (cot_other_hbm, cot_v.at[block:, :]),
        (w_proj_hbm.at[pl.ds(pl.multiple_of(core_ref[0] * half, 128), half), :], w_proj_v),
        (qt_hbm, qt_ref),
        (kv_hbm, kv_ref),
        (ot_hbm, ot_ref),
        (w_hbm.at[:, half:], w_ref),
    )
    loads = [begin(sems, i, source, target) for i, (source, target) in enumerate(pairs)]
    for load in loads[:4]:
        load.wait()
    gain = gain_ref[...].astype(F32)
    total = jnp.zeros((1, 2 * half), F32)
    for at, swapped in row_tiles(rows):
        keep_attn = keep_column(q_code_ref.at[:, at], flags_ref, 0, images)
        unit, scale = centre(middle_v[at, :])
        grad = (part_ref[at, :].astype(F32) + got_ref[swapped, :].astype(F32)) * gain
        grad_middle = cot_v[at, :].astype(F32) + norm_back(unit, scale, grad)
        grad_proj = (keep_attn * grad_middle).astype(BF16)
        grad_half_v[at, :] = jnp.where(core_ref[0] == 0, grad_proj[:, :half], grad_proj[:, half:])
        do_v[:, at] = mm(w_proj_v[...], grad_proj, NT).astype(BF16)
        if at.start < block:
            grad_middle_v[at, :] = grad_middle
            total = total + jnp.sum(grad_proj.astype(F32), 0, keepdims=True)
    small_v[...] = early_ref[...] + jnp.where(lane_of(small_v.shape) == 4, upright(total), 0.0)
    kept = ((do_v, do_hbm), (grad_half_v, grad_half_hbm), (grad_middle_v, grad_middle_hbm), (small_v, small_hbm))
    stores = [begin(sems, 8 + i, source, target) for i, (source, target) in enumerate(kept)]
    for load in loads[4:]:
        load.wait()

    def do(h, at):
        return do_v[rows_of(h), at]

    def lse(h, at):
        return lse_ref[h : h + 1, at]

    q_code, k_code = q_code_ref[0:1, :], k_code_ref[0:1, :]
    back_ready(act, kx, qx, kt, dox, delta, qt_ref, kv_ref, ot_ref, do, q_code, k_code, heads)
    dq_sum[...] = jnp.zeros_like(dq_sum)
    dk_sum[...] = jnp.zeros_like(dk_sum)
    dv_sum[...] = jnp.zeros_like(dv_sum)
    back_tiles(act, kx, qx, kt, dox, delta, qt_ref, kv_ref, do, lse, dq_sum, dk_sum, dv_sum, heads, 3)
    stores.append(begin(sems, 12, dq_sum, dq_hbm))
    out_ref[:half, :] = dk_sum[...].astype(BF16)
    out_ref[half:, :] = dv_sum[...].astype(BF16)
    stores.append(begin(sems, 13, out_ref, out_hbm))
    send_ref[...] = mm(w_ref[...], out_ref[:, block:]).astype(BF16)
    dx_ref[...] = mm(w_ref[...], out_ref[:, :block])
    sums_v[...] = jnp.broadcast_to(jnp.sum(out_ref[...].astype(F32), 1, keepdims=True), sums_v.shape)
    stores.append(begin(sems, 14, sums_v, sums_hbm))
    for store in stores:
        store.wait()


def far_back(after, core, flags, q_code, k_code, lse, part, got, gain, early, held):
    half, queries = held[4].shape
    keys = held[5].shape[0]
    heads = half // HEAD_DIM
    width = 2 * half
    kept = (
        ((half, queries), BF16),
        ((queries, half), BF16),
        ((queries // 2, width), F32),
    )
    column = ((width, 128), F32)
    dq, grad = ((half, queries), F32), ((width, keys), BF16)
    outs = (((width, keys // 2), F32), ((width, keys // 2), BF16), column, column) + kept + (dq, grad)
    scratch = back_scratch(heads, queries, keys) + [
        pltpu.VMEM((width, width), BF16),
        pltpu.VMEM(*dq),
        pltpu.VMEM(*grad),
        pltpu.VMEM((queries, width), F32),
        pltpu.VMEM((queries, width), BF16),
        pltpu.VMEM((half, width), BF16),
        *[pltpu.VMEM(*shape) for shape in kept],
        pltpu.VMEM(*column),
        pltpu.VMEM(*column),
        pltpu.SemaphoreType.DMA((15,)),
    ]
    specs = [SMEM] + [VMEM] * 7 + [HBM] * 8
    out_specs = (VMEM,) * 2 + (HBM,) * 7
    kernel = partial(far_back_kernel, heads=heads, images=flags.shape[1])
    run = call(kernel, "far_backward", outs, scratch, specs, out_specs, prefetch=1, after=after)
    return run(core, flags, q_code, k_code, lse, part, got, gain, early, *held)


def near_back_kernel(*refs, first, heads, unit, last):
    bits_ref, code_ref, lse_ref, do_ref, far_sums_ref, gain_ref, bias_ref, early_ref = refs[:8]
    if last:
        q_done_ref, v_done_ref, qt_hbm, kv_hbm, ot_hbm, dq_hbm, w_hbm, near_hbm, far_hbm, grad_hbm, done_hbm = refs[8:19]
        send_ref, send_part, keep_part, dx_hbm = refs[19:23]
        rest = refs[23:]
    else:
        qt_hbm, kv_hbm, ot_hbm, dq_hbm, w_hbm, near_hbm, far_hbm, grad_hbm, got_hbm, grad_half_hbm = refs[8:18]
        send_part, keep_part, small_ref, q_done_ref, v_done_ref, done_hbm = refs[18:24]
        rest = refs[24:]
    act, kx, qx, kt, dox, delta, qt_ref, kv_ref, ot_ref, dk_sum, dv_sum = rest[:11]
    dq_sum, out_ref, near_v, far_v, grad_v, w_ref, sems = rest[11:18]
    part = heads * HEAD_DIM
    half = do_ref.shape[0]
    low = first * HEAD_DIM
    mine = slice(low, low + part)
    block = kv_ref.shape[0] // 2
    pairs = [
        (qt_hbm.at[mine, :], qt_ref),
        (kv_hbm.at[:, mine], kv_ref.at[:, :part]),
        (kv_hbm.at[:, half + low : half + low + part], kv_ref.at[:, part:]),
    ]
    if last:
        done_v, dx_v, small_v = rest[18:]
        pairs += [(ot_hbm.at[mine, :], ot_ref), (dq_hbm.at[mine, :], dq_sum), (done_hbm, done_v)]
        other = part
        own_at = w_ref.shape[1] - 3 * part
        for i in range(3):
            pairs.append((w_hbm.at[:, i * half : i * half + low], w_ref.at[:, i * low : (i + 1) * low]))
    else:
        got_v, grad_half_v, whole_ot = rest[18:]
        pairs += [(ot_hbm, whole_ot), (dq_hbm.at[mine, :], dq_sum), (got_hbm, got_v), (grad_half_hbm, grad_half_v)]
        own_at = 0
        ot_ref = whole_ot
    for i in range(3):
        target = w_ref.at[:, own_at + i * part : own_at + (i + 1) * part]
        pairs.append((w_hbm.at[:, i * half + low : i * half + low + part], target))
    for i in range(2):
        pairs.append((grad_hbm.at[i * half + low : i * half + low + part, :], grad_v.at[i * part : (i + 1) * part, :]))
    pairs += [(near_hbm, near_v), (far_hbm, far_v)]
    loads = [begin(sems, i, source, target) for i, (source, target) in enumerate(pairs)]
    for load in loads[:5]:
        load.wait()

    def do(h, at):
        return do_ref[low + h * HEAD_DIM : low + (h + 1) * HEAD_DIM, at]

    def lse(h, at):
        return lse_ref[first + h : first + h + 1, at]

    code = code_ref[0:1, :]
    back_ready(act, kx, qx, kt, dox, delta, qt_ref, kv_ref, ot_ref, do, code, code, heads)
    dk_sum[...] = jnp.zeros_like(dk_sum)
    dv_sum[...] = jnp.zeros_like(dv_sum)
    back_tiles(act, kx, qx, kt, dox, delta, qt_ref, kv_ref, do, lse, dq_sum, dk_sum, dv_sum, heads, 2)
    out_ref[:part, :] = (dq_sum[...] * attn_scale).astype(BF16)
    out_ref[part : 2 * part, :] = dk_sum[...].astype(BF16)
    out_ref[2 * part :, :] = dv_sum[...].astype(BF16)
    for load in loads[5:]:
        load.wait()
    core = bits_ref[2]
    far_sums = [far_sums_ref[i * half + low : i * half + low + part, :] for i in range(2)]
    sums = jnp.broadcast_to(jnp.sum(out_ref[...].astype(F32), 1, keepdims=True), (3 * part, 128))
    sums = jnp.concatenate([sums[:part], sums[part : 2 * part] + far_sums[0], sums[2 * part :] + far_sums[1]], 0)
    q_column, v_column = sums[:part], sums[2 * part :]
    sums = sums.T[:1]
    if last:
        for start in (block, 0):
            both = mm(w_ref[:, :own_at], done_v[:, start : start + block])
            both = both + mm(w_ref[:, own_at:], out_ref[:, start : start + block])
            if start:
                send_ref[...] = both.astype(BF16)
            else:
                dx_v[...] = both
        stores = [begin(sems, len(pairs), dx_v, dx_hbm)]
        small_v[...] = early_ref[...]
        lane = lane_of((half // 2, 128))
        q_whole = jnp.concatenate([q_done_ref[...], q_column], 0)
        v_whole = jnp.concatenate([v_done_ref[...], v_column], 0)
        for base, column in ((0, q_whole), (half, v_whole)):
            rows = pl.ds(pl.multiple_of(base + core * (half // 2), 8), half // 2)
            for j, piece in enumerate(interleaved(column, unit, 2)):
                small_v[rows, :] += jnp.where(lane == 10 + j, piece, 0.0)
    else:
        stores = [begin(sems, len(pairs), out_ref, done_hbm)]
        q_done_ref[...] = q_column
        v_done_ref[...] = v_column
    gain, bias = gain_ref[...].astype(F32), bias_ref[...].astype(F32)
    for step in range(2 * half // ROW_STEP):
        at = slice(step * ROW_STEP, (step + 1) * ROW_STEP)
        out = mm(near_v[at, :], out_ref[...], NT)
        out = jnp.concatenate([out[:, :part], out[:, part:] + mm(far_v[at, :], grad_v[...], NT)], 1)
        columns = ln_columns(out, w_ref[at, own_at:].astype(F32), sums, gain[:, at], bias[:, at], 0)
        if last:
            deal_part(bits_ref[0], jnp.concatenate([out, small_v[at, :] + columns], 1), send_part, keep_part, step)
            continue
        small_ref[at, :] = early_ref[at, :] + columns

        def join(proj):
            deal_part(bits_ref[1], jnp.concatenate([out, proj], 1), send_part, keep_part, step)

        early, late = grad_half_v[:block, :], grad_half_v[block:, :]

        @pl.when(core == step)
        def _():
            join(mm(whole_ot[:, :block], early) + mm(whole_ot[:, block:], late))

        @pl.when(core != step)
        def _():
            join(mm(got_v[:block, :], late, TN) + mm(got_v[block:, :], early, TN))

    for store in stores:
        store.wait()


def near_back(after, unit, first, last, bits, small, held):
    code, lse, do, far_sums, gain, bias, early = small[:7]
    qt, kv, w = held[0], held[1], held[4]
    half, queries = qt.shape
    keys, width = kv.shape
    heads = half // HEAD_DIM - first if last else 4
    part = heads * HEAD_DIM
    grad = ((3 * part, keys), BF16)
    dx = ((width, keys // 2), F32)
    if last:
        outs = (((width, keys // 2), BF16), *dealt(width, 2 * unit, 3 * part + 128)[0], dx)
        hold = (False, False, False, True)
    else:
        column = ((part, 128), F32)
        outs = (*dealt(width, 4 * unit, 3 * part + half)[0], ((width, 128), F32), column, column, grad)
        hold = (False, False, True, True, True, True)
    scratch = back_scratch(heads, queries, keys) + [
        pltpu.VMEM((part, queries), F32),
        pltpu.VMEM(*grad),
        pltpu.VMEM((width, queries), BF16),
        pltpu.VMEM((width, queries), BF16),
        pltpu.VMEM((2 * part, keys), BF16),
        pltpu.VMEM((width, 3 * half if last else 3 * part), BF16),
        pltpu.SemaphoreType.DMA((17,)),
    ]
    if last:
        scratch += [pltpu.VMEM(held[-1].shape, BF16), pltpu.VMEM(*dx), pltpu.VMEM((width, 128), F32)]
    else:
        scratch += [pltpu.VMEM(held[-2].shape, BF16), pltpu.VMEM(held[-1].shape, BF16), pltpu.VMEM((half, queries), BF16)]
    specs = [VMEM] * len(small) + [HBM] * len(held)
    out_specs = (VMEM,) * (len(outs) - 1) + (HBM,)
    kernel = partial(near_back_kernel, first=first, heads=heads, unit=unit, last=last)
    name = "near_backward_last" if last else "near_backward_first"
    run = call(kernel, name, outs, scratch, specs, out_specs, prefetch=1, after=after, hold=hold)
    return run(bits, *small, *held)


def keep_column(code_ref, flags_ref, branch, images):
    code = jnp.minimum(code_ref[0:1, :], float(PAD_CLASS - 1))
    kept = jnp.zeros_like(code)
    for image in range(images):
        kept = kept + jnp.where(code == image, flags_ref[branch, image].astype(F32), 0.0)
    return jnp.broadcast_to(kept / keep_rate, (128, code.shape[1])).T[:, :1]


def gelu_both(hidden):
    size = jnp.abs(hidden)
    bell = jnp.exp(-0.5 * hidden * hidden)
    t = 1.0 / (1.0 + 0.23164189 * size)
    tail = ((((0.5307027145 * t - 0.7265760135) * t + 0.7107068705) * t - 0.142248368) * t + 0.127414796) * t * bell
    cdf = jnp.where(hidden >= 0, 1.0 - tail, tail)
    return hidden * cdf, cdf + hidden * (bell * 0.3989422804014327)


def row_tiles(rows):
    for start in range(0, rows, TILE):
        other = (start + rows // 2) % rows
        yield slice(start, start + TILE), slice(other, other + TILE)


def mlp_kernel(
    bits_ref,
    flags_ref,
    code_ref,
    own_ref,
    got_ref,
    b_proj_ref,
    gain_ref,
    bias_ref,
    b_up_ref,
    mine_hbm,
    other_hbm,
    cot_mine_hbm,
    cot_other_hbm,
    w_proj_hbm,
    w_up_hbm,
    w_down_hbm,
    part_ref,
    send_down,
    keep_down,
    send_up,
    keep_up,
    down_other_ref,
    small_ref,
    middle_hbm,
    down_hbm,
    x_v,
    cot_v,
    w_proj_v,
    w_up_v,
    w_down_v,
    middle_v,
    normed_v,
    grad_down_v,
    active_v,
    grad_hidden_v,
    down_v,
    up_sums_v,
    sems,
    *,
    images,
    unit,
):
    core = bits_ref[2]
    rows, width = x_v.shape
    block, half, units = rows // 2, width // 2, w_up_v.shape[1]
    mine_at, other_at = pl.multiple_of(core * half, 128), pl.multiple_of((1 - core) * half, 128)
    units_at = pl.multiple_of(core * units, 128)
    pairs = (
        (w_proj_hbm.at[pl.ds(mine_at, half), :], w_proj_v.at[:half, :]),
        (w_proj_hbm.at[pl.ds(other_at, half), :], w_proj_v.at[half:, :]),
        (mine_hbm, x_v.at[:block, :]),
        (other_hbm.at[:block, :], x_v.at[block:, :]),
        (cot_mine_hbm, cot_v.at[:block, :]),
        (cot_other_hbm, cot_v.at[block:, :]),
        (w_up_hbm.at[:, pl.ds(units_at, units)], w_up_v),
        (w_down_hbm.at[pl.ds(units_at, units), :], w_down_v),
    )
    loads = [begin(sems, i, source, target) for i, (source, target) in enumerate(pairs)]
    for load in loads[:6]:
        load.wait()
    gain, bias, b_proj = gain_ref[...].astype(F32), bias_ref[...].astype(F32), b_proj_ref[...].astype(F32)
    down_sums = jnp.zeros((1, width), F32)
    for at, swapped in row_tiles(rows):
        keep_attn = keep_column(code_ref.at[:, at], flags_ref, 0, images)
        keep_mlp = keep_column(code_ref.at[:, at], flags_ref, 1, images)
        branch = mm(own_ref[at, :], w_proj_v[:half, :]) + mm(got_ref[swapped, :], w_proj_v[half:, :]) + b_proj
        middle = x_v[at, :].astype(F32) + keep_attn * branch
        middle_v[at, :] = middle
        normed_v[at, :] = (centre(middle)[0] * gain + bias).astype(BF16)
        grad_down = (keep_mlp * cot_v[at, :].astype(F32)).astype(BF16)
        grad_down_v[at, :] = grad_down
        if at.start < block:
            down_sums = down_sums + jnp.sum(grad_down.astype(F32), 0, keepdims=True)
    stores = [begin(sems, 8, middle_v, middle_hbm)]
    for load in loads[6:]:
        load.wait()
    up_sums_v[...] = jnp.zeros_like(up_sums_v)
    chunk = 512

    def tile(index, carry):
        at = pl.ds(pl.multiple_of(index * TILE, TILE), TILE)
        for start in range(0, units, chunk):
            cols = slice(start, start + chunk)
            hidden = mm(normed_v[at, :], w_up_v[:, cols]) + b_up_ref[:, cols].astype(F32)
            active, slope = gelu_both(hidden)
            active_v[at, cols] = active.astype(BF16)
            grad_hidden = (mm(grad_down_v[at, :], w_down_v[cols, :], NT) * slope).astype(BF16)
            grad_hidden_v[at, cols] = grad_hidden
            up_sums_v[:, cols] += jnp.sum(grad_hidden.astype(F32), 0, keepdims=True)
        return carry

    lax.fori_loop(0, rows // TILE, tile, 0)
    for step in range(units // ROW_STEP):
        at = slice(step * ROW_STEP, (step + 1) * ROW_STEP)
        deal_part(bits_ref[0], mm(active_v[:, at], grad_down_v[...], TN), send_down, keep_down, step)
    for at, _ in row_tiles(rows):
        down = mm(active_v[at, :], w_down_v[...]).astype(BF16)
        if at.start < block:
            down_v[at, :] = down
        else:
            down_other_ref[at.start - block : at.stop - block, :] = down
    stores.append(begin(sems, 9, down_v, down_hbm))
    for step in range(width // ROW_STEP):
        at = slice(step * ROW_STEP, (step + 1) * ROW_STEP)
        out = mm(normed_v[:, at], grad_hidden_v[...], TN)
        deal_part(bits_ref[1], out, send_up, keep_up, step)
        columns = ln_columns(out, w_up_v[at, :].astype(F32), up_sums_v[...], gain[:, at], bias[:, at], 2)
        small_ref[at, :] = columns + jnp.where(lane_of(columns.shape) == 5, upright(down_sums[:, at]), 0.0)
    for at, _ in row_tiles(rows):
        part_ref[at, :] = mm(grad_hidden_v[at, :], w_up_v[...], NT).astype(BF16)
    lane = lane_of((half, 128))
    own = pl.ds(pl.multiple_of(core * half, 8), half)
    for j, column in enumerate(interleaved(upright(up_sums_v[...]), unit, units // half)):
        small_ref[own, :] += jnp.where(lane == 6 + j, column, 0.0)
    for store in stores:
        store.wait()


def mlp(unit, bits, flags, code, own, got, b_proj, gain, bias, b_up, mine, other, cot_mine, cot_other, w_proj, w_up, w_down):
    rows, half = own.shape
    width, units = 2 * half, w_up.shape[1] // 2
    specs = [SMEM] + [VMEM] * 6 + [pl.BlockSpec((1, units), lambda i, b: (0, b[2]))] + [HBM] * 7
    wide, tall = ((rows, width), BF16), ((rows, units), BF16)
    block = ((rows // 2, width), BF16)
    outs = (
        wide,
        *dealt(units, 2 * units // (width // unit // 2), width)[0],
        *dealt(width, 4 * unit, units)[0],
        block,
        ((width, 128), F32),
        ((rows, width), F32),
        block,
    )
    scratch = [
        pltpu.VMEM(*wide),
        pltpu.VMEM(*wide),
        pltpu.VMEM((width, width), BF16),
        pltpu.VMEM((width, units), BF16),
        pltpu.VMEM((units, width), BF16),
        pltpu.VMEM((rows, width), F32),
        pltpu.VMEM(*wide),
        pltpu.VMEM(*wide),
        pltpu.VMEM(*tall),
        pltpu.VMEM(*tall),
        pltpu.VMEM(*block),
        pltpu.VMEM((1, units), F32),
        pltpu.SemaphoreType.DMA((10,)),
    ]
    out_specs = (VMEM,) * 7 + (HBM,) * 2
    kernel = partial(mlp_kernel, images=flags.shape[1], unit=unit)
    run = call(kernel, "mlp", outs, scratch, specs, out_specs, prefetch=1)
    return run(
        bits, flags, code, own, got, b_proj, gain, bias, b_up, mine, other, cot_mine, cot_other, w_proj, w_up, w_down
    )


def deal(bit, rows, send_ref, keep_ref):
    run = send_ref.shape[1]
    for i in range(send_ref.shape[0]):
        low, high = rows[2 * i * run : (2 * i + 1) * run], rows[(2 * i + 1) * run : (2 * i + 2) * run]
        send_ref[i] = jnp.where(bit == 0, high, low).astype(BF16)
        keep_ref[i] = jnp.where(bit == 0, low, high).astype(BF16)


def deal_part(bit, rows, send_ref, keep_ref, step):
    count = rows.shape[0] // (2 * send_ref.shape[1])
    part = pl.ds(step * count, count)
    deal(bit, rows, send_ref.at[part], keep_ref.at[part])


def dealt(height, run, width):
    shape = (height // (2 * run), run, width)
    count = ROW_STEP // (2 * run)
    return [(shape, BF16)] * 2, [pl.BlockSpec((count, run, width), lambda i, *_: (i, 0, 0))] * 2


def upright(row):
    return jnp.broadcast_to(row, (128, row.shape[1])).T


def lane_of(shape):
    return lax.broadcasted_iota(jnp.int32, shape, 1)


def interleaved(column, unit, parts):
    blocks = column.shape[0] // (unit * parts)
    out = []
    for j in range(parts):
        pieces = [column[(k * parts + j) * unit : (k * parts + j + 1) * unit] for k in range(blocks)]
        out.append(jnp.concatenate(pieces, 0))
    return out


def ln_columns(grad, weight, sums, gain_ref, bias_ref, place):
    first = jnp.sum(weight * grad, 1, keepdims=True)
    second = jnp.sum(weight * sums, 1, keepdims=True)
    lane = lane_of((weight.shape[0], 128))
    scaled = (first - upright(bias_ref) * second) / upright(gain_ref)
    return jnp.where(lane == place, scaled, jnp.where(lane == place + 1, second, 0.0))


def add_kernel(left_ref, right_ref, out_ref):
    out_ref[...] = (left_ref[...].astype(F32) + right_ref[...].astype(F32)).astype(out_ref.dtype)


def add(after, left, right):
    run = call(add_kernel, "add_blocks", ((left.shape, BF16),), [], [VMEM, VMEM], after=after)
    return run(left, right)[0]


def sides(core_ref, kept, other):
    return jnp.where(core_ref[0] == 0, kept, other), jnp.where(core_ref[0] == 0, other, kept)


def join_up_kernel(core_ref, kept_ref, other_ref, out_ref):
    units = kept_ref.shape[1]
    out_ref[:, :units], out_ref[:, units:] = sides(core_ref, kept_ref[...], other_ref[...])


def join_up(after, core, kept, other):
    rows, units = kept.shape
    return call(join_up_kernel, "join_up", (((rows, 2 * units), F32),), [], [VMEM] * 2, prefetch=1, after=after)(
        core, kept, other
    )[0]


def join_kernel(core_ref, two_ref, two_other_ref, one_ref, one_other_ref, qkv_ref, proj_ref, *refs):
    rows, half = two_ref.shape[0], proj_ref.shape[1] // 2
    pad = refs[-1]
    big = (two_ref.shape[1] - half) // 3
    small = half - big
    twos = sides(core_ref, two_ref[...], two_other_ref[...])
    ones = sides(core_ref, one_ref[...], one_other_ref[...])
    for core, (two, one) in enumerate(zip(twos, ones)):
        proj_ref[:, core * half : (core + 1) * half] = two[:, 3 * big :]
        for i in range(3):
            at = 2 * i * half + core * half
            qkv_ref[:, at : at + big] = two[:, i * big : (i + 1) * big]
            qkv_ref[:, at + big : at + half] = one[:, i * small : (i + 1) * small]
    pad[...] = jnp.zeros_like(pad)
    pad[:rows, :] = one_ref[:, 3 * small :] + one_other_ref[:, 3 * small :]
    turned = pad[...].T
    lane = 0
    for ref in refs[:-1]:
        ref[...] = turned[lane : lane + ref.shape[0], :rows]
        lane += ref.shape[0]


def join_all(after, core, two, two_other, one, one_other, half):
    rows = two.shape[0]
    outs = [((rows, 6 * half), F32), ((rows, 2 * half), F32)] + [((count, rows), F32) for count in (1, 1, 1, 1, 1, 1, 4, 2)]
    scratch = [pltpu.VMEM((128, 128), F32)]
    run = call(join_kernel, "join_all", outs, scratch, [VMEM] * 4, prefetch=1, after=after)
    return run(core, two, two_other, one, one_other)


def finish_kernel(x_ref, dx_ref, beside_ref, across_ref, gain_ref, middle_ref, out_ref):
    unit, scale = centre(x_ref[...].astype(F32))
    grad = (dx_ref[...] + beside_ref[...].astype(F32) + across_ref[...].astype(F32)).T
    out_ref[...] = (middle_ref[...] + norm_back(unit, scale, grad * gain_ref[...].astype(F32))).astype(BF16)


def finish(after, x, dx, beside, across, gain, middle):
    rows, width = x.shape
    tile = pl.BlockSpec((TILE, width), lambda i: (i, 0))
    one = pl.BlockSpec((1, width), lambda i: (0, 0))
    turned = pl.BlockSpec((width, TILE), lambda i: (0, i))
    specs = [tile, turned, turned, turned, one, tile]
    run = call(finish_kernel, "token_gradient", ((x.shape, BF16),), [], specs, (tile,), (rows // TILE,), after=after)
    return run(x, dx, beside, across, gain, middle)[0]


def output_kernel(flags_ref, code_ref, middle_ref, down_ref, got_ref, bias_ref, out_ref, *, images):
    kept = keep_column(code_ref, flags_ref, 1, images)
    branch = down_ref[...].astype(F32) + got_ref[...].astype(F32) + bias_ref[...].astype(F32)
    out_ref[...] = (middle_ref[...] + kept * branch).astype(BF16)


def layer_out(after, flags, code, middle, down, got, bias):
    rows, width = got.shape
    tile = pl.BlockSpec((TILE, width), lambda i: (i, 0))
    one = pl.BlockSpec((1, width), lambda i: (0, 0))
    specs = [SMEM, pl.BlockSpec((8, TILE), lambda i: (0, i)), tile, tile, tile, one]
    kernel = partial(output_kernel, images=flags.shape[1])
    run = call(kernel, "layer_output", ((got.shape, BF16),), [], specs, (tile,), (rows // TILE,), after=after)
    return run(flags, code, middle, down, got, bias)[0]


def swap_halves(rows):
    half = rows.shape[0] // 2
    return jnp.concatenate([rows[half:], rows[:half]], 0)


def pick(array, index, dim):
    return lax.dynamic_index_in_dim(array, index, dim, keepdims=False)


class Links:
    def __init__(self, mesh):
        self.dp, self.blk = mesh.shape["dp"], mesh.shape["blk"]
        self.bits = self.dp.bit_length() - 1

    def core(self, value):
        return lax.ppermute(value, "blk", [(i, i ^ 1) for i in range(self.blk)])

    def side(self, value):
        return lax.ppermute(value, "blk", [(i, i ^ 2) for i in range(self.blk)])

    def cross(self, value, step):
        if step == "x":
            return self.side(value)
        return lax.ppermute(value, "dp", [(i, i ^ (1 << step)) for i in range(self.dp)])

    def bit(self, step):
        if step == "x":
            return lax.axis_index("blk") // 2
        return (lax.axis_index("dp") >> step) & 1

    def swap(self, value):
        top = self.dp // 2
        pairs = []
        for d in range(self.dp):
            for b in range(self.blk):
                high, core = d // top, b % 2
                pairs.append((d * self.blk + b, (d % top + core * top) * self.blk + (b - core + high)))
        return lax.ppermute(value, ("dp", "blk"), pairs)


class Portion:
    def __init__(self, links, send, keep, dims, order, by_core=True):
        self.links, self.order, self.by_core = links, list(order), by_core
        self.dims = [dim for dim in dims if dim != order[0]]
        self.tail = (send.shape[0] * send.shape[1] // 2 ** len(self.dims), send.shape[2])
        self.kept = keep
        self.arrived = links.cross(send, order[0])

    def advance(self, after):
        links = self.links
        self.order.pop(0)
        if not self.order:
            kept, arrived = self.kept.reshape(self.tail), self.arrived.reshape(self.tail)
            if not self.by_core:
                self.total = call(add_kernel, "sum_last", ((self.tail, F32),), [], [VMEM] * 2, after=after)(kept, arrived)[0]
                return self.total
            half = self.tail[0] // 2

            def last_kernel(core_ref, kept_ref, arrived_ref, send_ref, keep_ref):
                total = kept_ref[...].astype(F32) + arrived_ref[...].astype(F32)
                send_ref[...] = jnp.where(core_ref[0] == 0, total[half:], total[:half])
                keep_ref[...] = jnp.where(core_ref[0] == 0, total[:half], total[half:])

            shape = (half, self.tail[1])
            core = (lax.axis_index("blk") % 2).reshape(1).astype(jnp.int32)
            run = call(last_kernel, "sum_last", ((shape, F32), (shape, F32)), [], [VMEM] * 2, prefetch=1, after=after)
            send, self.total = run(core, kept, arrived)
            self.other = links.core(send)
            return self.total
        follow = self.order[0]
        spot = self.dims.index(follow)
        self.dims.pop(spot)
        outer, inner = 2**spot, 2 ** (len(self.dims) - spot)
        shape = (outer, inner) + self.tail
        view = (outer, 2, inner) + self.tail

        def kernel(bit_ref, kept_ref, arrived_ref, send_ref, keep_ref):
            for out_ref, where in ((send_ref, 1 - bit_ref[0]), (keep_ref, bit_ref[0])):
                out_ref[...] = (kept_ref[:, where].astype(F32) + arrived_ref[:, where].astype(F32)).astype(BF16)

        run = call(kernel, "sum_half", ((shape, BF16), (shape, BF16)), [], [VMEM] * 2, prefetch=1, after=after)
        send, keep = run(links.bit(follow).reshape(1).astype(jnp.int32), self.kept.reshape(view), self.arrived.reshape(view))
        self.kept = keep
        self.arrived = links.cross(send, follow)
        return keep


def local(
    links,
    tokens,
    cotangent,
    segments,
    padding,
    drop_keep,
    ln1_gain,
    ln1_bias,
    qkv_weight,
    qv_bias,
    proj_weight,
    proj_bias,
    ln2_gain,
    ln2_bias,
    fc1_weight,
    fc1_bias,
    fc2_weight,
    fc2_bias,
):
    _, block, width = tokens.shape
    half = width // 2
    units = fc1_weight.shape[1] // 2
    core = lax.axis_index("blk") % 2
    core_arg = core.reshape(1).astype(jnp.int32)
    owners = links.dp * links.blk
    rows = 2 * block

    code = jnp.where(padding == 1, segments, PAD_CLASS).astype(BF16)
    mine = jnp.concatenate([tokens[0], jnp.pad(code, ((0, 15), (0, width - block)))], 0)
    far = links.side(mine)
    other = links.core(mine)
    cot_mine = cotangent[0]
    cot_other = links.core(cot_mine)
    flags = drop_keep[:, 0, :]
    bits = links.bits
    low = [bits - 1 - i for i in range(bits)]
    chip = low + ["x"]
    by_core = low[1:] + ["x", low[0]]
    tail = [s for s in low if s > 1][::-1]
    side_bits = jnp.stack([links.bit("x"), links.bit(0), core, links.bit(1)]).astype(jnp.int32)
    unit = width // owners

    gain_one, bias_one = ln1_gain.reshape(1, -1), ln1_bias.reshape(1, -1)
    gain_two, bias_two = ln2_gain.reshape(1, -1), ln2_bias.reshape(1, -1)
    bias_qv = qv_bias.reshape(1, -1)
    near_code, top, total, near_normed, w_qkv, qt, near_kv, acc = forward_near(
        core_arg, mine, other, gain_one, bias_one, qkv_weight, bias_qv
    )
    far = lax.dynamic_update_slice(far, near_code[:, :128].astype(BF16), (block + 8, 0))
    far_other = links.core(far)
    bias_v = lax.dynamic_slice(bias_qv, (0, width + core * half), (1, half))
    far_code, own, lse, far_normed, far_kv, ot = forward_far(
        far, far_other, gain_one, bias_one, w_qkv, bias_v, qt, near_code, top, total, acc
    )
    got = links.core(own)
    part, send_down, keep_down, send_up, keep_up, down_send, small, middle, down = mlp(
        unit,
        side_bits,
        flags,
        near_code,
        own,
        got,
        proj_bias.reshape(1, -1),
        gain_two,
        bias_two,
        fc1_bias.reshape(1, -1),
        tokens[0],
        other,
        cot_mine,
        cot_other,
        proj_weight,
        fc1_weight,
        fc2_weight,
    )
    got_part = links.core(part)
    down_portion = Portion(links, send_down, keep_down, by_core, ["x", 0, 1] + tail, False)
    up_portion = Portion(links, send_up, keep_up, chip, [0, 1, "x"] + tail)
    down_other = links.core(down_send)
    held = (middle, cot_mine, cot_other, proj_weight, qt, far_kv, ot, w_qkv)
    far_dx, far_send, far_sums, small, do, grad_half, grad_middle, dq, far_grad = far_back(
        (), core_arg, flags, near_code, far_code, lse, part, got_part, gain_two, small, held
    )
    last = down_portion.advance((far_grad,))
    last = up_portion.advance((last,))
    far_sum = add((last,), far_dx, links.core(far_send))
    across = links.side(far_sum)
    ready = (near_code, lse, do, far_sums, gain_one, bias_one)
    held = (qt, near_kv, ot, dq, w_qkv, near_normed, far_normed, far_grad)
    send, keep, small, q_done, v_done, done = near_back(
        (far_sum,), unit, 0, False, side_bits, ready + (small,), held + (got, grad_half)
    )
    two_portion = Portion(links, send, keep, chip, [0, 1, "x"] + tail)
    last = down_portion.advance((keep,))
    last = up_portion.advance((last,))
    near_send, send, keep, near_dx = near_back(
        (last,), unit, 4, True, side_bits, ready + (small, q_done, v_done), held + (done,)
    )
    one_portion = Portion(links, send, keep, chip, ["x", 0, 1] + tail)
    last = down_portion.advance((keep,))
    last = up_portion.advance((last,))
    last = two_portion.advance((last,))
    layer_output = layer_out((last,), flags, near_code, middle, down, down_other, fc2_bias.reshape(1, -1))
    last = layer_output
    for _ in tail:
        last = one_portion.advance((last,))
        last = down_portion.advance((last,))
        last = up_portion.advance((last,))
        last = two_portion.advance((last,))
    down_grad = links.swap(down_portion.total)
    tokens_grad = finish((last,), tokens[0], near_dx, links.core(near_send), across, gain_one, grad_middle)
    last = one_portion.advance((tokens_grad,))
    last = two_portion.advance((last,))
    up_grad = join_up((last,), core_arg, up_portion.total, up_portion.other)
    last = one_portion.advance((up_grad,))
    while two_portion.order:
        last = two_portion.advance((last,))
    while one_portion.order:
        last = one_portion.advance((last,))
    qkv_grad, proj_grad, *vectors = join_all(
        (last,), core_arg, two_portion.total, two_portion.other, one_portion.total, one_portion.other, half
    )
    g1, b1, g2, b2, pb, d2, u1, qvb = (vector.reshape(-1) for vector in vectors)
    shape = tokens.shape
    return (
        layer_output.reshape(shape),
        tokens_grad.reshape(shape),
        g1,
        b1,
        qkv_grad,
        qvb,
        proj_grad,
        pb,
        g2,
        b2,
        up_grad,
        u1,
        down_grad,
        d2,
    )


def solution(mesh):
    both = P(("dp", "blk"))
    rows = P(("dp", "blk"), None)
    token = P("dp", "blk", None)
    placed = (token, token, P("dp", "blk"), P("dp", "blk"), P(None, "dp", None)) + (P(),) * 12
    return jax.shard_map(
        partial(local, Links(mesh)),
        mesh=mesh,
        in_specs=placed,
        out_specs=(token, token, both, both, rows, both, rows, both, both, both, rows, both, rows, both),
        check_vma=False,
    )
```

```python
from functools import partial

import jax
import jax.numpy as jnp
from jax import lax
from jax.experimental import pallas as pl
from jax.experimental.pallas import tpu as pltpu
from jax.sharding import PartitionSpec as P

HEAD_DIM = 64
F32 = jnp.float32
BF16 = jnp.bfloat16
epsilon = 1e-06
keep_rate = 0.9
attn_scale = 0.125
negative = -1e30
PAD_CLASS = 4
TILE = 256
MIB = 2**20
FLOPS_PER_US = 1.0 * 10**9
BUDGET = {
    "near_forward": (28, 16),
    "far_forward": (28, 13),
    "mlp": (44, 30),
    "far_backward": (42, 20),
    "near_backward_first": (36, 19),
    "near_backward_last": (36, 13),
    "join_up": (8, 1),
    "sum_both": (12, 2),
    "part_both": (8, 1),
    "join_all": (8, 1),
    "sum_half": (8, 2),
    "sum_last": (8, 1),
    "add_blocks": (8, 2),
    "token_gradient": (12, 2),
    "layer_output": (12, 2),
}
NN = ((1,), (0,))
NT = ((1,), (1,))
TN = ((0,), (0,))
VMEM = pl.BlockSpec(memory_space=pltpu.VMEM)
SMEM = pl.BlockSpec(memory_space=pltpu.SMEM)
HBM = pl.BlockSpec(memory_space=pltpu.HBM)
ROW_STEP = 384


def mm(left, right, dims=NN):
    return lax.dot_general(left, right, (dims, ((), ())), preferred_element_type=F32)


def rows_of(head):
    return slice(head * HEAD_DIM, (head + 1) * HEAD_DIM)


def lanes_of(pair):
    return slice(pair * 128, (pair + 1) * 128)


def centre(values):
    shifted = values - jnp.mean(values, -1, keepdims=True)
    spread = jnp.mean(shifted * shifted, -1, keepdims=True)
    scale = lax.rsqrt(spread + epsilon)
    return shifted * scale, scale


def norm_back(unit, scale, grad):
    return (grad - jnp.mean(grad, -1, keepdims=True) - unit * jnp.mean(grad * unit, -1, keepdims=True)) * scale


def call(kernel, name, outs, scratch, specs, out_specs=None, grid=None, prefetch=0, after=(), pin=(), hold=()):
    limit, cost = BUDGET[name]
    out_specs = out_specs or tuple(VMEM for _ in outs)
    first = prefetch + len(specs)

    def ordered(*refs):
        kernel(*refs[:first], *refs[first + len(after) :])

    spec = pltpu.PrefetchScalarGridSpec(
        num_scalar_prefetch=prefetch,
        grid=grid or (1,),
        in_specs=list(specs) + [pl.BlockSpec(memory_space=pl.ANY)] * len(after),
        out_specs=out_specs,
        scratch_shapes=scratch,
    )
    run = pl.pallas_call(
        ordered,
        out_shape=tuple(
            (pltpu.HBM if pinned else jax.ShapeDtypeStruct)(shape, kind)
            for (shape, kind), pinned in zip(outs, hold if hold else [spec is HBM for spec in out_specs])
        ),
        grid_spec=spec,
        compiler_params=pltpu.CompilerParams(vmem_limit_bytes=limit * MIB),
        cost_estimate=pl.CostEstimate(flops=int(cost * FLOPS_PER_US), bytes_accessed=1, transcendentals=0),
        name=name,
    )

    def place(*args):
        held = list(args)
        for i, spec in enumerate(specs):
            if spec is HBM or i in pin:
                held[prefetch + i] = pltpu.with_memory_space_constraint(held[prefetch + i], pltpu.HBM)
        return run(*held, *after)

    return place


def query_mask(code):
    kind = lax.broadcasted_iota(jnp.int32, (HEAD_DIM, code.shape[1]), 0).astype(F32)
    seen = (code == kind) | ((code == PAD_CLASS) & (kind == PAD_CLASS - 1)) | (kind > PAD_CLASS)
    return jnp.where(seen, 0.0, negative).astype(BF16)


def load_queries(qt_ref, code, qx, heads):
    mask = query_mask(code)
    for h in range(heads):
        own = slice(0, HEAD_DIM) if h % 2 == 0 else slice(HEAD_DIM, 128)
        rest = slice(HEAD_DIM, 128) if h % 2 == 0 else slice(0, HEAD_DIM)
        qx[h, own, :] = qt_ref[rows_of(h), :]
        qx[h, rest, :] = mask


def load_keys(k_ref, first, code, kx, heads):
    keys = k_ref.shape[0]
    kind = lax.broadcasted_iota(jnp.int32, (128, keys), 0).astype(F32)
    low = (kind == code).astype(F32).T.astype(BF16)
    high = (kind - HEAD_DIM == code).astype(F32).T.astype(BF16)
    lane = lax.broadcasted_iota(jnp.int32, (keys, 128), 1)
    for pair in range(heads // 2):
        slab = k_ref[:, first + pair * 128 : first + (pair + 1) * 128]
        kx[2 * pair] = jnp.where(lane < HEAD_DIM, slab, high)
        kx[2 * pair + 1] = jnp.where(lane < HEAD_DIM, low, slab)


def tile_ranges(code):
    image = jnp.minimum(code, float(PAD_CLASS - 1))
    cuts = [image[:, i : i + TILE] for i in range(0, code.shape[1], TILE)]
    return [(jnp.min(c), jnp.max(c)) for c in cuts]


def note_tiles(q_code, k_code, act):
    q_ranges, k_ranges = tile_ranges(q_code), tile_ranges(k_code)
    for i, (q_low, q_high) in enumerate(q_ranges):
        for j, (k_low, k_high) in enumerate(k_ranges):
            act[i, j] = ((q_low <= k_high) & (q_high >= k_low)).astype(jnp.int32)


def each_tile(act, queries, keys, body):
    for q_tile in range(queries // TILE):
        at = slice(q_tile * TILE, (q_tile + 1) * TILE)

        def step(k_tile, carry):
            @pl.when(act[q_tile, k_tile] > 0)
            def _():
                body(at, pl.ds(pl.multiple_of(k_tile * TILE, TILE), TILE))

            return carry

        lax.fori_loop(0, keys // TILE, step, 0)


def fold_keys(act, kx, qx, vt, top, total, acc, heads):
    def body(at, span):
        hs = range(heads)
        scores = [mm(kx[h, span, :], qx[h, :, at]) for h in hs]
        old = [top[h : h + 1, at] for h in hs]
        new = [jnp.maximum(old[h], jnp.max(scores[h], 0, keepdims=True)) for h in hs]
        decay = [jnp.exp(old[h] - new[h]) for h in hs]
        weights = [jnp.exp(scores[h] - new[h]) for h in hs]
        added = [mm(vt[rows_of(h), span], weights[h].astype(BF16)) for h in hs]
        for h in hs:
            top[h : h + 1, at] = new[h]
            total[h : h + 1, at] = decay[h] * total[h : h + 1, at] + jnp.sum(weights[h], 0, keepdims=True)
            acc[rows_of(h), at] = decay[h] * acc[rows_of(h), at] + added[h]

    each_tile(act, qx.shape[2], kx.shape[1], body)


def normed_rows(ref, at, gain, bias):
    return (centre(ref[at, :].astype(F32))[0] * gain + bias).astype(BF16)


def begin(sems, index, source, target):
    copy = pltpu.make_async_copy(source, target, sems.at[index])
    copy.start()
    return copy


def load_tokens(refs, code_ref):
    block = refs[0].shape[0] - 16
    for index, ref in enumerate(refs):
        row = ref[block : block + 16, :block].astype(F32)[:1]
        code_ref[:, index * block : (index + 1) * block] = jnp.broadcast_to(row, (8, block))
        for start in range(0, block, TILE):
            at = slice(index * block + start, index * block + start + TILE)
            yield at, ref[start : start + TILE, :]


def turn(array):
    return array.astype(F32).T.astype(BF16)


def near_kernel(
    core_ref,
    mine_ref,
    other_ref,
    gain_ref,
    bias_ref,
    bq_ref,
    bv_ref,
    weight_hbm,
    code_ref,
    normed_hbm,
    w_hbm,
    qt_hbm,
    kv_hbm,
    state_hbm,
    act,
    kx,
    qx,
    vt,
    normed_v,
    w_v,
    qt_v,
    kv_v,
    state,
    sems,
    *,
    heads,
):
    half = heads * HEAD_DIM
    acc, top, total = state.at[:half, :], state.at[half : half + 8, :], state.at[half + 8 :, :]
    first = pl.multiple_of(core_ref[0] * half, 128)
    loads = [
        begin(sems, i, weight_hbm.at[:, pl.ds(2 * i * half + first, half)], w_v.at[:, i * half : (i + 1) * half])
        for i in range(3)
    ]
    gain, bias = gain_ref[...].astype(F32), bias_ref[...].astype(F32)
    bq, bv = bq_ref[...].astype(F32), bv_ref[...].astype(F32)
    for at, tokens in load_tokens((mine_ref, other_ref), code_ref):
        normed = (centre(tokens.astype(F32))[0] * gain + bias).astype(BF16)
        normed_v[:, at] = turn(normed)
        for load in loads:
            load.wait()
        loads = []
        q = (mm(normed, w_v[:, :half]) + bq).astype(BF16).astype(F32) * attn_scale
        qt_v[:, at] = q.T.astype(BF16)
        kv_v[at, :half] = mm(normed, w_v[:, half : 2 * half]).astype(BF16)
        v = (mm(normed, w_v[:, 2 * half :]) + bv).astype(BF16)
        kv_v[at, half:] = v
        vt[:, at] = turn(v)
    pairs = ((normed_v, normed_hbm), (w_v, w_hbm), (qt_v, qt_hbm), (kv_v, kv_hbm))
    stores = [begin(sems, 3 + i, source, target) for i, (source, target) in enumerate(pairs)]
    code = code_ref[0:1, :]
    note_tiles(code, code, act)
    load_queries(qt_v, code, qx, heads)
    load_keys(kv_v, 0, code, kx, heads)
    top[...] = jnp.full_like(top, -1e29)
    total[...] = jnp.zeros_like(total)
    acc[...] = jnp.zeros_like(acc)
    fold_keys(act, kx, qx, vt, top, total, acc, heads)
    stores.append(begin(sems, 7, state, state_hbm))
    for store in stores:
        store.wait()


def forward_near(core, mine, other, gain, bias, qkv_weight, qv_bias):
    padded, width = mine.shape
    half = width // 2
    heads = half // HEAD_DIM
    rows = 2 * (padded - 16)
    specs = [VMEM] * 4 + [
        pl.BlockSpec((1, half), lambda i, c: (0, c[0])),
        pl.BlockSpec((1, half), lambda i, c: (0, 2 + c[0])),
        HBM,
    ]
    kept = (((width, rows), BF16), ((width, 3 * half), BF16), ((half, rows), BF16), ((rows, width), BF16))
    kept += (((half + 16, rows), F32),)
    outs = (((8, rows), F32),) + kept
    scratch = [
        pltpu.SMEM((rows // TILE, rows // TILE), jnp.int32),
        pltpu.VMEM((heads, rows, 128), BF16),
        pltpu.VMEM((heads, 128, rows), BF16),
        pltpu.VMEM((half, rows), BF16),
    ]
    scratch += [pltpu.VMEM(shape, kind) for shape, kind in kept] + [pltpu.SemaphoreType.DMA((8,))]
    run = call(
        partial(near_kernel, heads=heads),
        "near_forward",
        outs,
        scratch,
        specs,
        (VMEM,) + (HBM,) * 5,
        prefetch=1,
        hold=(True,) * 6,
    )
    return run(core, mine, other, gain, bias, qv_bias, qv_bias, qkv_weight)


def far_kernel(
    far_ref,
    other_ref,
    gain_ref,
    bias_ref,
    bv_ref,
    w_hbm,
    qt_hbm,
    state_hbm,
    code_hbm,
    far_code_ref,
    lse_ref,
    o_ref,
    normed_hbm,
    kv_hbm,
    ot_hbm,
    act,
    kx,
    qx,
    vt,
    state,
    code_ref,
    w_v,
    qt_v,
    normed_v,
    kv_v,
    ot_v,
    sems,
    *,
    heads,
):
    half = heads * HEAD_DIM
    acc, top, total = state.at[:half, :], state.at[half : half + 8, :], state.at[half + 8 :, :]
    pairs = ((w_hbm.at[:, half:], w_v), (qt_hbm, qt_v), (state_hbm, state), (code_hbm, code_ref))
    loads = [begin(sems, i, source, target) for i, (source, target) in enumerate(pairs)]
    gain, bias = gain_ref[...].astype(F32), bias_ref[...].astype(F32)
    bv = bv_ref[...].astype(F32)
    for at, tokens in load_tokens((far_ref, other_ref), far_code_ref):
        normed = (centre(tokens.astype(F32))[0] * gain + bias).astype(BF16)
        normed_v[:, at] = turn(normed)
        for load in loads:
            load.wait()
        loads = []
        kv_v[at, :half] = mm(normed, w_v[:, :half]).astype(BF16)
        v = (mm(normed, w_v[:, half:]) + bv).astype(BF16)
        kv_v[at, half:] = v
        vt[:, at] = turn(v)
    stores = [begin(sems, 4, normed_v, normed_hbm), begin(sems, 5, kv_v, kv_hbm)]
    code, far_code = code_ref[0:1, :], far_code_ref[0:1, :]
    note_tiles(code, far_code, act)
    load_queries(qt_v, code, qx, heads)
    load_keys(kv_v, 0, far_code, kx, heads)
    fold_keys(act, kx, qx, vt, top, total, acc, heads)
    lse_ref[...] = top[...] + jnp.log(jnp.maximum(total[...], 1e-30))
    for h in range(heads):
        acc[rows_of(h), :] = acc[rows_of(h), :] / total[h : h + 1, :]
    ot_v[...] = acc[...].astype(BF16)
    stores.append(begin(sems, 6, ot_v, ot_hbm))
    for pair in range(heads // 2):
        o_ref[:, lanes_of(pair)] = acc[lanes_of(pair), :].T.astype(BF16)
    for store in stores:
        store.wait()


def forward_far(far, other, gain, bias, w, qv_bias, qt, code, state):
    padded, width = far.shape
    half = width // 2
    heads = half // HEAD_DIM
    rows = 2 * (padded - 16)
    specs = [VMEM] * 5 + [HBM] * 4
    kept = (((width, rows), BF16), ((rows, width), BF16), ((half, rows), BF16))
    outs = (((8, rows), F32), ((8, rows), F32), ((rows, half), BF16)) + kept
    scratch = [
        pltpu.SMEM((rows // TILE, rows // TILE), jnp.int32),
        pltpu.VMEM((heads, rows, 128), BF16),
        pltpu.VMEM((heads, 128, rows), BF16),
        pltpu.VMEM((half, rows), BF16),
        pltpu.VMEM((half + 16, rows), F32),
        pltpu.VMEM((8, rows), F32),
        pltpu.VMEM((width, width), BF16),
        pltpu.VMEM((half, rows), BF16),
    ]
    scratch += [pltpu.VMEM(shape, kind) for shape, kind in kept] + [pltpu.SemaphoreType.DMA((7,))]
    run = call(partial(far_kernel, heads=heads), "far_forward", outs, scratch, specs, (VMEM,) * 3 + (HBM,) * 3, hold=(True,) * 6)
    return run(far, other, gain, bias, qv_bias, w, qt, state, code)


def back_tiles(act, kx, qx, kt, dox, delta, qt_ref, kv_ref, do, lse, dq_sum, dk_sum, dv_sum, heads, group):
    half = heads * HEAD_DIM

    def body(at, span):
        for first in range(0, heads, group):
            hs = range(first, first + group)
            scores = {h: mm(kx[h, span, :], qx[h, :, at]) for h in hs}
            dp = {h: mm(kv_ref[span, half + (h // 2) * 128 : half + (h // 2 + 1) * 128], dox[h, :, at]) for h in hs}
            probs = {h: jnp.exp(scores[h] - lse(h, at)) for h in hs}
            rounded = {h: probs[h].astype(BF16) for h in hs}
            ds = {h: (probs[h] * (dp[h] - delta[h : h + 1, at])).astype(BF16) for h in hs}
            dv = {h: mm(do(h, at), rounded[h], NT) for h in hs}
            dk = {h: mm(qt_ref[rows_of(h), at], ds[h], NT) for h in hs}
            dq = {h: mm(kt[rows_of(h), span], ds[h]) for h in hs}
            for h in hs:
                dv_sum[rows_of(h), span] += dv[h]
                dk_sum[rows_of(h), span] += dk[h]
                dq_sum[rows_of(h), at] += dq[h]

    each_tile(act, qx.shape[2], kx.shape[1], body)


def back_ready(act, kx, qx, kt, dox, delta, qt_ref, kv_ref, ot_ref, do, q_code, k_code, heads):
    queries = qt_ref.shape[1]
    note_tiles(q_code, k_code, act)
    load_queries(qt_ref, q_code, qx, heads)
    load_keys(kv_ref, 0, k_code, kx, heads)
    zero = jnp.zeros((HEAD_DIM, queries), BF16)
    for h in range(heads):
        own = slice(0, HEAD_DIM) if h % 2 == 0 else slice(HEAD_DIM, 128)
        rest = slice(HEAD_DIM, 128) if h % 2 == 0 else slice(0, HEAD_DIM)
        grad = do(h, slice(0, queries))
        dox[h, own, :] = grad
        dox[h, rest, :] = zero
        delta[h : h + 1, :] = jnp.sum(grad.astype(F32) * ot_ref[rows_of(h), :].astype(F32), 0, keepdims=True)
    for pair in range(heads // 2):
        kt[lanes_of(pair), :] = turn(kv_ref[:, lanes_of(pair)])


def back_scratch(heads, queries, keys):
    half = heads * HEAD_DIM
    return [
        pltpu.SMEM((queries // TILE, keys // TILE), jnp.int32),
        pltpu.VMEM((heads, keys, 128), BF16),
        pltpu.VMEM((heads, 128, queries), BF16),
        pltpu.VMEM((half, keys), BF16),
        pltpu.VMEM((heads, 128, queries), BF16),
        pltpu.VMEM((8, queries), F32),
        pltpu.VMEM((half, queries), BF16),
        pltpu.VMEM((keys, 2 * half), BF16),
        pltpu.VMEM((half, queries), BF16),
        pltpu.VMEM((half, keys), F32),
        pltpu.VMEM((half, keys), F32),
    ]


def far_back_kernel(
    core_ref,
    flags_ref,
    gain_ref,
    q_code_hbm,
    k_code_hbm,
    lse_hbm,
    part_hbm,
    got_hbm,
    early_hbm,
    middle_hbm,
    cot_mine_hbm,
    cot_other_hbm,
    w_proj_hbm,
    qt_hbm,
    kv_hbm,
    ot_hbm,
    w_hbm,
    dx_ref,
    send_ref,
    sums_hbm,
    small_hbm,
    do_hbm,
    grad_half_hbm,
    grad_middle_hbm,
    dq_hbm,
    out_hbm,
    act,
    kx,
    qx,
    kt,
    dox,
    delta,
    qt_ref,
    kv_ref,
    ot_ref,
    dk_sum,
    dv_sum,
    w_ref,
    dq_sum,
    out_ref,
    middle_v,
    cot_v,
    w_proj_v,
    do_v,
    grad_half_v,
    grad_middle_v,
    sums_v,
    small_v,
    q_code_ref,
    k_code_ref,
    lse_ref,
    part_ref,
    got_ref,
    early_ref,
    sems,
    *,
    heads,
    images,
):
    half = heads * HEAD_DIM
    rows = middle_v.shape[0]
    block = rows // 2
    pairs = (
        (middle_hbm, middle_v),
        (part_hbm, part_ref),
        (got_hbm, got_ref),
        (cot_mine_hbm, cot_v.at[:block, :]),
        (cot_other_hbm, cot_v.at[block:, :]),
        (early_hbm, early_ref),
        (q_code_hbm, q_code_ref),
        (w_proj_hbm.at[pl.ds(pl.multiple_of(core_ref[0] * half, 128), half), :], w_proj_v),
        (qt_hbm, qt_ref),
        (kv_hbm, kv_ref),
        (ot_hbm, ot_ref),
        (k_code_hbm, k_code_ref),
        (lse_hbm, lse_ref),
        (w_hbm.at[:, half:], w_ref),
    )
    loads = [begin(sems, i, source, target) for i, (source, target) in enumerate(pairs)]
    for load in loads[:8]:
        load.wait()
    gain = gain_ref[...].astype(F32)
    total = jnp.zeros((1, 2 * half), F32)
    for at, swapped in row_tiles(rows):
        keep_attn = keep_column(q_code_ref.at[:, at], flags_ref, 0, images)
        unit, scale = centre(middle_v[at, :])
        grad = (part_ref[at, :].astype(F32) + got_ref[swapped, :].astype(F32)) * gain
        grad_middle = cot_v[at, :].astype(F32) + norm_back(unit, scale, grad)
        grad_proj = (keep_attn * grad_middle).astype(BF16)
        grad_half_v[at, :] = jnp.where(core_ref[0] == 0, grad_proj[:, :half], grad_proj[:, half:])
        do_v[:, at] = mm(w_proj_v[...], grad_proj, NT).astype(BF16)
        if at.start < block:
            grad_middle_v[at, :] = grad_middle
            total = total + jnp.sum(grad_proj.astype(F32), 0, keepdims=True)
    small_v[...] = early_ref[...] + jnp.where(lane_of(small_v.shape) == 4, upright(total), 0.0)
    kept = ((do_v, do_hbm), (grad_half_v, grad_half_hbm), (grad_middle_v, grad_middle_hbm), (small_v, small_hbm))
    stores = [begin(sems, 14 + i, source, target) for i, (source, target) in enumerate(kept)]
    for load in loads[8:]:
        load.wait()

    def do(h, at):
        return do_v[rows_of(h), at]

    def lse(h, at):
        return lse_ref[h : h + 1, at]

    q_code, k_code = q_code_ref[0:1, :], k_code_ref[0:1, :]
    back_ready(act, kx, qx, kt, dox, delta, qt_ref, kv_ref, ot_ref, do, q_code, k_code, heads)
    dq_sum[...] = jnp.zeros_like(dq_sum)
    dk_sum[...] = jnp.zeros_like(dk_sum)
    dv_sum[...] = jnp.zeros_like(dv_sum)
    back_tiles(act, kx, qx, kt, dox, delta, qt_ref, kv_ref, do, lse, dq_sum, dk_sum, dv_sum, heads, 3)
    stores.append(begin(sems, 18, dq_sum, dq_hbm))
    out_ref[:half, :] = dk_sum[...].astype(BF16)
    out_ref[half:, :] = dv_sum[...].astype(BF16)
    stores.append(begin(sems, 19, out_ref, out_hbm))
    send_ref[...] = mm(w_ref[...], out_ref[:, block:]).astype(BF16)
    dx_ref[...] = mm(w_ref[...], out_ref[:, :block])
    sums_v[...] = jnp.broadcast_to(jnp.sum(out_ref[...].astype(F32), 1, keepdims=True), sums_v.shape)
    stores.append(begin(sems, 20, sums_v, sums_hbm))
    for store in stores:
        store.wait()


def far_back(after, core, flags, q_code, k_code, lse, part, got, gain, early, held):
    half, queries = held[4].shape
    keys = held[5].shape[0]
    heads = half // HEAD_DIM
    width = 2 * half
    kept = (
        ((half, queries), BF16),
        ((queries, half), BF16),
        ((queries // 2, width), F32),
    )
    column = ((width, 128), F32)
    dq, grad = ((half, queries), F32), ((width, keys), BF16)
    outs = (((width, keys // 2), F32), ((width, keys // 2), BF16), column, column) + kept + (dq, grad)
    scratch = back_scratch(heads, queries, keys) + [
        pltpu.VMEM((width, width), BF16),
        pltpu.VMEM(*dq),
        pltpu.VMEM(*grad),
        pltpu.VMEM((queries, width), F32),
        pltpu.VMEM((queries, width), BF16),
        pltpu.VMEM((half, width), BF16),
        *[pltpu.VMEM(*shape) for shape in kept],
        pltpu.VMEM(*column),
        pltpu.VMEM(*column),
        *[pltpu.VMEM(array.shape, array.dtype) for array in (q_code, k_code, lse, part, got, early)],
        pltpu.SemaphoreType.DMA((21,)),
    ]
    specs = [SMEM, VMEM] + [HBM] * 14
    out_specs = (VMEM,) * 2 + (HBM,) * 7
    kernel = partial(far_back_kernel, heads=heads, images=flags.shape[1])
    run = call(kernel, "far_backward", outs, scratch, specs, out_specs, prefetch=1, after=after)
    return run(core, flags, gain, q_code, k_code, lse, part, got, early, *held)


def near_back_kernel(*refs, first, heads, unit, last):
    bits_ref, code_ref, lse_ref, do_ref, far_sums_ref, gain_ref, bias_ref, early_ref = refs[:8]
    if last:
        q_done_ref, v_done_ref, qt_hbm, kv_hbm, ot_hbm, dq_hbm, w_hbm, near_hbm, far_hbm, grad_hbm, done_hbm = refs[8:19]
        send_ref, send_part, keep_part, dx_hbm = refs[19:23]
        rest = refs[23:]
    else:
        qt_hbm, kv_hbm, ot_hbm, dq_hbm, w_hbm, near_hbm, far_hbm, grad_hbm, got_hbm, grad_half_hbm = refs[8:18]
        send_part, keep_part, small_ref, q_done_ref, v_done_ref, done_hbm = refs[18:24]
        rest = refs[24:]
    act, kx, qx, kt, dox, delta, qt_ref, kv_ref, ot_ref, dk_sum, dv_sum = rest[:11]
    dq_sum, out_ref, near_v, far_v, grad_v, w_ref, sems = rest[11:18]
    part = heads * HEAD_DIM
    half = do_ref.shape[0]
    low = first * HEAD_DIM
    mine = slice(low, low + part)
    block = kv_ref.shape[0] // 2
    pairs = [
        (qt_hbm.at[mine, :], qt_ref),
        (kv_hbm.at[:, mine], kv_ref.at[:, :part]),
        (kv_hbm.at[:, half + low : half + low + part], kv_ref.at[:, part:]),
    ]
    if last:
        done_v, dx_v, small_v = rest[18:]
        pairs += [(ot_hbm.at[mine, :], ot_ref), (dq_hbm.at[mine, :], dq_sum), (done_hbm, done_v)]
        other = part
        own_at = w_ref.shape[1] - 3 * part
        for i in range(3):
            pairs.append((w_hbm.at[:, i * half : i * half + low], w_ref.at[:, i * low : (i + 1) * low]))
    else:
        got_v, grad_half_v, whole_ot = rest[18:]
        pairs += [(ot_hbm, whole_ot), (dq_hbm.at[mine, :], dq_sum), (got_hbm, got_v), (grad_half_hbm, grad_half_v)]
        own_at = 0
        ot_ref = whole_ot
    for i in range(3):
        target = w_ref.at[:, own_at + i * part : own_at + (i + 1) * part]
        pairs.append((w_hbm.at[:, i * half + low : i * half + low + part], target))
    for i in range(2):
        pairs.append((grad_hbm.at[i * half + low : i * half + low + part, :], grad_v.at[i * part : (i + 1) * part, :]))
    pairs += [(near_hbm, near_v), (far_hbm, far_v)]
    loads = [begin(sems, i, source, target) for i, (source, target) in enumerate(pairs)]
    for load in loads[:5]:
        load.wait()

    def do(h, at):
        return do_ref[low + h * HEAD_DIM : low + (h + 1) * HEAD_DIM, at]

    def lse(h, at):
        return lse_ref[first + h : first + h + 1, at]

    code = code_ref[0:1, :]
    back_ready(act, kx, qx, kt, dox, delta, qt_ref, kv_ref, ot_ref, do, code, code, heads)
    dk_sum[...] = jnp.zeros_like(dk_sum)
    dv_sum[...] = jnp.zeros_like(dv_sum)
    back_tiles(act, kx, qx, kt, dox, delta, qt_ref, kv_ref, do, lse, dq_sum, dk_sum, dv_sum, heads, 2)
    out_ref[:part, :] = (dq_sum[...] * attn_scale).astype(BF16)
    out_ref[part : 2 * part, :] = dk_sum[...].astype(BF16)
    out_ref[2 * part :, :] = dv_sum[...].astype(BF16)
    for load in loads[5:]:
        load.wait()
    core = bits_ref[2]
    far_sums = [far_sums_ref[i * half + low : i * half + low + part, :] for i in range(2)]
    sums = jnp.broadcast_to(jnp.sum(out_ref[...].astype(F32), 1, keepdims=True), (3 * part, 128))
    sums = jnp.concatenate([sums[:part], sums[part : 2 * part] + far_sums[0], sums[2 * part :] + far_sums[1]], 0)
    q_column, v_column = sums[:part], sums[2 * part :]
    sums = sums.T[:1]
    if last:
        for start in (block, 0):
            both = mm(w_ref[:, :own_at], done_v[:, start : start + block])
            both = both + mm(w_ref[:, own_at:], out_ref[:, start : start + block])
            if start:
                send_ref[...] = both.astype(BF16)
            else:
                dx_v[...] = both
        stores = [begin(sems, len(pairs), dx_v, dx_hbm)]
        small_v[...] = early_ref[...]
        lane = lane_of((half // 2, 128))
        q_whole = jnp.concatenate([q_done_ref[...], q_column], 0)
        v_whole = jnp.concatenate([v_done_ref[...], v_column], 0)
        for base, column in ((0, q_whole), (half, v_whole)):
            rows = pl.ds(pl.multiple_of(base + core * (half // 2), 8), half // 2)
            for j, piece in enumerate(interleaved(column, unit, 2)):
                small_v[rows, :] += jnp.where(lane == 10 + j, piece, 0.0)
    else:
        stores = [begin(sems, len(pairs), out_ref, done_hbm)]
        q_done_ref[...] = q_column
        v_done_ref[...] = v_column
    gain, bias = gain_ref[...].astype(F32), bias_ref[...].astype(F32)
    for step in range(2 * half // ROW_STEP):
        at = slice(step * ROW_STEP, (step + 1) * ROW_STEP)
        out = mm(near_v[at, :], out_ref[...], NT)
        out = jnp.concatenate([out[:, :part], out[:, part:] + mm(far_v[at, :], grad_v[...], NT)], 1)
        columns = ln_columns(out, w_ref[at, own_at:].astype(F32), sums, gain[:, at], bias[:, at], 0)
        if last:
            deal_part(bits_ref[0], jnp.concatenate([out, small_v[at, :] + columns], 1), send_part, keep_part, step)
            continue
        small_ref[at, :] = early_ref[at, :] + columns

        def join(proj):
            deal_part(bits_ref[1], jnp.concatenate([out, proj], 1), send_part, keep_part, step)

        early, late = grad_half_v[:block, :], grad_half_v[block:, :]

        @pl.when(core == step)
        def _():
            join(mm(whole_ot[:, :block], early) + mm(whole_ot[:, block:], late))

        @pl.when(core != step)
        def _():
            join(mm(got_v[:block, :], late, TN) + mm(got_v[block:, :], early, TN))

    for store in stores:
        store.wait()


def near_back(after, unit, first, last, bits, small, held):
    code, lse, do, far_sums, gain, bias, early = small[:7]
    qt, kv, w = held[0], held[1], held[4]
    half, queries = qt.shape
    keys, width = kv.shape
    heads = half // HEAD_DIM - first if last else 4
    part = heads * HEAD_DIM
    grad = ((3 * part, keys), BF16)
    dx = ((width, keys // 2), F32)
    if last:
        outs = (((width, keys // 2), BF16), *dealt(width, 2 * unit, 3 * part + 128)[0], dx)
        hold = (False, False, False, True)
    else:
        column = ((part, 128), F32)
        outs = (*dealt(width, 4 * unit, 3 * part + half)[0], ((width, 128), F32), column, column, grad)
        hold = (False, False, True, True, True, True)
    scratch = back_scratch(heads, queries, keys) + [
        pltpu.VMEM((part, queries), F32),
        pltpu.VMEM(*grad),
        pltpu.VMEM((width, queries), BF16),
        pltpu.VMEM((width, queries), BF16),
        pltpu.VMEM((2 * part, keys), BF16),
        pltpu.VMEM((width, 3 * half if last else 3 * part), BF16),
        pltpu.SemaphoreType.DMA((17,)),
    ]
    if last:
        scratch += [pltpu.VMEM(held[-1].shape, BF16), pltpu.VMEM(*dx), pltpu.VMEM((width, 128), F32)]
    else:
        scratch += [pltpu.VMEM(held[-2].shape, BF16), pltpu.VMEM(held[-1].shape, BF16), pltpu.VMEM((half, queries), BF16)]
    specs = [VMEM] * len(small) + [HBM] * len(held)
    out_specs = (VMEM,) * (len(outs) - 1) + (HBM,)
    kernel = partial(near_back_kernel, first=first, heads=heads, unit=unit, last=last)
    name = "near_backward_last" if last else "near_backward_first"
    run = call(kernel, name, outs, scratch, specs, out_specs, prefetch=1, after=after, hold=hold)
    return run(bits, *small, *held)


def keep_column(code_ref, flags_ref, branch, images):
    code = jnp.minimum(code_ref[0:1, :], float(PAD_CLASS - 1))
    kept = jnp.zeros_like(code)
    for image in range(images):
        kept = kept + jnp.where(code == image, flags_ref[branch, image].astype(F32), 0.0)
    return jnp.broadcast_to(kept / keep_rate, (128, code.shape[1])).T[:, :1]


def gelu_both(hidden):
    size = jnp.abs(hidden)
    bell = jnp.exp(-0.5 * hidden * hidden)
    t = 1.0 / (1.0 + 0.23164189 * size)
    tail = ((((0.5307027145 * t - 0.7265760135) * t + 0.7107068705) * t - 0.142248368) * t + 0.127414796) * t * bell
    cdf = jnp.where(hidden >= 0, 1.0 - tail, tail)
    return hidden * cdf, cdf + hidden * (bell * 0.3989422804014327)


def row_tiles(rows):
    for start in range(0, rows, TILE):
        other = (start + rows // 2) % rows
        yield slice(start, start + TILE), slice(other, other + TILE)


def mlp_kernel(
    bits_ref,
    flags_ref,
    b_proj_ref,
    gain_ref,
    bias_ref,
    b_up_ref,
    code_hbm,
    own_hbm,
    got_hbm,
    mine_hbm,
    other_hbm,
    cot_mine_hbm,
    cot_other_hbm,
    w_proj_hbm,
    w_up_hbm,
    w_down_hbm,
    part_ref,
    send_down,
    keep_down,
    send_up,
    keep_up,
    down_other_ref,
    small_ref,
    middle_hbm,
    down_hbm,
    x_v,
    cot_v,
    w_proj_v,
    w_up_v,
    w_down_v,
    middle_v,
    normed_v,
    grad_down_v,
    active_v,
    grad_hidden_v,
    down_v,
    up_sums_v,
    code_ref,
    own_ref,
    got_ref,
    sems,
    *,
    images,
    unit,
):
    core = bits_ref[2]
    rows, width = x_v.shape
    block, half, units = rows // 2, width // 2, w_up_v.shape[1]
    mine_at, other_at = pl.multiple_of(core * half, 128), pl.multiple_of((1 - core) * half, 128)
    units_at = pl.multiple_of(core * units, 128)
    pairs = (
        (w_proj_hbm.at[pl.ds(mine_at, half), :], w_proj_v.at[:half, :]),
        (w_proj_hbm.at[pl.ds(other_at, half), :], w_proj_v.at[half:, :]),
        (mine_hbm, x_v.at[:block, :]),
        (other_hbm.at[:block, :], x_v.at[block:, :]),
        (cot_mine_hbm, cot_v.at[:block, :]),
        (cot_other_hbm, cot_v.at[block:, :]),
        (code_hbm, code_ref),
        (own_hbm, own_ref),
        (got_hbm, got_ref),
        (w_up_hbm.at[:, pl.ds(units_at, units)], w_up_v),
        (w_down_hbm.at[pl.ds(units_at, units), :], w_down_v),
    )
    loads = [begin(sems, i, source, target) for i, (source, target) in enumerate(pairs)]
    for load in loads[:9]:
        load.wait()
    gain, bias, b_proj = gain_ref[...].astype(F32), bias_ref[...].astype(F32), b_proj_ref[...].astype(F32)
    down_sums = jnp.zeros((1, width), F32)
    for at, swapped in row_tiles(rows):
        keep_attn = keep_column(code_ref.at[:, at], flags_ref, 0, images)
        keep_mlp = keep_column(code_ref.at[:, at], flags_ref, 1, images)
        branch = mm(own_ref[at, :], w_proj_v[:half, :]) + mm(got_ref[swapped, :], w_proj_v[half:, :]) + b_proj
        middle = x_v[at, :].astype(F32) + keep_attn * branch
        middle_v[at, :] = middle
        normed_v[at, :] = (centre(middle)[0] * gain + bias).astype(BF16)
        grad_down = (keep_mlp * cot_v[at, :].astype(F32)).astype(BF16)
        grad_down_v[at, :] = grad_down
        if at.start < block:
            down_sums = down_sums + jnp.sum(grad_down.astype(F32), 0, keepdims=True)
    stores = [begin(sems, 11, middle_v, middle_hbm)]
    for load in loads[9:]:
        load.wait()
    up_sums_v[...] = jnp.zeros_like(up_sums_v)
    chunk = 512

    def tile(index, carry):
        at = pl.ds(pl.multiple_of(index * TILE, TILE), TILE)
        for start in range(0, units, chunk):
            cols = slice(start, start + chunk)
            hidden = mm(normed_v[at, :], w_up_v[:, cols]) + b_up_ref[:, cols].astype(F32)
            active, slope = gelu_both(hidden)
            active_v[at, cols] = active.astype(BF16)
            grad_hidden = (mm(grad_down_v[at, :], w_down_v[cols, :], NT) * slope).astype(BF16)
            grad_hidden_v[at, cols] = grad_hidden
            up_sums_v[:, cols] += jnp.sum(grad_hidden.astype(F32), 0, keepdims=True)
        return carry

    lax.fori_loop(0, rows // TILE, tile, 0)
    for step in range(units // ROW_STEP):
        at = slice(step * ROW_STEP, (step + 1) * ROW_STEP)
        deal_part(bits_ref[0], mm(active_v[:, at], grad_down_v[...], TN), send_down, keep_down, step)
    for at, _ in row_tiles(rows):
        down = mm(active_v[at, :], w_down_v[...]).astype(BF16)
        if at.start < block:
            down_v[at, :] = down
        else:
            down_other_ref[at.start - block : at.stop - block, :] = down
    stores.append(begin(sems, 12, down_v, down_hbm))
    for step in range(width // ROW_STEP):
        at = slice(step * ROW_STEP, (step + 1) * ROW_STEP)
        out = mm(normed_v[:, at], grad_hidden_v[...], TN)
        deal_part(bits_ref[1], out, send_up, keep_up, step)
        columns = ln_columns(out, w_up_v[at, :].astype(F32), up_sums_v[...], gain[:, at], bias[:, at], 2)
        small_ref[at, :] = columns + jnp.where(lane_of(columns.shape) == 5, upright(down_sums[:, at]), 0.0)
    for at, _ in row_tiles(rows):
        part_ref[at, :] = mm(grad_hidden_v[at, :], w_up_v[...], NT).astype(BF16)
    lane = lane_of((half, 128))
    own = pl.ds(pl.multiple_of(core * half, 8), half)
    for j, column in enumerate(interleaved(upright(up_sums_v[...]), unit, units // half)):
        small_ref[own, :] += jnp.where(lane == 6 + j, column, 0.0)
    for store in stores:
        store.wait()


def mlp(unit, bits, flags, b_proj, gain, bias, b_up, code, own, got, mine, other, cot_mine, cot_other, w_proj, w_up, w_down):
    rows, half = own.shape
    width, units = 2 * half, w_up.shape[1] // 2
    specs = [SMEM] + [VMEM] * 3 + [pl.BlockSpec((1, units), lambda i, b: (0, b[2]))] + [HBM] * 10
    wide, tall = ((rows, width), BF16), ((rows, units), BF16)
    block = ((rows // 2, width), BF16)
    outs = (
        wide,
        *dealt(units, 2 * units // (width // unit // 2), width)[0],
        *dealt(width, 4 * unit, units)[0],
        block,
        ((width, 128), F32),
        ((rows, width), F32),
        block,
    )
    scratch = [
        pltpu.VMEM(*wide),
        pltpu.VMEM(*wide),
        pltpu.VMEM((width, width), BF16),
        pltpu.VMEM((width, units), BF16),
        pltpu.VMEM((units, width), BF16),
        pltpu.VMEM((rows, width), F32),
        pltpu.VMEM(*wide),
        pltpu.VMEM(*wide),
        pltpu.VMEM(*tall),
        pltpu.VMEM(*tall),
        pltpu.VMEM(*block),
        pltpu.VMEM((1, units), F32),
        pltpu.VMEM(code.shape, F32),
        pltpu.VMEM((rows, half), BF16),
        pltpu.VMEM((rows, half), BF16),
        pltpu.SemaphoreType.DMA((13,)),
    ]
    out_specs = (VMEM,) * 7 + (HBM,) * 2
    hold = (True,) + (False,) * 4 + (True,) * 4
    kernel = partial(mlp_kernel, images=flags.shape[1], unit=unit)
    run = call(kernel, "mlp", outs, scratch, specs, out_specs, prefetch=1, hold=hold)
    return run(
        bits, flags, b_proj, gain, bias, b_up, code, own, got, mine, other, cot_mine, cot_other, w_proj, w_up, w_down
    )


def deal(bit, rows, send_ref, keep_ref):
    run = send_ref.shape[1]
    for i in range(send_ref.shape[0]):
        low, high = rows[2 * i * run : (2 * i + 1) * run], rows[(2 * i + 1) * run : (2 * i + 2) * run]
        send_ref[i] = jnp.where(bit == 0, high, low).astype(BF16)
        keep_ref[i] = jnp.where(bit == 0, low, high).astype(BF16)


def deal_part(bit, rows, send_ref, keep_ref, step):
    count = rows.shape[0] // (2 * send_ref.shape[1])
    part = pl.ds(step * count, count)
    deal(bit, rows, send_ref.at[part], keep_ref.at[part])


def dealt(height, run, width):
    shape = (height // (2 * run), run, width)
    count = ROW_STEP // (2 * run)
    return [(shape, BF16)] * 2, [pl.BlockSpec((count, run, width), lambda i, *_: (i, 0, 0))] * 2


def upright(row):
    return jnp.broadcast_to(row, (128, row.shape[1])).T


def lane_of(shape):
    return lax.broadcasted_iota(jnp.int32, shape, 1)


def interleaved(column, unit, parts):
    blocks = column.shape[0] // (unit * parts)
    out = []
    for j in range(parts):
        pieces = [column[(k * parts + j) * unit : (k * parts + j + 1) * unit] for k in range(blocks)]
        out.append(jnp.concatenate(pieces, 0))
    return out


def ln_columns(grad, weight, sums, gain_ref, bias_ref, place):
    first = jnp.sum(weight * grad, 1, keepdims=True)
    second = jnp.sum(weight * sums, 1, keepdims=True)
    lane = lane_of((weight.shape[0], 128))
    scaled = (first - upright(bias_ref) * second) / upright(gain_ref)
    return jnp.where(lane == place, scaled, jnp.where(lane == place + 1, second, 0.0))


def add_kernel(left_ref, right_ref, out_ref):
    out_ref[...] = (left_ref[...].astype(F32) + right_ref[...].astype(F32)).astype(out_ref.dtype)


def add(after, left, right):
    run = call(add_kernel, "add_blocks", ((left.shape, BF16),), [], [VMEM, VMEM], after=after)
    return run(left, right)[0]


def sides(core_ref, kept, other):
    return jnp.where(core_ref[0] == 0, kept, other), jnp.where(core_ref[0] == 0, other, kept)


def join_up_kernel(core_ref, kept_ref, other_ref, out_ref):
    units = kept_ref.shape[1]
    out_ref[:, :units], out_ref[:, units:] = sides(core_ref, kept_ref[...], other_ref[...])


def join_up(after, core, kept, other):
    rows, units = kept.shape
    return call(join_up_kernel, "join_up", (((rows, 2 * units), F32),), [], [VMEM] * 2, prefetch=1, after=after)(
        core, kept, other
    )[0]


def join_kernel(core_ref, two_ref, two_other_ref, one_ref, one_other_ref, qkv_ref, proj_ref, *refs):
    rows, half = two_ref.shape[0], proj_ref.shape[1] // 2
    pad = refs[-1]
    big = (two_ref.shape[1] - half) // 3
    small = half - big
    twos = sides(core_ref, two_ref[...], two_other_ref[...])
    ones = sides(core_ref, one_ref[...], one_other_ref[...])
    for core, (two, one) in enumerate(zip(twos, ones)):
        proj_ref[:, core * half : (core + 1) * half] = two[:, 3 * big :]
        for i in range(3):
            at = 2 * i * half + core * half
            qkv_ref[:, at : at + big] = two[:, i * big : (i + 1) * big]
            qkv_ref[:, at + big : at + half] = one[:, i * small : (i + 1) * small]
    pad[...] = jnp.zeros_like(pad)
    pad[:rows, :] = one_ref[:, 3 * small :] + one_other_ref[:, 3 * small :]
    turned = pad[...].T
    lane = 0
    for ref in refs[:-1]:
        ref[...] = turned[lane : lane + ref.shape[0], :rows]
        lane += ref.shape[0]


def join_all(after, core, two, two_other, one, one_other, half):
    rows = two.shape[0]
    outs = [((rows, 6 * half), F32), ((rows, 2 * half), F32)] + [((count, rows), F32) for count in (1, 1, 1, 1, 1, 1, 4, 2)]
    scratch = [pltpu.VMEM((128, 128), F32)]
    run = call(join_kernel, "join_all", outs, scratch, [VMEM] * 4, prefetch=1, after=after)
    return run(core, two, two_other, one, one_other)


def finish_kernel(x_ref, dx_ref, beside_ref, across_ref, gain_ref, middle_ref, out_ref):
    unit, scale = centre(x_ref[...].astype(F32))
    grad = (dx_ref[...] + beside_ref[...].astype(F32) + across_ref[...].astype(F32)).T
    out_ref[...] = (middle_ref[...] + norm_back(unit, scale, grad * gain_ref[...].astype(F32))).astype(BF16)


def finish(after, x, dx, beside, across, gain, middle):
    rows, width = x.shape
    tile = pl.BlockSpec((TILE, width), lambda i: (i, 0))
    one = pl.BlockSpec((1, width), lambda i: (0, 0))
    turned = pl.BlockSpec((width, TILE), lambda i: (0, i))
    specs = [tile, turned, turned, turned, one, tile]
    run = call(finish_kernel, "token_gradient", ((x.shape, BF16),), [], specs, (tile,), (rows // TILE,), after=after)
    return run(x, dx, beside, across, gain, middle)[0]


def output_kernel(flags_ref, code_ref, middle_ref, down_ref, got_ref, bias_ref, out_ref, *, images):
    kept = keep_column(code_ref, flags_ref, 1, images)
    branch = down_ref[...].astype(F32) + got_ref[...].astype(F32) + bias_ref[...].astype(F32)
    out_ref[...] = (middle_ref[...] + kept * branch).astype(BF16)


def layer_out(after, flags, code, middle, down, got, bias):
    rows, width = got.shape
    tile = pl.BlockSpec((TILE, width), lambda i: (i, 0))
    one = pl.BlockSpec((1, width), lambda i: (0, 0))
    specs = [SMEM, pl.BlockSpec((8, TILE), lambda i: (0, i)), tile, tile, tile, one]
    kernel = partial(output_kernel, images=flags.shape[1])
    run = call(kernel, "layer_output", ((got.shape, BF16),), [], specs, (tile,), (rows // TILE,), after=after)
    return run(flags, code, middle, down, got, bias)[0]


def swap_halves(rows):
    half = rows.shape[0] // 2
    return jnp.concatenate([rows[half:], rows[:half]], 0)


def pick(array, index, dim):
    return lax.dynamic_index_in_dim(array, index, dim, keepdims=False)


class Links:
    def __init__(self, mesh):
        self.dp, self.blk = mesh.shape["dp"], mesh.shape["blk"]
        self.bits = self.dp.bit_length() - 1

    def core(self, value):
        return lax.ppermute(value, "blk", [(i, i ^ 1) for i in range(self.blk)])

    def side(self, value):
        return lax.ppermute(value, "blk", [(i, i ^ 2) for i in range(self.blk)])

    def cross(self, value, step):
        if step == "x":
            return self.side(value)
        return lax.ppermute(value, "dp", [(i, i ^ (1 << step)) for i in range(self.dp)])

    def bit(self, step):
        if step == "x":
            return lax.axis_index("blk") // 2
        return (lax.axis_index("dp") >> step) & 1

    def swap(self, value):
        top = self.dp // 2
        pairs = []
        for d in range(self.dp):
            for b in range(self.blk):
                high, core = d // top, b % 2
                pairs.append((d * self.blk + b, (d % top + core * top) * self.blk + (b - core + high)))
        return lax.ppermute(value, ("dp", "blk"), pairs)


class Portion:
    def __init__(self, links, send, keep, dims, order, by_core=True):
        self.links, self.order, self.by_core = links, list(order), by_core
        self.dims = [dim for dim in dims if dim != order[0]]
        self.tail = (send.shape[0] * send.shape[1] // 2 ** len(self.dims), send.shape[2])
        self.kept = keep
        self.arrived = links.cross(send, order[0])

    def advance(self, after):
        links = self.links
        self.order.pop(0)
        if not self.order:
            kept, arrived = self.kept.reshape(self.tail), self.arrived.reshape(self.tail)
            if not self.by_core:
                self.total = call(add_kernel, "sum_last", ((self.tail, F32),), [], [VMEM] * 2, after=after)(kept, arrived)[0]
                return self.total
            half = self.tail[0] // 2

            def last_kernel(core_ref, kept_ref, arrived_ref, send_ref, keep_ref):
                total = kept_ref[...].astype(F32) + arrived_ref[...].astype(F32)
                send_ref[...] = jnp.where(core_ref[0] == 0, total[half:], total[:half])
                keep_ref[...] = jnp.where(core_ref[0] == 0, total[:half], total[half:])

            shape = (half, self.tail[1])
            core = (lax.axis_index("blk") % 2).reshape(1).astype(jnp.int32)
            run = call(last_kernel, "sum_last", ((shape, F32), (shape, F32)), [], [VMEM] * 2, prefetch=1, after=after)
            send, self.total = run(core, kept, arrived)
            self.other = links.core(send)
            return self.total
        follow = self.order[0]
        spot = self.dims.index(follow)
        self.dims.pop(spot)
        outer, inner = 2**spot, 2 ** (len(self.dims) - spot)
        shape = (outer, inner) + self.tail
        view = (outer, 2, inner) + self.tail

        def kernel(bit_ref, kept_ref, arrived_ref, send_ref, keep_ref):
            for out_ref, where in ((send_ref, 1 - bit_ref[0]), (keep_ref, bit_ref[0])):
                out_ref[...] = (kept_ref[:, where].astype(F32) + arrived_ref[:, where].astype(F32)).astype(BF16)

        run = call(kernel, "sum_half", ((shape, BF16), (shape, BF16)), [], [VMEM] * 2, prefetch=1, after=after)
        send, keep = run(links.bit(follow).reshape(1).astype(jnp.int32), self.kept.reshape(view), self.arrived.reshape(view))
        self.kept = keep
        self.arrived = links.cross(send, follow)
        return keep


def merged(links, down, up, after):
    count, rb, width = 2 ** len(down.dims), down.tail[0], down.tail[1]
    double, units = up.tail
    high = count // 2
    top = high // 2

    def kernel(bit_ref, down_ref, down_got_ref, up_ref, up_got_ref, send_ref, keep_ref):
        for out_ref, where in ((send_ref, 1 - bit_ref[0]), (keep_ref, bit_ref[0])):
            for i in range(high):
                at = ((i % top) * 2 + where) * 2 + i // top
                out_ref[i, :rb] = (down_ref[at].astype(F32) + down_got_ref[at].astype(F32)).astype(BF16)
                total = (up_ref[2 * i + where].astype(F32) + up_got_ref[2 * i + where].astype(F32)).astype(BF16)
                for part in range(units // width):
                    start = rb + part * double
                    out_ref[i, start : start + double] = total[:, part * width : (part + 1) * width]

    shape = (high, rb + double * (units // width), width)
    bit = links.bit(1).reshape(1).astype(jnp.int32)
    run = call(kernel, "sum_both", ((shape, BF16), (shape, BF16)), [], [VMEM] * 4, prefetch=1, after=after)
    fold = (count, rb, width), (count, double, units)
    return run(
        bit, down.kept.reshape(fold[0]), down.arrived.reshape(fold[0]), up.kept.reshape(fold[1]), up.arrived.reshape(fold[1])
    )


def parted(after, core, kept, arrived, rb, unit, units):
    width = kept.shape[1]

    def kernel(core_ref, kept_ref, arrived_ref, down_ref, send_ref, keep_ref):
        total = kept_ref[...].astype(F32) + arrived_ref[...].astype(F32)
        down_ref[...] = total[:rb]
        for part in range(units // width):
            start = rb + part * 2 * unit
            low, high = total[start : start + unit], total[start + unit : start + 2 * unit]
            cols = slice(part * width, (part + 1) * width)
            send_ref[:, cols] = jnp.where(core_ref[0] == 0, high, low)
            keep_ref[:, cols] = jnp.where(core_ref[0] == 0, low, high)

    outs = (((rb, width), F32), ((unit, units), F32), ((unit, units), F32))
    return call(kernel, "part_both", outs, [], [VMEM] * 2, prefetch=1, after=after)(core, kept, arrived)


def local(
    links,
    tokens,
    cotangent,
    segments,
    padding,
    drop_keep,
    ln1_gain,
    ln1_bias,
    qkv_weight,
    qv_bias,
    proj_weight,
    proj_bias,
    ln2_gain,
    ln2_bias,
    fc1_weight,
    fc1_bias,
    fc2_weight,
    fc2_bias,
):
    _, block, width = tokens.shape
    half = width // 2
    units = fc1_weight.shape[1] // 2
    core = lax.axis_index("blk") % 2
    core_arg = core.reshape(1).astype(jnp.int32)
    owners = links.dp * links.blk
    rows = 2 * block

    code = jnp.where(padding == 1, segments, PAD_CLASS).astype(BF16)
    mine = jnp.concatenate([tokens[0], jnp.pad(code, ((0, 15), (0, width - block)))], 0)
    far = links.side(mine)
    other = links.core(mine)
    cot_mine = cotangent[0]
    cot_other = links.core(cot_mine)
    flags = drop_keep[:, 0, :]
    bits = links.bits
    low = [bits - 1 - i for i in range(bits)]
    chip = low + ["x"]
    by_core = low[1:] + ["x", low[0]]
    tail = [s for s in low if s > 1][::-1]
    side_bits = jnp.stack([links.bit("x"), links.bit(0), core, links.bit(1)]).astype(jnp.int32)
    unit = width // owners

    gain_one, bias_one = ln1_gain.reshape(1, -1), ln1_bias.reshape(1, -1)
    gain_two, bias_two = ln2_gain.reshape(1, -1), ln2_bias.reshape(1, -1)
    bias_qv = qv_bias.reshape(1, -1)
    near_code, near_normed, w_qkv, qt, near_kv, state = forward_near(
        core_arg, mine, other, gain_one, bias_one, qkv_weight, bias_qv
    )
    far = lax.dynamic_update_slice(far, near_code[:, :128].astype(BF16), (block + 8, 0))
    far_other = links.core(far)
    bias_v = lax.dynamic_slice(bias_qv, (0, width + core * half), (1, half))
    far_code, lse, own, far_normed, far_kv, ot = forward_far(
        far, far_other, gain_one, bias_one, w_qkv, bias_v, qt, near_code, state
    )
    got = links.core(own)
    part, send_down, keep_down, send_up, keep_up, down_send, small, middle, down = mlp(
        unit,
        side_bits,
        flags,
        proj_bias.reshape(1, -1),
        gain_two,
        bias_two,
        fc1_bias.reshape(1, -1),
        near_code,
        own,
        got,
        tokens[0],
        other,
        cot_mine,
        cot_other,
        proj_weight,
        fc1_weight,
        fc2_weight,
    )
    got_part = links.core(part)
    down_portion = Portion(links, send_down, keep_down, by_core, ["x", 0, 1] + tail, False)
    up_portion = Portion(links, send_up, keep_up, chip, [0, "x", 1] + tail)
    down_other = links.core(down_send)
    held = (middle, cot_mine, cot_other, proj_weight, qt, far_kv, ot, w_qkv)
    far_dx, far_send, far_sums, small, do, grad_half, grad_middle, dq, far_grad = far_back(
        (), core_arg, flags, near_code, far_code, lse, part, got_part, gain_two, small, held
    )
    last = down_portion.advance((far_grad,))
    last = up_portion.advance((last,))
    far_got = links.core(far_send)
    ready = (near_code, lse, do, far_sums, gain_one, bias_one)
    held = (qt, near_kv, ot, dq, w_qkv, near_normed, far_normed, far_grad)
    send, keep, small, q_done, v_done, done = near_back(
        (last,), unit, 0, False, side_bits, ready + (small,), held + (got, grad_half)
    )
    two_portion = Portion(links, send, keep, chip, [0, 1, "x"] + tail)
    far_sum = add((keep,), far_dx, far_got)
    across = links.side(far_sum)
    send, keep = merged(links, down_portion, up_portion, (far_sum,))
    both_portion = Portion(links, send, keep, low[:-1], [1] + tail)
    near_send, send, keep, near_dx = near_back(
        (keep,), unit, 4, True, side_bits, ready + (small, q_done, v_done), held + (done,)
    )
    near_got = links.core(near_send)
    one_portion = Portion(links, send, keep, chip, ["x", 0, 1] + tail)
    last = both_portion.advance((keep,))
    last = two_portion.advance((last, across))
    layer_output = layer_out((last,), flags, near_code, middle, down, down_other, fc2_bias.reshape(1, -1))
    last = one_portion.advance((layer_output,))
    last = two_portion.advance((last,))
    for _ in tail[1:]:
        last = both_portion.advance((last,))
    last = one_portion.advance((last,))
    tokens_grad = finish((last,), tokens[0], near_dx, near_got, across, gain_one, grad_middle)
    last = two_portion.advance((tokens_grad,))
    last = one_portion.advance((last,))
    down_total, send, keep = parted(
        (last,),
        core_arg,
        both_portion.kept.reshape(both_portion.tail),
        both_portion.arrived.reshape(both_portion.tail),
        2 * units // owners,
        unit,
        units,
    )
    down_grad = links.swap(down_total)
    up_got = links.core(send)
    last = down_total
    while two_portion.order:
        last = two_portion.advance((last,))
    while one_portion.order:
        last = one_portion.advance((last,))
    up_grad = join_up((last,), core_arg, keep, up_got)
    qkv_grad, proj_grad, *vectors = join_all(
        (up_grad,), core_arg, two_portion.total, two_portion.other, one_portion.total, one_portion.other, half
    )
    g1, b1, g2, b2, pb, d2, u1, qvb = (vector.reshape(-1) for vector in vectors)
    shape = tokens.shape
    return (
        layer_output.reshape(shape),
        tokens_grad.reshape(shape),
        g1,
        b1,
        qkv_grad,
        qvb,
        proj_grad,
        pb,
        g2,
        b2,
        up_grad,
        u1,
        down_grad,
        d2,
    )


def solution(mesh):
    both = P(("dp", "blk"))
    rows = P(("dp", "blk"), None)
    token = P("dp", "blk", None)
    placed = (token, token, P("dp", "blk"), P("dp", "blk"), P(None, "dp", None)) + (P(),) * 12
    return jax.shard_map(
        partial(local, Links(mesh)),
        mesh=mesh,
        in_specs=placed,
        out_specs=(token, token, both, both, rows, both, rows, both, both, both, rows, both, rows, both),
        check_vma=False,
    )
```

```python
from functools import partial

import jax
import jax.numpy as jnp
from jax import lax
from jax.experimental import pallas as pl
from jax.experimental.pallas import tpu as pltpu
from jax.sharding import PartitionSpec as P

HEAD_DIM = 64
F32 = jnp.float32
BF16 = jnp.bfloat16
epsilon = 1e-06
keep_rate = 0.9
attn_scale = 0.125
negative = -1e30
PAD_CLASS = 4
TILE = 256
MIB = 2**20
FLOPS_PER_US = 1.0 * 10**9
BUDGET = {
    "near_forward": (28, 16),
    "far_forward": (28, 13),
    "mlp": (44, 30),
    "far_backward": (42, 20),
    "near_backward_first": (36, 19),
    "near_backward_last": (36, 13),
    "join_up": (8, 1),
    "sum_both": (12, 2),
    "part_both": (8, 1),
    "join_all": (8, 1),
    "sum_half": (8, 2),
    "sum_last": (8, 1),
    "add_blocks": (8, 2),
    "token_gradient": (12, 2),
    "layer_output": (12, 2),
}
NN = ((1,), (0,))
NT = ((1,), (1,))
TN = ((0,), (0,))
VMEM = pl.BlockSpec(memory_space=pltpu.VMEM)
SMEM = pl.BlockSpec(memory_space=pltpu.SMEM)
HBM = pl.BlockSpec(memory_space=pltpu.HBM)
ROW_STEP = 384


def mm(left, right, dims=NN):
    return lax.dot_general(left, right, (dims, ((), ())), preferred_element_type=F32)


def rows_of(head):
    return slice(head * HEAD_DIM, (head + 1) * HEAD_DIM)


def lanes_of(pair):
    return slice(pair * 128, (pair + 1) * 128)


def centre(values):
    shifted = values - jnp.mean(values, -1, keepdims=True)
    spread = jnp.mean(shifted * shifted, -1, keepdims=True)
    scale = lax.rsqrt(spread + epsilon)
    return shifted * scale, scale


def norm_back(unit, scale, grad):
    return (grad - jnp.mean(grad, -1, keepdims=True) - unit * jnp.mean(grad * unit, -1, keepdims=True)) * scale


def call(kernel, name, outs, scratch, specs, out_specs=None, grid=None, prefetch=0, after=(), pin=(), hold=()):
    limit, cost = BUDGET[name]
    out_specs = out_specs or tuple(VMEM for _ in outs)
    first = prefetch + len(specs)

    def ordered(*refs):
        kernel(*refs[:first], *refs[first + len(after) :])

    spec = pltpu.PrefetchScalarGridSpec(
        num_scalar_prefetch=prefetch,
        grid=grid or (1,),
        in_specs=list(specs) + [pl.BlockSpec(memory_space=pl.ANY)] * len(after),
        out_specs=out_specs,
        scratch_shapes=scratch,
    )
    run = pl.pallas_call(
        ordered,
        out_shape=tuple(
            (pltpu.HBM if pinned else jax.ShapeDtypeStruct)(shape, kind)
            for (shape, kind), pinned in zip(outs, hold if hold else [spec is HBM for spec in out_specs])
        ),
        grid_spec=spec,
        compiler_params=pltpu.CompilerParams(vmem_limit_bytes=limit * MIB),
        cost_estimate=pl.CostEstimate(flops=int(cost * FLOPS_PER_US), bytes_accessed=1, transcendentals=0),
        name=name,
    )

    def place(*args):
        held = list(args)
        for i, spec in enumerate(specs):
            if spec is HBM or i in pin:
                held[prefetch + i] = pltpu.with_memory_space_constraint(held[prefetch + i], pltpu.HBM)
        return run(*held, *after)

    return place


def query_mask(code):
    kind = lax.broadcasted_iota(jnp.int32, (HEAD_DIM, code.shape[1]), 0).astype(F32)
    seen = (code == kind) | ((code == PAD_CLASS) & (kind == PAD_CLASS - 1)) | (kind > PAD_CLASS)
    return jnp.where(seen, 0.0, negative).astype(BF16)


def load_queries(qt_ref, code, qx, heads):
    mask = query_mask(code)
    for h in range(heads):
        own = slice(0, HEAD_DIM) if h % 2 == 0 else slice(HEAD_DIM, 128)
        rest = slice(HEAD_DIM, 128) if h % 2 == 0 else slice(0, HEAD_DIM)
        qx[h, own, :] = qt_ref[rows_of(h), :]
        qx[h, rest, :] = mask


def load_keys(k_ref, first, code, kx, heads):
    keys = k_ref.shape[0]
    kind = lax.broadcasted_iota(jnp.int32, (128, keys), 0).astype(F32)
    low = (kind == code).astype(F32).T.astype(BF16)
    high = (kind - HEAD_DIM == code).astype(F32).T.astype(BF16)
    lane = lax.broadcasted_iota(jnp.int32, (keys, 128), 1)
    for pair in range(heads // 2):
        slab = k_ref[:, first + pair * 128 : first + (pair + 1) * 128]
        kx[2 * pair] = jnp.where(lane < HEAD_DIM, slab, high)
        kx[2 * pair + 1] = jnp.where(lane < HEAD_DIM, low, slab)


def note_tiles(q_code, k_code, act):
    def ranges(code):
        image = jnp.minimum(code, float(PAD_CLASS - 1))
        cuts = [image[:, i : i + TILE // 2] for i in range(0, code.shape[1], TILE // 2)]
        return [(jnp.min(c), jnp.max(c)) for c in cuts]

    q_ranges = ranges(q_code)
    k_ranges = q_ranges if k_code is q_code else ranges(k_code)

    def meet(i, j):
        return (q_ranges[i][0] <= k_ranges[j][1]) & (q_ranges[i][1] >= k_ranges[j][0])

    for i in range(len(q_ranges) // 2):
        for j in range(len(k_ranges) // 2):
            four = [[meet(2 * i + u, 2 * j + v) for v in range(2)] for u in range(2)]
            queries = [four[u][0] | four[u][1] for u in range(2)]
            keys = [four[0][v] | four[1][v] for v in range(2)]
            keys = keys[0].astype(jnp.int32) + 2 * keys[1].astype(jnp.int32)
            queries = queries[0].astype(jnp.int32) + 2 * queries[1].astype(jnp.int32)
            act[i, j] = jnp.where((keys == 3) & (queries < 3), 3 + queries, keys)


def each_tile(act, queries, keys, body):
    across = keys // TILE
    half = TILE // 2

    def step(index, carry):
        q_tile, k_tile = index // across, index % across
        kind = act[q_tile, k_tile]
        q_start, k_start = q_tile * TILE, k_tile * TILE

        def span(start, size):
            return pl.ds(pl.multiple_of(start, half), size)

        @pl.when(kind == 3)
        def _():
            body(span(q_start, TILE), span(k_start, TILE))

        @pl.when((kind == 1) | (kind == 2))
        def _():
            body(span(q_start, TILE), span(k_start + (kind - 1) * half, half))

        @pl.when(kind > 3)
        def _():
            body(span(q_start + (kind - 4) * half, half), span(k_start, TILE))

        return carry

    lax.fori_loop(0, (queries // TILE) * across, step, 0)


def fold_keys(act, kx, qx, vt, top, total, acc, heads):
    def body(at, span):
        hs = range(heads)
        scores = [mm(kx[h, span, :], qx[h, :, at]) for h in hs]
        old = [top[h : h + 1, at] for h in hs]
        new = [jnp.maximum(old[h], jnp.max(scores[h], 0, keepdims=True)) for h in hs]
        decay = [jnp.exp(old[h] - new[h]) for h in hs]
        weights = [jnp.exp(scores[h] - new[h]) for h in hs]
        added = [mm(vt[rows_of(h), span], weights[h].astype(BF16)) for h in hs]
        for h in hs:
            top[h : h + 1, at] = new[h]
            total[h : h + 1, at] = decay[h] * total[h : h + 1, at] + jnp.sum(weights[h], 0, keepdims=True)
            acc[rows_of(h), at] = decay[h] * acc[rows_of(h), at] + added[h]

    each_tile(act, qx.shape[2], kx.shape[1], body)


def normed_rows(ref, at, gain, bias):
    return (centre(ref[at, :].astype(F32))[0] * gain + bias).astype(BF16)


def begin(sems, index, source, target):
    copy = pltpu.make_async_copy(source, target, sems.at[index])
    copy.start()
    return copy


def load_tokens(refs, code_ref):
    block = refs[0].shape[0] - 16
    for index, ref in enumerate(refs):
        row = ref[block : block + 16, :block].astype(F32)[:1]
        code_ref[:, index * block : (index + 1) * block] = jnp.broadcast_to(row, (8, block))
        for start in range(0, block, TILE):
            at = slice(index * block + start, index * block + start + TILE)
            yield at, ref[start : start + TILE, :]


def turn(array):
    return array.astype(F32).T.astype(BF16)


def near_kernel(
    core_ref,
    mine_ref,
    other_ref,
    gain_ref,
    bias_ref,
    bq_ref,
    bv_ref,
    weight_hbm,
    code_ref,
    normed_hbm,
    w_hbm,
    qt_hbm,
    kv_hbm,
    state_hbm,
    act,
    kx,
    qx,
    vt,
    normed_v,
    w_v,
    qt_v,
    kv_v,
    state,
    sems,
    *,
    heads,
):
    half = heads * HEAD_DIM
    acc, top, total = state.at[:half, :], state.at[half : half + 8, :], state.at[half + 8 :, :]
    first = pl.multiple_of(core_ref[0] * half, 128)
    loads = [
        begin(sems, i, weight_hbm.at[:, pl.ds(2 * i * half + first, half)], w_v.at[:, i * half : (i + 1) * half])
        for i in range(3)
    ]
    gain, bias = gain_ref[...].astype(F32), bias_ref[...].astype(F32)
    bq, bv = bq_ref[...].astype(F32), bv_ref[...].astype(F32)
    for at, tokens in load_tokens((mine_ref, other_ref), code_ref):
        normed = (centre(tokens.astype(F32))[0] * gain + bias).astype(BF16)
        normed_v[:, at] = turn(normed)
        for load in loads:
            load.wait()
        loads = []
        q = (mm(normed, w_v[:, :half]) + bq).astype(BF16).astype(F32) * attn_scale
        qt_v[:, at] = q.T.astype(BF16)
        kv_v[at, :half] = mm(normed, w_v[:, half : 2 * half]).astype(BF16)
        v = (mm(normed, w_v[:, 2 * half :]) + bv).astype(BF16)
        kv_v[at, half:] = v
        vt[:, at] = turn(v)
    pairs = ((normed_v, normed_hbm), (w_v, w_hbm), (qt_v, qt_hbm), (kv_v, kv_hbm))
    stores = [begin(sems, 3 + i, source, target) for i, (source, target) in enumerate(pairs)]
    code = code_ref[0:1, :]
    note_tiles(code, code, act)
    load_queries(qt_v, code, qx, heads)
    load_keys(kv_v, 0, code, kx, heads)
    top[...] = jnp.full_like(top, -1e29)
    total[...] = jnp.zeros_like(total)
    acc[...] = jnp.zeros_like(acc)
    fold_keys(act, kx, qx, vt, top, total, acc, heads)
    stores.append(begin(sems, 7, state, state_hbm))
    for store in stores:
        store.wait()


def forward_near(core, mine, other, gain, bias, qkv_weight, qv_bias):
    padded, width = mine.shape
    half = width // 2
    heads = half // HEAD_DIM
    rows = 2 * (padded - 16)
    specs = [VMEM] * 4 + [
        pl.BlockSpec((1, half), lambda i, c: (0, c[0])),
        pl.BlockSpec((1, half), lambda i, c: (0, 2 + c[0])),
        HBM,
    ]
    kept = (((width, rows), BF16), ((width, 3 * half), BF16), ((half, rows), BF16), ((rows, width), BF16))
    kept += (((half + 16, rows), F32),)
    outs = (((8, rows), F32),) + kept
    scratch = [
        pltpu.SMEM((rows // TILE, rows // TILE), jnp.int32),
        pltpu.VMEM((heads, rows, 128), BF16),
        pltpu.VMEM((heads, 128, rows), BF16),
        pltpu.VMEM((half, rows), BF16),
    ]
    scratch += [pltpu.VMEM(shape, kind) for shape, kind in kept] + [pltpu.SemaphoreType.DMA((8,))]
    run = call(
        partial(near_kernel, heads=heads),
        "near_forward",
        outs,
        scratch,
        specs,
        (VMEM,) + (HBM,) * 5,
        prefetch=1,
        hold=(True,) * 6,
    )
    return run(core, mine, other, gain, bias, qv_bias, qv_bias, qkv_weight)


def far_kernel(
    far_ref,
    other_ref,
    gain_ref,
    bias_ref,
    bv_ref,
    w_hbm,
    qt_hbm,
    state_hbm,
    code_hbm,
    far_code_ref,
    lse_ref,
    o_ref,
    normed_hbm,
    kv_hbm,
    ot_hbm,
    act,
    kx,
    qx,
    vt,
    state,
    code_ref,
    w_v,
    qt_v,
    normed_v,
    kv_v,
    ot_v,
    sems,
    *,
    heads,
):
    half = heads * HEAD_DIM
    acc, top, total = state.at[:half, :], state.at[half : half + 8, :], state.at[half + 8 :, :]
    pairs = ((w_hbm.at[:, half:], w_v), (qt_hbm, qt_v), (state_hbm, state), (code_hbm, code_ref))
    loads = [begin(sems, i, source, target) for i, (source, target) in enumerate(pairs)]
    gain, bias = gain_ref[...].astype(F32), bias_ref[...].astype(F32)
    bv = bv_ref[...].astype(F32)
    for at, tokens in load_tokens((far_ref, other_ref), far_code_ref):
        normed = (centre(tokens.astype(F32))[0] * gain + bias).astype(BF16)
        normed_v[:, at] = turn(normed)
        for load in loads:
            load.wait()
        loads = []
        kv_v[at, :half] = mm(normed, w_v[:, :half]).astype(BF16)
        v = (mm(normed, w_v[:, half:]) + bv).astype(BF16)
        kv_v[at, half:] = v
        vt[:, at] = turn(v)
    stores = [begin(sems, 4, normed_v, normed_hbm), begin(sems, 5, kv_v, kv_hbm)]
    code, far_code = code_ref[0:1, :], far_code_ref[0:1, :]
    note_tiles(code, far_code, act)
    load_queries(qt_v, code, qx, heads)
    load_keys(kv_v, 0, far_code, kx, heads)
    fold_keys(act, kx, qx, vt, top, total, acc, heads)
    lse_ref[...] = top[...] + jnp.log(jnp.maximum(total[...], 1e-30))
    for h in range(heads):
        acc[rows_of(h), :] = acc[rows_of(h), :] / total[h : h + 1, :]
    ot_v[...] = acc[...].astype(BF16)
    stores.append(begin(sems, 6, ot_v, ot_hbm))
    for pair in range(heads // 2):
        o_ref[:, lanes_of(pair)] = acc[lanes_of(pair), :].T.astype(BF16)
    for store in stores:
        store.wait()


def forward_far(far, other, gain, bias, w, qv_bias, qt, code, state):
    padded, width = far.shape
    half = width // 2
    heads = half // HEAD_DIM
    rows = 2 * (padded - 16)
    specs = [VMEM] * 5 + [HBM] * 4
    kept = (((width, rows), BF16), ((rows, width), BF16), ((half, rows), BF16))
    outs = (((8, rows), F32), ((8, rows), F32), ((rows, half), BF16)) + kept
    scratch = [
        pltpu.SMEM((rows // TILE, rows // TILE), jnp.int32),
        pltpu.VMEM((heads, rows, 128), BF16),
        pltpu.VMEM((heads, 128, rows), BF16),
        pltpu.VMEM((half, rows), BF16),
        pltpu.VMEM((half + 16, rows), F32),
        pltpu.VMEM((8, rows), F32),
        pltpu.VMEM((width, width), BF16),
        pltpu.VMEM((half, rows), BF16),
    ]
    scratch += [pltpu.VMEM(shape, kind) for shape, kind in kept] + [pltpu.SemaphoreType.DMA((7,))]
    run = call(partial(far_kernel, heads=heads), "far_forward", outs, scratch, specs, (VMEM,) * 3 + (HBM,) * 3, hold=(True,) * 6)
    return run(far, other, gain, bias, qv_bias, w, qt, state, code)


def back_tiles(act, kx, qx, kt, dox, delta, qt_ref, kv_ref, do, lse, dq_sum, dk_sum, dv_sum, heads, group):
    half = heads * HEAD_DIM

    def body(at, span):
        for first in range(0, heads, group):
            hs = range(first, first + group)
            scores = {h: mm(kx[h, span, :], qx[h, :, at]) for h in hs}
            dp = {h: mm(kv_ref[span, half + (h // 2) * 128 : half + (h // 2 + 1) * 128], dox[h, :, at]) for h in hs}
            probs = {h: jnp.exp(scores[h] - lse(h, at)) for h in hs}
            rounded = {h: probs[h].astype(BF16) for h in hs}
            ds = {h: (probs[h] * (dp[h] - delta[h : h + 1, at])).astype(BF16) for h in hs}
            dv = {h: mm(do(h, at), rounded[h], NT) for h in hs}
            dk = {h: mm(qt_ref[rows_of(h), at], ds[h], NT) for h in hs}
            dq = {h: mm(kt[rows_of(h), span], ds[h]) for h in hs}
            for h in hs:
                dv_sum[rows_of(h), span] += dv[h]
                dk_sum[rows_of(h), span] += dk[h]
                dq_sum[rows_of(h), at] += dq[h]

    each_tile(act, qx.shape[2], kx.shape[1], body)


def back_ready(act, kx, qx, kt, dox, delta, qt_ref, kv_ref, ot_ref, do, q_code, k_code, heads):
    queries = qt_ref.shape[1]
    note_tiles(q_code, k_code, act)
    load_queries(qt_ref, q_code, qx, heads)
    load_keys(kv_ref, 0, k_code, kx, heads)
    zero = jnp.zeros((HEAD_DIM, queries), BF16)
    for h in range(heads):
        own = slice(0, HEAD_DIM) if h % 2 == 0 else slice(HEAD_DIM, 128)
        rest = slice(HEAD_DIM, 128) if h % 2 == 0 else slice(0, HEAD_DIM)
        grad = do(h, slice(0, queries))
        dox[h, own, :] = grad
        dox[h, rest, :] = zero
        delta[h : h + 1, :] = jnp.sum(grad.astype(F32) * ot_ref[rows_of(h), :].astype(F32), 0, keepdims=True)
    for pair in range(heads // 2):
        kt[lanes_of(pair), :] = turn(kv_ref[:, lanes_of(pair)])


def back_scratch(heads, queries, keys):
    half = heads * HEAD_DIM
    return [
        pltpu.SMEM((queries // TILE, keys // TILE), jnp.int32),
        pltpu.VMEM((heads, keys, 128), BF16),
        pltpu.VMEM((heads, 128, queries), BF16),
        pltpu.VMEM((half, keys), BF16),
        pltpu.VMEM((heads, 128, queries), BF16),
        pltpu.VMEM((8, queries), F32),
        pltpu.VMEM((half, queries), BF16),
        pltpu.VMEM((keys, 2 * half), BF16),
        pltpu.VMEM((half, queries), BF16),
        pltpu.VMEM((half, keys), F32),
        pltpu.VMEM((half, keys), F32),
    ]


def far_back_kernel(
    core_ref,
    flags_ref,
    gain_ref,
    q_code_hbm,
    k_code_hbm,
    lse_hbm,
    part_hbm,
    got_hbm,
    early_hbm,
    middle_hbm,
    cot_mine_hbm,
    cot_other_hbm,
    w_proj_hbm,
    qt_hbm,
    kv_hbm,
    ot_hbm,
    w_hbm,
    dx_ref,
    send_ref,
    sums_hbm,
    small_hbm,
    do_hbm,
    grad_half_hbm,
    grad_middle_hbm,
    dq_hbm,
    out_hbm,
    act,
    kx,
    qx,
    kt,
    dox,
    delta,
    qt_ref,
    kv_ref,
    ot_ref,
    dk_sum,
    dv_sum,
    w_ref,
    dq_sum,
    out_ref,
    middle_v,
    cot_v,
    w_proj_v,
    do_v,
    grad_half_v,
    grad_middle_v,
    sums_v,
    small_v,
    q_code_ref,
    k_code_ref,
    lse_ref,
    part_ref,
    got_ref,
    early_ref,
    sems,
    *,
    heads,
    images,
):
    half = heads * HEAD_DIM
    rows = middle_v.shape[0]
    block = rows // 2
    pairs = (
        (middle_hbm, middle_v),
        (part_hbm, part_ref),
        (got_hbm, got_ref),
        (cot_mine_hbm, cot_v.at[:block, :]),
        (cot_other_hbm, cot_v.at[block:, :]),
        (early_hbm, early_ref),
        (q_code_hbm, q_code_ref),
        (w_proj_hbm.at[pl.ds(pl.multiple_of(core_ref[0] * half, 128), half), :], w_proj_v),
        (qt_hbm, qt_ref),
        (kv_hbm, kv_ref),
        (ot_hbm, ot_ref),
        (k_code_hbm, k_code_ref),
        (lse_hbm, lse_ref),
        (w_hbm.at[:, half:], w_ref),
    )
    loads = [begin(sems, i, source, target) for i, (source, target) in enumerate(pairs)]
    for load in loads[:8]:
        load.wait()
    gain = gain_ref[...].astype(F32)
    total = jnp.zeros((1, 2 * half), F32)
    for at, swapped in row_tiles(rows):
        keep_attn = keep_column(q_code_ref.at[:, at], flags_ref, 0, images)
        unit, scale = centre(middle_v[at, :])
        grad = (part_ref[at, :].astype(F32) + got_ref[swapped, :].astype(F32)) * gain
        grad_middle = cot_v[at, :].astype(F32) + norm_back(unit, scale, grad)
        grad_proj = (keep_attn * grad_middle).astype(BF16)
        grad_half_v[at, :] = jnp.where(core_ref[0] == 0, grad_proj[:, :half], grad_proj[:, half:])
        do_v[:, at] = mm(w_proj_v[...], grad_proj, NT).astype(BF16)
        if at.start < block:
            grad_middle_v[at, :] = grad_middle
            total = total + jnp.sum(grad_proj.astype(F32), 0, keepdims=True)
    small_v[...] = early_ref[...] + jnp.where(lane_of(small_v.shape) == 4, upright(total), 0.0)
    kept = ((do_v, do_hbm), (grad_half_v, grad_half_hbm), (grad_middle_v, grad_middle_hbm), (small_v, small_hbm))
    stores = [begin(sems, 14 + i, source, target) for i, (source, target) in enumerate(kept)]
    for load in loads[8:]:
        load.wait()

    def do(h, at):
        return do_v[rows_of(h), at]

    def lse(h, at):
        return lse_ref[h : h + 1, at]

    q_code, k_code = q_code_ref[0:1, :], k_code_ref[0:1, :]
    back_ready(act, kx, qx, kt, dox, delta, qt_ref, kv_ref, ot_ref, do, q_code, k_code, heads)
    dq_sum[...] = jnp.zeros_like(dq_sum)
    dk_sum[...] = jnp.zeros_like(dk_sum)
    dv_sum[...] = jnp.zeros_like(dv_sum)
    back_tiles(act, kx, qx, kt, dox, delta, qt_ref, kv_ref, do, lse, dq_sum, dk_sum, dv_sum, heads, 3)
    stores.append(begin(sems, 18, dq_sum, dq_hbm))
    out_ref[:half, :] = dk_sum[...].astype(BF16)
    out_ref[half:, :] = dv_sum[...].astype(BF16)
    stores.append(begin(sems, 19, out_ref, out_hbm))
    send_ref[...] = mm(w_ref[...], out_ref[:, block:]).astype(BF16)
    dx_ref[...] = mm(w_ref[...], out_ref[:, :block])
    sums_v[...] = jnp.broadcast_to(jnp.sum(out_ref[...].astype(F32), 1, keepdims=True), sums_v.shape)
    stores.append(begin(sems, 20, sums_v, sums_hbm))
    for store in stores:
        store.wait()


def far_back(after, core, flags, q_code, k_code, lse, part, got, gain, early, held):
    half, queries = held[4].shape
    keys = held[5].shape[0]
    heads = half // HEAD_DIM
    width = 2 * half
    kept = (
        ((half, queries), BF16),
        ((queries, half), BF16),
        ((queries // 2, width), F32),
    )
    column = ((width, 128), F32)
    dq, grad = ((half, queries), F32), ((width, keys), BF16)
    outs = (((width, keys // 2), F32), ((width, keys // 2), BF16), column, column) + kept + (dq, grad)
    scratch = back_scratch(heads, queries, keys) + [
        pltpu.VMEM((width, width), BF16),
        pltpu.VMEM(*dq),
        pltpu.VMEM(*grad),
        pltpu.VMEM((queries, width), F32),
        pltpu.VMEM((queries, width), BF16),
        pltpu.VMEM((half, width), BF16),
        *[pltpu.VMEM(*shape) for shape in kept],
        pltpu.VMEM(*column),
        pltpu.VMEM(*column),
        *[pltpu.VMEM(array.shape, array.dtype) for array in (q_code, k_code, lse, part, got, early)],
        pltpu.SemaphoreType.DMA((21,)),
    ]
    specs = [SMEM, VMEM] + [HBM] * 14
    out_specs = (VMEM,) * 2 + (HBM,) * 7
    kernel = partial(far_back_kernel, heads=heads, images=flags.shape[1])
    run = call(kernel, "far_backward", outs, scratch, specs, out_specs, prefetch=1, after=after)
    return run(core, flags, gain, q_code, k_code, lse, part, got, early, *held)


def near_back_kernel(*refs, first, heads, unit, last):
    bits_ref, code_ref, lse_ref, do_ref, far_sums_ref, gain_ref, bias_ref, early_ref = refs[:8]
    if last:
        q_done_ref, v_done_ref, qt_hbm, kv_hbm, ot_hbm, dq_hbm, w_hbm, near_hbm, far_hbm, grad_hbm, done_hbm = refs[8:19]
        send_ref, send_part, keep_part, dx_hbm = refs[19:23]
        rest = refs[23:]
    else:
        qt_hbm, kv_hbm, ot_hbm, dq_hbm, w_hbm, near_hbm, far_hbm, grad_hbm, got_hbm, grad_half_hbm = refs[8:18]
        send_part, keep_part, small_ref, q_done_ref, v_done_ref, done_hbm = refs[18:24]
        rest = refs[24:]
    act, kx, qx, kt, dox, delta, qt_ref, kv_ref, ot_ref, dk_sum, dv_sum = rest[:11]
    dq_sum, out_ref, near_v, far_v, grad_v, w_ref, sems = rest[11:18]
    part = heads * HEAD_DIM
    half = do_ref.shape[0]
    low = first * HEAD_DIM
    mine = slice(low, low + part)
    block = kv_ref.shape[0] // 2
    pairs = [
        (qt_hbm.at[mine, :], qt_ref),
        (kv_hbm.at[:, mine], kv_ref.at[:, :part]),
        (kv_hbm.at[:, half + low : half + low + part], kv_ref.at[:, part:]),
    ]
    if last:
        done_v, dx_v, small_v = rest[18:]
        pairs += [(ot_hbm.at[mine, :], ot_ref), (dq_hbm.at[mine, :], dq_sum), (done_hbm, done_v)]
        other = part
        own_at = w_ref.shape[1] - 3 * part
        for i in range(3):
            pairs.append((w_hbm.at[:, i * half : i * half + low], w_ref.at[:, i * low : (i + 1) * low]))
    else:
        got_v, grad_half_v, whole_ot = rest[18:]
        pairs += [(ot_hbm, whole_ot), (dq_hbm.at[mine, :], dq_sum), (got_hbm, got_v), (grad_half_hbm, grad_half_v)]
        own_at = 0
        ot_ref = whole_ot
    for i in range(3):
        target = w_ref.at[:, own_at + i * part : own_at + (i + 1) * part]
        pairs.append((w_hbm.at[:, i * half + low : i * half + low + part], target))
    for i in range(2):
        pairs.append((grad_hbm.at[i * half + low : i * half + low + part, :], grad_v.at[i * part : (i + 1) * part, :]))
    pairs += [(near_hbm, near_v), (far_hbm, far_v)]
    loads = [begin(sems, i, source, target) for i, (source, target) in enumerate(pairs)]
    for load in loads[:5]:
        load.wait()

    def do(h, at):
        return do_ref[low + h * HEAD_DIM : low + (h + 1) * HEAD_DIM, at]

    def lse(h, at):
        return lse_ref[first + h : first + h + 1, at]

    code = code_ref[0:1, :]
    back_ready(act, kx, qx, kt, dox, delta, qt_ref, kv_ref, ot_ref, do, code, code, heads)
    dk_sum[...] = jnp.zeros_like(dk_sum)
    dv_sum[...] = jnp.zeros_like(dv_sum)
    back_tiles(act, kx, qx, kt, dox, delta, qt_ref, kv_ref, do, lse, dq_sum, dk_sum, dv_sum, heads, 2)
    out_ref[:part, :] = (dq_sum[...] * attn_scale).astype(BF16)
    out_ref[part : 2 * part, :] = dk_sum[...].astype(BF16)
    out_ref[2 * part :, :] = dv_sum[...].astype(BF16)
    for load in loads[5:]:
        load.wait()
    core = bits_ref[2]
    far_sums = [far_sums_ref[i * half + low : i * half + low + part, :] for i in range(2)]
    sums = jnp.broadcast_to(jnp.sum(out_ref[...].astype(F32), 1, keepdims=True), (3 * part, 128))
    sums = jnp.concatenate([sums[:part], sums[part : 2 * part] + far_sums[0], sums[2 * part :] + far_sums[1]], 0)
    q_column, v_column = sums[:part], sums[2 * part :]
    sums = sums.T[:1]
    if last:
        for start in (block, 0):
            both = mm(w_ref[:, :own_at], done_v[:, start : start + block])
            both = both + mm(w_ref[:, own_at:], out_ref[:, start : start + block])
            if start:
                send_ref[...] = both.astype(BF16)
            else:
                dx_v[...] = both
        stores = [begin(sems, len(pairs), dx_v, dx_hbm)]
        small_v[...] = early_ref[...]
        lane = lane_of((half // 2, 128))
        q_whole = jnp.concatenate([q_done_ref[...], q_column], 0)
        v_whole = jnp.concatenate([v_done_ref[...], v_column], 0)
        for base, column in ((0, q_whole), (half, v_whole)):
            rows = pl.ds(pl.multiple_of(base + core * (half // 2), 8), half // 2)
            for j, piece in enumerate(interleaved(column, unit, 2)):
                small_v[rows, :] += jnp.where(lane == 10 + j, piece, 0.0)
    else:
        stores = [begin(sems, len(pairs), out_ref, done_hbm)]
        q_done_ref[...] = q_column
        v_done_ref[...] = v_column
    gain, bias = gain_ref[...].astype(F32), bias_ref[...].astype(F32)
    for step in range(2 * half // ROW_STEP):
        at = slice(step * ROW_STEP, (step + 1) * ROW_STEP)
        out = mm(near_v[at, :], out_ref[...], NT)
        out = jnp.concatenate([out[:, :part], out[:, part:] + mm(far_v[at, :], grad_v[...], NT)], 1)
        columns = ln_columns(out, w_ref[at, own_at:].astype(F32), sums, gain[:, at], bias[:, at], 0)
        if last:
            deal_part(bits_ref[0], jnp.concatenate([out, small_v[at, :] + columns], 1), send_part, keep_part, step)
            continue
        small_ref[at, :] = early_ref[at, :] + columns

        def join(proj):
            deal_part(bits_ref[1], jnp.concatenate([out, proj], 1), send_part, keep_part, step)

        early, late = grad_half_v[:block, :], grad_half_v[block:, :]

        @pl.when(core == step)
        def _():
            join(mm(whole_ot[:, :block], early) + mm(whole_ot[:, block:], late))

        @pl.when(core != step)
        def _():
            join(mm(got_v[:block, :], late, TN) + mm(got_v[block:, :], early, TN))

    for store in stores:
        store.wait()


def near_back(after, unit, first, last, bits, small, held):
    code, lse, do, far_sums, gain, bias, early = small[:7]
    qt, kv, w = held[0], held[1], held[4]
    half, queries = qt.shape
    keys, width = kv.shape
    heads = half // HEAD_DIM - first if last else 4
    part = heads * HEAD_DIM
    grad = ((3 * part, keys), BF16)
    dx = ((width, keys // 2), F32)
    if last:
        outs = (((width, keys // 2), BF16), *dealt(width, 2 * unit, 3 * part + 128)[0], dx)
        hold = (False, False, False, True)
    else:
        column = ((part, 128), F32)
        outs = (*dealt(width, 4 * unit, 3 * part + half)[0], ((width, 128), F32), column, column, grad)
        hold = (False, False, True, True, True, True)
    scratch = back_scratch(heads, queries, keys) + [
        pltpu.VMEM((part, queries), F32),
        pltpu.VMEM(*grad),
        pltpu.VMEM((width, queries), BF16),
        pltpu.VMEM((width, queries), BF16),
        pltpu.VMEM((2 * part, keys), BF16),
        pltpu.VMEM((width, 3 * half if last else 3 * part), BF16),
        pltpu.SemaphoreType.DMA((17,)),
    ]
    if last:
        scratch += [pltpu.VMEM(held[-1].shape, BF16), pltpu.VMEM(*dx), pltpu.VMEM((width, 128), F32)]
    else:
        scratch += [pltpu.VMEM(held[-2].shape, BF16), pltpu.VMEM(held[-1].shape, BF16), pltpu.VMEM((half, queries), BF16)]
    specs = [VMEM] * len(small) + [HBM] * len(held)
    out_specs = (VMEM,) * (len(outs) - 1) + (HBM,)
    kernel = partial(near_back_kernel, first=first, heads=heads, unit=unit, last=last)
    name = "near_backward_last" if last else "near_backward_first"
    run = call(kernel, name, outs, scratch, specs, out_specs, prefetch=1, after=after, hold=hold)
    return run(bits, *small, *held)


def keep_column(code_ref, flags_ref, branch, images):
    code = jnp.minimum(code_ref[0:1, :], float(PAD_CLASS - 1))
    kept = jnp.zeros_like(code)
    for image in range(images):
        kept = kept + jnp.where(code == image, flags_ref[branch, image].astype(F32), 0.0)
    return jnp.broadcast_to(kept / keep_rate, (128, code.shape[1])).T[:, :1]


def gelu_both(hidden):
    size = jnp.abs(hidden)
    bell = jnp.exp(-0.5 * hidden * hidden)
    t = 1.0 / (1.0 + 0.23164189 * size)
    tail = ((((0.5307027145 * t - 0.7265760135) * t + 0.7107068705) * t - 0.142248368) * t + 0.127414796) * t * bell
    cdf = jnp.where(hidden >= 0, 1.0 - tail, tail)
    return hidden * cdf, cdf + hidden * (bell * 0.3989422804014327)


def row_tiles(rows):
    for start in range(0, rows, TILE):
        other = (start + rows // 2) % rows
        yield slice(start, start + TILE), slice(other, other + TILE)


def mlp_kernel(
    bits_ref,
    flags_ref,
    b_proj_ref,
    gain_ref,
    bias_ref,
    b_up_ref,
    code_hbm,
    own_hbm,
    got_hbm,
    mine_hbm,
    other_hbm,
    cot_mine_hbm,
    cot_other_hbm,
    w_proj_hbm,
    w_up_hbm,
    w_down_hbm,
    part_ref,
    down_other_ref,
    small_ref,
    send_down_hbm,
    keep_down_hbm,
    send_up_hbm,
    keep_up_hbm,
    middle_hbm,
    down_hbm,
    send_down,
    keep_down,
    send_up,
    keep_up,
    x_v,
    cot_v,
    w_proj_v,
    w_up_v,
    w_down_v,
    middle_v,
    normed_v,
    grad_down_v,
    active_v,
    grad_hidden_v,
    down_v,
    up_sums_v,
    code_ref,
    own_ref,
    got_ref,
    sems,
    *,
    images,
    unit,
):
    core = bits_ref[2]
    rows, width = x_v.shape
    block, half, units = rows // 2, width // 2, w_up_v.shape[1]
    mine_at, other_at = pl.multiple_of(core * half, 128), pl.multiple_of((1 - core) * half, 128)
    units_at = pl.multiple_of(core * units, 128)
    pairs = (
        (w_proj_hbm.at[pl.ds(mine_at, half), :], w_proj_v.at[:half, :]),
        (w_proj_hbm.at[pl.ds(other_at, half), :], w_proj_v.at[half:, :]),
        (mine_hbm, x_v.at[:block, :]),
        (other_hbm.at[:block, :], x_v.at[block:, :]),
        (cot_mine_hbm, cot_v.at[:block, :]),
        (cot_other_hbm, cot_v.at[block:, :]),
        (code_hbm, code_ref),
        (own_hbm, own_ref),
        (got_hbm, got_ref),
        (w_up_hbm.at[:, pl.ds(units_at, units)], w_up_v),
        (w_down_hbm.at[pl.ds(units_at, units), :], w_down_v),
    )
    loads = [begin(sems, i, source, target) for i, (source, target) in enumerate(pairs)]
    for load in loads[:9]:
        load.wait()
    gain, bias, b_proj = gain_ref[...].astype(F32), bias_ref[...].astype(F32), b_proj_ref[...].astype(F32)
    down_sums = jnp.zeros((1, width), F32)
    for at, swapped in row_tiles(rows):
        keep_attn = keep_column(code_ref.at[:, at], flags_ref, 0, images)
        keep_mlp = keep_column(code_ref.at[:, at], flags_ref, 1, images)
        branch = mm(own_ref[at, :], w_proj_v[:half, :]) + mm(got_ref[swapped, :], w_proj_v[half:, :]) + b_proj
        middle = x_v[at, :].astype(F32) + keep_attn * branch
        middle_v[at, :] = middle
        normed_v[at, :] = (centre(middle)[0] * gain + bias).astype(BF16)
        grad_down = (keep_mlp * cot_v[at, :].astype(F32)).astype(BF16)
        grad_down_v[at, :] = grad_down
        if at.start < block:
            down_sums = down_sums + jnp.sum(grad_down.astype(F32), 0, keepdims=True)
    stores = [begin(sems, 11, middle_v, middle_hbm)]
    for load in loads[9:]:
        load.wait()
    up_sums_v[...] = jnp.zeros_like(up_sums_v)
    chunk = 512

    def tile(index, carry):
        at = pl.ds(pl.multiple_of(index * TILE, TILE), TILE)
        for start in range(0, units, chunk):
            cols = slice(start, start + chunk)
            hidden = mm(normed_v[at, :], w_up_v[:, cols]) + b_up_ref[:, cols].astype(F32)
            active, slope = gelu_both(hidden)
            active_v[at, cols] = active.astype(BF16)
            grad_hidden = (mm(grad_down_v[at, :], w_down_v[cols, :], NT) * slope).astype(BF16)
            grad_hidden_v[at, cols] = grad_hidden
            up_sums_v[:, cols] += jnp.sum(grad_hidden.astype(F32), 0, keepdims=True)
        return carry

    lax.fori_loop(0, rows // TILE, tile, 0)
    for step in range(units // ROW_STEP):
        at = slice(step * ROW_STEP, (step + 1) * ROW_STEP)
        deal_part(bits_ref[0], mm(active_v[:, at], grad_down_v[...], TN), send_down, keep_down, step)
    stores += [begin(sems, 13, send_down, send_down_hbm), begin(sems, 14, keep_down, keep_down_hbm)]
    for at, _ in row_tiles(rows):
        down = mm(active_v[at, :], w_down_v[...]).astype(BF16)
        if at.start < block:
            down_v[at, :] = down
        else:
            down_other_ref[at.start - block : at.stop - block, :] = down
    stores.append(begin(sems, 12, down_v, down_hbm))
    for step in range(width // ROW_STEP):
        at = slice(step * ROW_STEP, (step + 1) * ROW_STEP)
        out = mm(normed_v[:, at], grad_hidden_v[...], TN)
        deal_part(bits_ref[1], out, send_up, keep_up, step)
        columns = ln_columns(out, w_up_v[at, :].astype(F32), up_sums_v[...], gain[:, at], bias[:, at], 2)
        small_ref[at, :] = columns + jnp.where(lane_of(columns.shape) == 5, upright(down_sums[:, at]), 0.0)
    stores += [begin(sems, 15, send_up, send_up_hbm), begin(sems, 16, keep_up, keep_up_hbm)]
    for at, _ in row_tiles(rows):
        part_ref[at, :] = mm(grad_hidden_v[at, :], w_up_v[...], NT).astype(BF16)
    lane = lane_of((half, 128))
    own = pl.ds(pl.multiple_of(core * half, 8), half)
    for j, column in enumerate(interleaved(upright(up_sums_v[...]), unit, units // half)):
        small_ref[own, :] += jnp.where(lane == 6 + j, column, 0.0)
    for store in stores:
        store.wait()


def mlp(unit, bits, flags, b_proj, gain, bias, b_up, code, own, got, mine, other, cot_mine, cot_other, w_proj, w_up, w_down):
    rows, half = own.shape
    width, units = 2 * half, w_up.shape[1] // 2
    specs = [SMEM] + [VMEM] * 3 + [pl.BlockSpec((1, units), lambda i, b: (0, b[2]))] + [HBM] * 10
    wide, tall = ((rows, width), BF16), ((rows, units), BF16)
    block = ((rows // 2, width), BF16)
    parts = [*dealt(units, 2 * units // (width // unit // 2), width)[0], *dealt(width, 4 * unit, units)[0]]
    outs = (wide, block, ((width, 128), F32), *parts, ((rows, width), F32), block)
    scratch = [pltpu.VMEM(*shape) for shape in parts] + [
        pltpu.VMEM(*wide),
        pltpu.VMEM(*wide),
        pltpu.VMEM((width, width), BF16),
        pltpu.VMEM((width, units), BF16),
        pltpu.VMEM((units, width), BF16),
        pltpu.VMEM((rows, width), F32),
        pltpu.VMEM(*wide),
        pltpu.VMEM(*wide),
        pltpu.VMEM(*tall),
        pltpu.VMEM(*tall),
        pltpu.VMEM(*block),
        pltpu.VMEM((1, units), F32),
        pltpu.VMEM(code.shape, F32),
        pltpu.VMEM((rows, half), BF16),
        pltpu.VMEM((rows, half), BF16),
        pltpu.SemaphoreType.DMA((17,)),
    ]
    out_specs = (VMEM,) * 3 + (HBM,) * 6
    hold = (True,) * 9
    kernel = partial(mlp_kernel, images=flags.shape[1], unit=unit)
    run = call(kernel, "mlp", outs, scratch, specs, out_specs, prefetch=1, hold=hold)
    return run(
        bits, flags, b_proj, gain, bias, b_up, code, own, got, mine, other, cot_mine, cot_other, w_proj, w_up, w_down
    )


def deal(bit, rows, send_ref, keep_ref):
    run = send_ref.shape[1]
    for i in range(send_ref.shape[0]):
        low, high = rows[2 * i * run : (2 * i + 1) * run], rows[(2 * i + 1) * run : (2 * i + 2) * run]
        send_ref[i] = jnp.where(bit == 0, high, low).astype(BF16)
        keep_ref[i] = jnp.where(bit == 0, low, high).astype(BF16)


def deal_part(bit, rows, send_ref, keep_ref, step):
    count = rows.shape[0] // (2 * send_ref.shape[1])
    part = pl.ds(step * count, count)
    deal(bit, rows, send_ref.at[part], keep_ref.at[part])


def dealt(height, run, width):
    shape = (height // (2 * run), run, width)
    count = ROW_STEP // (2 * run)
    return [(shape, BF16)] * 2, [pl.BlockSpec((count, run, width), lambda i, *_: (i, 0, 0))] * 2


def upright(row):
    return jnp.broadcast_to(row, (128, row.shape[1])).T


def lane_of(shape):
    return lax.broadcasted_iota(jnp.int32, shape, 1)


def interleaved(column, unit, parts):
    blocks = column.shape[0] // (unit * parts)
    out = []
    for j in range(parts):
        pieces = [column[(k * parts + j) * unit : (k * parts + j + 1) * unit] for k in range(blocks)]
        out.append(jnp.concatenate(pieces, 0))
    return out


def ln_columns(grad, weight, sums, gain_ref, bias_ref, place):
    first = jnp.sum(weight * grad, 1, keepdims=True)
    second = jnp.sum(weight * sums, 1, keepdims=True)
    lane = lane_of((weight.shape[0], 128))
    scaled = (first - upright(bias_ref) * second) / upright(gain_ref)
    return jnp.where(lane == place, scaled, jnp.where(lane == place + 1, second, 0.0))


def add_kernel(left_ref, right_ref, out_ref):
    out_ref[...] = (left_ref[...].astype(F32) + right_ref[...].astype(F32)).astype(out_ref.dtype)


def add(after, left, right):
    run = call(add_kernel, "add_blocks", ((left.shape, BF16),), [], [VMEM, VMEM], after=after)
    return run(left, right)[0]


def sides(core_ref, kept, other):
    return jnp.where(core_ref[0] == 0, kept, other), jnp.where(core_ref[0] == 0, other, kept)


def join_up_kernel(core_ref, kept_ref, other_ref, down_ref, out_ref, down_out_ref):
    units = kept_ref.shape[1]
    down_out_ref[...] = down_ref[...].astype(F32)
    out_ref[:, :units], out_ref[:, units:] = sides(core_ref, kept_ref[...], other_ref[...])


def join_up(after, core, kept, other, down):
    rows, units = kept.shape
    outs = (((rows, 2 * units), F32), (down.shape, F32))
    return call(join_up_kernel, "join_up", outs, [], [VMEM] * 3, prefetch=1, after=after)(core, kept, other, down)


def join_kernel(core_ref, two_ref, two_other_ref, one_ref, one_other_ref, qkv_ref, proj_ref, *refs):
    rows, half = two_ref.shape[0], proj_ref.shape[1] // 2
    pad = refs[-1]
    big = (two_ref.shape[1] - half) // 3
    small = half - big
    twos = sides(core_ref, two_ref[...], two_other_ref[...])
    ones = sides(core_ref, one_ref[...], one_other_ref[...])
    for core, (two, one) in enumerate(zip(twos, ones)):
        proj_ref[:, core * half : (core + 1) * half] = two[:, 3 * big :]
        for i in range(3):
            at = 2 * i * half + core * half
            qkv_ref[:, at : at + big] = two[:, i * big : (i + 1) * big]
            qkv_ref[:, at + big : at + half] = one[:, i * small : (i + 1) * small]
    pad[...] = jnp.zeros_like(pad)
    pad[:rows, :] = one_ref[:, 3 * small :] + one_other_ref[:, 3 * small :]
    turned = pad[...].T
    lane = 0
    for ref in refs[:-1]:
        count = ref.shape[1] // rows
        ref[...] = jnp.concatenate([turned[lane + i : lane + i + 1, :rows] for i in range(count)], 1)
        lane += count


def join_all(after, core, two, two_other, one, one_other, half):
    rows = two.shape[0]
    outs = [((rows, 6 * half), F32), ((rows, 2 * half), F32)] + [((1, count * rows), F32) for count in (1, 1, 1, 1, 1, 1, 4, 2)]
    scratch = [pltpu.VMEM((128, 128), F32)]
    run = call(join_kernel, "join_all", outs, scratch, [VMEM] * 4, prefetch=1, after=after)
    return run(core, two, two_other, one, one_other)


def finish_kernel(x_ref, dx_ref, beside_ref, across_ref, gain_ref, middle_ref, out_ref):
    unit, scale = centre(x_ref[...].astype(F32))
    grad = (dx_ref[...] + beside_ref[...].astype(F32) + across_ref[...].astype(F32)).T
    out_ref[...] = (middle_ref[...] + norm_back(unit, scale, grad * gain_ref[...].astype(F32))).astype(BF16)


def finish(after, x, dx, beside, across, gain, middle):
    rows, width = x.shape
    tile = pl.BlockSpec((TILE, width), lambda i: (i, 0))
    one = pl.BlockSpec((1, width), lambda i: (0, 0))
    turned = pl.BlockSpec((width, TILE), lambda i: (0, i))
    specs = [tile, turned, turned, turned, one, tile]
    run = call(finish_kernel, "token_gradient", ((x.shape, BF16),), [], specs, (tile,), (rows // TILE,), after=after)
    return run(x, dx, beside, across, gain, middle)[0]


def output_kernel(flags_ref, code_ref, middle_ref, down_ref, got_ref, bias_ref, out_ref, *, images):
    kept = keep_column(code_ref, flags_ref, 1, images)
    branch = down_ref[...].astype(F32) + got_ref[...].astype(F32) + bias_ref[...].astype(F32)
    out_ref[...] = (middle_ref[...] + kept * branch).astype(BF16)


def layer_out(after, flags, code, middle, down, got, bias):
    rows, width = got.shape
    tile = pl.BlockSpec((TILE, width), lambda i: (i, 0))
    one = pl.BlockSpec((1, width), lambda i: (0, 0))
    specs = [SMEM, pl.BlockSpec((8, TILE), lambda i: (0, i)), tile, tile, tile, one]
    kernel = partial(output_kernel, images=flags.shape[1])
    run = call(kernel, "layer_output", ((got.shape, BF16),), [], specs, (tile,), (rows // TILE,), after=after)
    return run(flags, code, middle, down, got, bias)[0]


def swap_halves(rows):
    half = rows.shape[0] // 2
    return jnp.concatenate([rows[half:], rows[:half]], 0)


def pick(array, index, dim):
    return lax.dynamic_index_in_dim(array, index, dim, keepdims=False)


class Links:
    def __init__(self, mesh):
        self.dp, self.blk = mesh.shape["dp"], mesh.shape["blk"]
        self.bits = self.dp.bit_length() - 1

    def core(self, value):
        return lax.ppermute(value, "blk", [(i, i ^ 1) for i in range(self.blk)])

    def side(self, value):
        return lax.ppermute(value, "blk", [(i, i ^ 2) for i in range(self.blk)])

    def cross(self, value, step):
        if step == "x":
            return self.side(value)
        return lax.ppermute(value, "dp", [(i, i ^ (1 << step)) for i in range(self.dp)])

    def bit(self, step):
        if step == "x":
            return lax.axis_index("blk") // 2
        return (lax.axis_index("dp") >> step) & 1

    def swap(self, value):
        top = self.dp // 2
        pairs = []
        for d in range(self.dp):
            for b in range(self.blk):
                high, core = d // top, b % 2
                pairs.append((d * self.blk + b, (d % top + core * top) * self.blk + (b - core + high)))
        return lax.ppermute(value, ("dp", "blk"), pairs)


class Portion:
    def __init__(self, links, send, keep, dims, order, by_core=True):
        self.links, self.order, self.by_core = links, list(order), by_core
        self.dims = [dim for dim in dims if dim != order[0]]
        self.tail = (send.shape[0] * send.shape[1] // 2 ** len(self.dims), send.shape[2])
        self.kept = keep
        self.arrived = links.cross(send, order[0])

    def advance(self, after):
        links = self.links
        self.order.pop(0)
        if not self.order:
            kept, arrived = self.kept.reshape(self.tail), self.arrived.reshape(self.tail)
            if not self.by_core:
                self.total = call(add_kernel, "sum_last", ((self.tail, F32),), [], [VMEM] * 2, after=after)(kept, arrived)[0]
                return self.total
            half = self.tail[0] // 2

            def last_kernel(core_ref, kept_ref, arrived_ref, send_ref, keep_ref):
                total = kept_ref[...].astype(F32) + arrived_ref[...].astype(F32)
                send_ref[...] = jnp.where(core_ref[0] == 0, total[half:], total[:half])
                keep_ref[...] = jnp.where(core_ref[0] == 0, total[:half], total[half:])

            shape = (half, self.tail[1])
            core = (lax.axis_index("blk") % 2).reshape(1).astype(jnp.int32)
            run = call(last_kernel, "sum_last", ((shape, F32), (shape, F32)), [], [VMEM] * 2, prefetch=1, after=after)
            send, self.total = run(core, kept, arrived)
            self.other = links.core(send)
            return self.total
        follow = self.order[0]
        spot = self.dims.index(follow)
        self.dims.pop(spot)
        outer, inner = 2**spot, 2 ** (len(self.dims) - spot)
        shape = (outer, inner) + self.tail
        view = (outer, 2, inner) + self.tail

        def kernel(bit_ref, kept_ref, arrived_ref, send_ref, keep_ref):
            for out_ref, where in ((send_ref, 1 - bit_ref[0]), (keep_ref, bit_ref[0])):
                out_ref[...] = (kept_ref[:, where].astype(F32) + arrived_ref[:, where].astype(F32)).astype(BF16)

        run = call(kernel, "sum_half", ((shape, BF16), (shape, BF16)), [], [VMEM] * 2, prefetch=1, after=after)
        send, keep = run(links.bit(follow).reshape(1).astype(jnp.int32), self.kept.reshape(view), self.arrived.reshape(view))
        self.kept = keep
        self.arrived = links.cross(send, follow)
        return keep


def merged(links, down, up, after):
    count, rb, width = 2 ** len(down.dims), down.tail[0], down.tail[1]
    double, units = up.tail
    high = count // 2
    top = high // 2

    def kernel(bit_ref, down_ref, down_got_ref, up_ref, up_got_ref, send_ref, keep_ref):
        for out_ref, where in ((send_ref, 1 - bit_ref[0]), (keep_ref, bit_ref[0])):
            for i in range(high):
                at = ((i % top) * 2 + where) * 2 + i // top
                out_ref[i, :rb] = (down_ref[at].astype(F32) + down_got_ref[at].astype(F32)).astype(BF16)
                total = (up_ref[2 * i + where].astype(F32) + up_got_ref[2 * i + where].astype(F32)).astype(BF16)
                for part in range(units // width):
                    start = rb + part * double
                    out_ref[i, start : start + double] = total[:, part * width : (part + 1) * width]

    shape = (high, rb + double * (units // width), width)
    bit = links.bit(1).reshape(1).astype(jnp.int32)
    run = call(kernel, "sum_both", ((shape, BF16), (shape, BF16)), [], [VMEM] * 4, prefetch=1, after=after)
    fold = (count, rb, width), (count, double, units)
    return run(
        bit, down.kept.reshape(fold[0]), down.arrived.reshape(fold[0]), up.kept.reshape(fold[1]), up.arrived.reshape(fold[1])
    )


def parted(after, core, kept, arrived, rb, unit, units):
    width = kept.shape[1]

    def kernel(core_ref, kept_ref, arrived_ref, down_ref, send_ref, keep_ref):
        total = kept_ref[...].astype(F32) + arrived_ref[...].astype(F32)
        down_ref[...] = total[:rb].astype(BF16)
        for part in range(units // width):
            start = rb + part * 2 * unit
            low, high = total[start : start + unit], total[start + unit : start + 2 * unit]
            cols = slice(part * width, (part + 1) * width)
            send_ref[:, cols] = jnp.where(core_ref[0] == 0, high, low)
            keep_ref[:, cols] = jnp.where(core_ref[0] == 0, low, high)

    outs = (((rb, width), BF16), ((unit, units), F32), ((unit, units), F32))
    return call(kernel, "part_both", outs, [], [VMEM] * 2, prefetch=1, after=after)(core, kept, arrived)


def local(
    links,
    tokens,
    cotangent,
    segments,
    padding,
    drop_keep,
    ln1_gain,
    ln1_bias,
    qkv_weight,
    qv_bias,
    proj_weight,
    proj_bias,
    ln2_gain,
    ln2_bias,
    fc1_weight,
    fc1_bias,
    fc2_weight,
    fc2_bias,
):
    _, block, width = tokens.shape
    half = width // 2
    units = fc1_weight.shape[1] // 2
    core = lax.axis_index("blk") % 2
    core_arg = core.reshape(1).astype(jnp.int32)
    owners = links.dp * links.blk
    rows = 2 * block

    code = jnp.where(padding == 1, segments, PAD_CLASS).astype(BF16)
    mine = jnp.concatenate([tokens[0], jnp.pad(code, ((0, 15), (0, width - block)))], 0)
    far = links.side(mine)
    other = links.core(mine)
    cot_mine = cotangent[0]
    cot_other = links.core(cot_mine)
    flags = drop_keep[:, 0, :]
    bits = links.bits
    low = [bits - 1 - i for i in range(bits)]
    chip = low + ["x"]
    by_core = low[1:] + ["x", low[0]]
    tail = [s for s in low if s > 1][::-1]
    side_bits = jnp.stack([links.bit("x"), links.bit(0), core, links.bit(1)]).astype(jnp.int32)
    unit = width // owners

    gain_one, bias_one = ln1_gain.reshape(1, -1), ln1_bias.reshape(1, -1)
    gain_two, bias_two = ln2_gain.reshape(1, -1), ln2_bias.reshape(1, -1)
    bias_qv = qv_bias.reshape(1, -1)
    near_code, near_normed, w_qkv, qt, near_kv, state = forward_near(
        core_arg, mine, other, gain_one, bias_one, qkv_weight, bias_qv
    )
    far = lax.dynamic_update_slice(far, near_code[:, :128].astype(BF16), (block + 8, 0))
    far_other = links.core(far)
    bias_v = lax.dynamic_slice(bias_qv, (0, width + core * half), (1, half))
    far_code, lse, own, far_normed, far_kv, ot = forward_far(
        far, far_other, gain_one, bias_one, w_qkv, bias_v, qt, near_code, state
    )
    got = links.core(own)
    part, down_send, small, send_down, keep_down, send_up, keep_up, middle, down = mlp(
        unit,
        side_bits,
        flags,
        proj_bias.reshape(1, -1),
        gain_two,
        bias_two,
        fc1_bias.reshape(1, -1),
        near_code,
        own,
        got,
        tokens[0],
        other,
        cot_mine,
        cot_other,
        proj_weight,
        fc1_weight,
        fc2_weight,
    )
    got_part = links.core(part)
    down_portion = Portion(links, send_down, keep_down, by_core, ["x", 0, 1] + tail, False)
    up_portion = Portion(links, send_up, keep_up, chip, [0, "x", 1] + tail)
    down_other = links.core(down_send)
    held = (middle, cot_mine, cot_other, proj_weight, qt, far_kv, ot, w_qkv)
    far_dx, far_send, far_sums, small, do, grad_half, grad_middle, dq, far_grad = far_back(
        (), core_arg, flags, near_code, far_code, lse, part, got_part, gain_two, small, held
    )
    last = down_portion.advance((far_grad,))
    last = up_portion.advance((last,))
    far_got = links.core(far_send)
    ready = (near_code, lse, do, far_sums, gain_one, bias_one)
    held = (qt, near_kv, ot, dq, w_qkv, near_normed, far_normed, far_grad)
    send, keep, small, q_done, v_done, done = near_back(
        (last,), unit, 0, False, side_bits, ready + (small,), held + (got, grad_half)
    )
    two_portion = Portion(links, send, keep, chip, [0, 1, "x"] + tail)
    far_sum = add((keep,), far_dx, far_got)
    across = links.side(far_sum)
    send, keep = merged(links, down_portion, up_portion, (far_sum,))
    both_portion = Portion(links, send, keep, low[:-1], [1] + tail)
    near_send, send, keep, near_dx = near_back(
        (keep,), unit, 4, True, side_bits, ready + (small, q_done, v_done), held + (done,)
    )
    near_got = links.core(near_send)
    one_portion = Portion(links, send, keep, chip, ["x", 0, 1] + tail)
    last = both_portion.advance((keep,))
    last = two_portion.advance((last, across))
    layer_output = layer_out((last,), flags, near_code, middle, down, down_other, fc2_bias.reshape(1, -1))
    last = one_portion.advance((layer_output,))
    last = two_portion.advance((last,))
    for _ in tail[1:]:
        last = both_portion.advance((last,))
    last = one_portion.advance((last, both_portion.arrived))
    tokens_grad = finish((last,), tokens[0], near_dx, near_got, across, gain_one, grad_middle)
    last = two_portion.advance((tokens_grad,))
    last = one_portion.advance((last,))
    down_total, send, keep = parted(
        (last,),
        core_arg,
        both_portion.kept.reshape(both_portion.tail),
        both_portion.arrived.reshape(both_portion.tail),
        2 * units // owners,
        unit,
        units,
    )
    down_got = links.swap(down_total)
    up_got = links.core(send)
    last = down_total
    while two_portion.order:
        last = two_portion.advance((last,))
    while one_portion.order:
        last = one_portion.advance((last,))
    up_grad, down_grad = join_up((last,), core_arg, keep, up_got, down_got)
    qkv_grad, proj_grad, *vectors = join_all(
        (up_grad,), core_arg, two_portion.total, two_portion.other, one_portion.total, one_portion.other, half
    )
    g1, b1, g2, b2, pb, d2, u1, qvb = (vector.reshape(-1) for vector in vectors)
    shape = tokens.shape
    return (
        layer_output.reshape(shape),
        tokens_grad.reshape(shape),
        g1,
        b1,
        qkv_grad,
        qvb,
        proj_grad,
        pb,
        g2,
        b2,
        up_grad,
        u1,
        down_grad,
        d2,
    )


def solution(mesh):
    both = P(("dp", "blk"))
    rows = P(("dp", "blk"), None)
    token = P("dp", "blk", None)
    placed = (token, token, P("dp", "blk"), P("dp", "blk"), P(None, "dp", None)) + (P(),) * 12
    return jax.shard_map(
        partial(local, Links(mesh)),
        mesh=mesh,
        in_specs=placed,
        out_specs=(token, token, both, both, rows, both, rows, both, both, both, rows, both, rows, both),
        check_vma=False,
    )
```

```python
from functools import partial

import jax
import jax.numpy as jnp
from jax import lax
from jax.experimental import pallas as pl
from jax.experimental.pallas import tpu as pltpu
from jax.sharding import PartitionSpec as P

HEAD_DIM = 64
F32 = jnp.float32
BF16 = jnp.bfloat16
epsilon = 1e-06
keep_rate = 0.9
attn_scale = 0.125
negative = -1e30
PAD_CLASS = 4
TILE = 256
MIB = 2**20
FLOPS_PER_US = 1.0 * 10**9
BUDGET = {
    "near_forward": (28, 16),
    "far_forward": (28, 13),
    "mlp": (44, 30),
    "far_backward": (42, 20),
    "near_backward_first": (36, 19),
    "near_backward_last": (36, 13),
    "join_up": (8, 1),
    "sum_both": (12, 2),
    "part_both": (8, 1),
    "join_all": (8, 1),
    "sum_half": (8, 2),
    "sum_last": (8, 1),
    "add_blocks": (8, 2),
    "token_gradient": (12, 2),
    "layer_output": (12, 2),
}
NN = ((1,), (0,))
NT = ((1,), (1,))
TN = ((0,), (0,))
VMEM = pl.BlockSpec(memory_space=pltpu.VMEM)
SMEM = pl.BlockSpec(memory_space=pltpu.SMEM)
HBM = pl.BlockSpec(memory_space=pltpu.HBM)
ROW_STEP = 384


def mm(left, right, dims=NN):
    return lax.dot_general(left, right, (dims, ((), ())), preferred_element_type=F32)


def rows_of(head):
    return slice(head * HEAD_DIM, (head + 1) * HEAD_DIM)


def lanes_of(pair):
    return slice(pair * 128, (pair + 1) * 128)


def centre(values):
    shifted = values - jnp.mean(values, -1, keepdims=True)
    spread = jnp.mean(shifted * shifted, -1, keepdims=True)
    scale = lax.rsqrt(spread + epsilon)
    return shifted * scale, scale


def norm_back(unit, scale, grad):
    return (grad - jnp.mean(grad, -1, keepdims=True) - unit * jnp.mean(grad * unit, -1, keepdims=True)) * scale


def call(kernel, name, outs, scratch, specs, out_specs=None, grid=None, prefetch=0, after=(), pin=(), hold=()):
    limit, cost = BUDGET[name]
    out_specs = out_specs or tuple(VMEM for _ in outs)
    first = prefetch + len(specs)

    def ordered(*refs):
        kernel(*refs[:first], *refs[first + len(after) :])

    spec = pltpu.PrefetchScalarGridSpec(
        num_scalar_prefetch=prefetch,
        grid=grid or (1,),
        in_specs=list(specs) + [pl.BlockSpec(memory_space=pl.ANY)] * len(after),
        out_specs=out_specs,
        scratch_shapes=scratch,
    )
    run = pl.pallas_call(
        ordered,
        out_shape=tuple(
            (pltpu.HBM if pinned else jax.ShapeDtypeStruct)(shape, kind)
            for (shape, kind), pinned in zip(outs, hold if hold else [spec is HBM for spec in out_specs])
        ),
        grid_spec=spec,
        compiler_params=pltpu.CompilerParams(vmem_limit_bytes=limit * MIB),
        cost_estimate=pl.CostEstimate(flops=int(cost * FLOPS_PER_US), bytes_accessed=1, transcendentals=0),
        name=name,
    )

    def place(*args):
        held = list(args)
        for i, spec in enumerate(specs):
            if spec is HBM or i in pin:
                held[prefetch + i] = pltpu.with_memory_space_constraint(held[prefetch + i], pltpu.HBM)
        return run(*held, *after)

    return place


def query_mask(code):
    kind = lax.broadcasted_iota(jnp.int32, (HEAD_DIM, code.shape[1]), 0).astype(F32)
    seen = (code == kind) | ((code == PAD_CLASS) & (kind == PAD_CLASS - 1)) | (kind > PAD_CLASS)
    return jnp.where(seen, 0.0, negative).astype(BF16)


def load_queries(qt_ref, code, qx, heads):
    mask = query_mask(code)
    for h in range(heads):
        own = slice(0, HEAD_DIM) if h % 2 == 0 else slice(HEAD_DIM, 128)
        rest = slice(HEAD_DIM, 128) if h % 2 == 0 else slice(0, HEAD_DIM)
        qx[h, own, :] = qt_ref[rows_of(h), :]
        qx[h, rest, :] = mask


def load_keys(k_ref, first, code, kx, heads):
    keys = k_ref.shape[0]
    kind = lax.broadcasted_iota(jnp.int32, (128, keys), 0).astype(F32)
    low = (kind == code).astype(F32).T.astype(BF16)
    high = (kind - HEAD_DIM == code).astype(F32).T.astype(BF16)
    lane = lax.broadcasted_iota(jnp.int32, (keys, 128), 1)
    for pair in range(heads // 2):
        slab = k_ref[:, first + pair * 128 : first + (pair + 1) * 128]
        kx[2 * pair] = jnp.where(lane < HEAD_DIM, slab, high)
        kx[2 * pair + 1] = jnp.where(lane < HEAD_DIM, low, slab)


def note_tiles(q_code, k_code, act):
    def ranges(code):
        image = jnp.minimum(code, float(PAD_CLASS - 1))
        cuts = [image[:, i : i + TILE // 2] for i in range(0, code.shape[1], TILE // 2)]
        return [(jnp.min(c), jnp.max(c)) for c in cuts]

    q_ranges = ranges(q_code)
    k_ranges = q_ranges if k_code is q_code else ranges(k_code)

    def meet(i, j):
        return (q_ranges[i][0] <= k_ranges[j][1]) & (q_ranges[i][1] >= k_ranges[j][0])

    for i in range(len(q_ranges) // 2):
        for j in range(len(k_ranges) // 2):
            four = [[meet(2 * i + u, 2 * j + v) for v in range(2)] for u in range(2)]
            queries = [four[u][0] | four[u][1] for u in range(2)]
            keys = [four[0][v] | four[1][v] for v in range(2)]
            keys = keys[0].astype(jnp.int32) + 2 * keys[1].astype(jnp.int32)
            queries = queries[0].astype(jnp.int32) + 2 * queries[1].astype(jnp.int32)
            act[i, j] = jnp.where((keys == 3) & (queries < 3), 3 + queries, keys)


def each_tile(act, queries, keys, body):
    across = keys // TILE
    half = TILE // 2

    def step(index, carry):
        q_tile, k_tile = index // across, index % across
        kind = act[q_tile, k_tile]
        q_start, k_start = q_tile * TILE, k_tile * TILE

        def span(start, size):
            return pl.ds(pl.multiple_of(start, half), size)

        @pl.when(kind == 3)
        def _():
            body(span(q_start, TILE), span(k_start, TILE))

        @pl.when((kind == 1) | (kind == 2))
        def _():
            body(span(q_start, TILE), span(k_start + (kind - 1) * half, half))

        @pl.when(kind > 3)
        def _():
            body(span(q_start + (kind - 4) * half, half), span(k_start, TILE))

        return carry

    lax.fori_loop(0, (queries // TILE) * across, step, 0)


def fold_keys(act, kx, qx, vt, top, total, acc, heads):
    def body(at, span):
        hs = range(heads)
        scores = [mm(kx[h, span, :], qx[h, :, at]) for h in hs]
        old = [top[h : h + 1, at] for h in hs]
        new = [jnp.maximum(old[h], jnp.max(scores[h], 0, keepdims=True)) for h in hs]
        decay = [jnp.exp(old[h] - new[h]) for h in hs]
        weights = [jnp.exp(scores[h] - new[h]) for h in hs]
        added = [mm(vt[rows_of(h), span], weights[h].astype(BF16)) for h in hs]
        for h in hs:
            top[h : h + 1, at] = new[h]
            total[h : h + 1, at] = decay[h] * total[h : h + 1, at] + jnp.sum(weights[h], 0, keepdims=True)
            acc[rows_of(h), at] = decay[h] * acc[rows_of(h), at] + added[h]

    each_tile(act, qx.shape[2], kx.shape[1], body)


def normed_rows(ref, at, gain, bias):
    return (centre(ref[at, :].astype(F32))[0] * gain + bias).astype(BF16)


def begin(sems, index, source, target):
    copy = pltpu.make_async_copy(source, target, sems.at[index])
    copy.start()
    return copy


def load_tokens(refs, code_ref):
    block = refs[0].shape[0] - 16
    for index, ref in enumerate(refs):
        row = ref[block : block + 16, :block].astype(F32)[:1]
        code_ref[:, index * block : (index + 1) * block] = jnp.broadcast_to(row, (8, block))
        for start in range(0, block, TILE):
            at = slice(index * block + start, index * block + start + TILE)
            yield at, ref[start : start + TILE, :]


def turn(array):
    return array.astype(F32).T.astype(BF16)


def near_kernel(
    core_ref,
    mine_ref,
    other_ref,
    gain_ref,
    bias_ref,
    bq_ref,
    bv_ref,
    weight_hbm,
    code_ref,
    normed_hbm,
    w_hbm,
    qt_hbm,
    kv_hbm,
    state_hbm,
    act,
    kx,
    qx,
    vt,
    normed_v,
    w_v,
    qt_v,
    kv_v,
    state,
    sems,
    *,
    heads,
):
    half = heads * HEAD_DIM
    acc, top, total = state.at[:half, :], state.at[half : half + 8, :], state.at[half + 8 :, :]
    first = pl.multiple_of(core_ref[0] * half, 128)
    loads = [
        begin(sems, i, weight_hbm.at[:, pl.ds(2 * i * half + first, half)], w_v.at[:, i * half : (i + 1) * half])
        for i in range(3)
    ]
    gain, bias = gain_ref[...].astype(F32), bias_ref[...].astype(F32)
    bq, bv = bq_ref[...].astype(F32), bv_ref[...].astype(F32)
    for at, tokens in load_tokens((mine_ref, other_ref), code_ref):
        normed = (centre(tokens.astype(F32))[0] * gain + bias).astype(BF16)
        normed_v[:, at] = turn(normed)
        for load in loads:
            load.wait()
        loads = []
        q = (mm(normed, w_v[:, :half]) + bq).astype(BF16).astype(F32) * attn_scale
        qt_v[:, at] = q.T.astype(BF16)
        kv_v[at, :half] = mm(normed, w_v[:, half : 2 * half]).astype(BF16)
        v = (mm(normed, w_v[:, 2 * half :]) + bv).astype(BF16)
        kv_v[at, half:] = v
        vt[:, at] = turn(v)
    pairs = ((normed_v, normed_hbm), (w_v, w_hbm), (qt_v, qt_hbm), (kv_v, kv_hbm))
    stores = [begin(sems, 3 + i, source, target) for i, (source, target) in enumerate(pairs)]
    code = code_ref[0:1, :]
    note_tiles(code, code, act)
    load_queries(qt_v, code, qx, heads)
    load_keys(kv_v, 0, code, kx, heads)
    top[...] = jnp.full_like(top, -1e29)
    total[...] = jnp.zeros_like(total)
    acc[...] = jnp.zeros_like(acc)
    fold_keys(act, kx, qx, vt, top, total, acc, heads)
    stores.append(begin(sems, 7, state, state_hbm))
    for store in stores:
        store.wait()


def forward_near(core, mine, other, gain, bias, qkv_weight, qv_bias):
    padded, width = mine.shape
    half = width // 2
    heads = half // HEAD_DIM
    rows = 2 * (padded - 16)
    specs = [VMEM] * 4 + [
        pl.BlockSpec((1, half), lambda i, c: (0, c[0])),
        pl.BlockSpec((1, half), lambda i, c: (0, 2 + c[0])),
        HBM,
    ]
    kept = (((width, rows), BF16), ((width, 3 * half), BF16), ((half, rows), BF16), ((rows, width), BF16))
    kept += (((half + 16, rows), F32),)
    outs = (((8, rows), F32),) + kept
    scratch = [
        pltpu.SMEM((rows // TILE, rows // TILE), jnp.int32),
        pltpu.VMEM((heads, rows, 128), BF16),
        pltpu.VMEM((heads, 128, rows), BF16),
        pltpu.VMEM((half, rows), BF16),
    ]
    scratch += [pltpu.VMEM(shape, kind) for shape, kind in kept] + [pltpu.SemaphoreType.DMA((8,))]
    run = call(
        partial(near_kernel, heads=heads),
        "near_forward",
        outs,
        scratch,
        specs,
        (VMEM,) + (HBM,) * 5,
        prefetch=1,
        hold=(True,) * 6,
    )
    return run(core, mine, other, gain, bias, qv_bias, qv_bias, qkv_weight)


def far_kernel(
    far_ref,
    other_ref,
    gain_ref,
    bias_ref,
    bv_ref,
    w_hbm,
    qt_hbm,
    state_hbm,
    code_hbm,
    far_code_ref,
    lse_ref,
    o_ref,
    normed_hbm,
    kv_hbm,
    ot_hbm,
    act,
    kx,
    qx,
    vt,
    state,
    code_ref,
    w_v,
    qt_v,
    normed_v,
    kv_v,
    ot_v,
    sems,
    *,
    heads,
):
    half = heads * HEAD_DIM
    acc, top, total = state.at[:half, :], state.at[half : half + 8, :], state.at[half + 8 :, :]
    pairs = ((w_hbm.at[:, half:], w_v), (qt_hbm, qt_v), (state_hbm, state), (code_hbm, code_ref))
    loads = [begin(sems, i, source, target) for i, (source, target) in enumerate(pairs)]
    gain, bias = gain_ref[...].astype(F32), bias_ref[...].astype(F32)
    bv = bv_ref[...].astype(F32)
    for at, tokens in load_tokens((far_ref, other_ref), far_code_ref):
        normed = (centre(tokens.astype(F32))[0] * gain + bias).astype(BF16)
        normed_v[:, at] = turn(normed)
        for load in loads:
            load.wait()
        loads = []
        kv_v[at, :half] = mm(normed, w_v[:, :half]).astype(BF16)
        v = (mm(normed, w_v[:, half:]) + bv).astype(BF16)
        kv_v[at, half:] = v
        vt[:, at] = turn(v)
    stores = [begin(sems, 4, normed_v, normed_hbm), begin(sems, 5, kv_v, kv_hbm)]
    code, far_code = code_ref[0:1, :], far_code_ref[0:1, :]
    note_tiles(code, far_code, act)
    load_queries(qt_v, code, qx, heads)
    load_keys(kv_v, 0, far_code, kx, heads)
    fold_keys(act, kx, qx, vt, top, total, acc, heads)
    lse_ref[...] = top[...] + jnp.log(jnp.maximum(total[...], 1e-30))
    for h in range(heads):
        acc[rows_of(h), :] = acc[rows_of(h), :] / total[h : h + 1, :]
    ot_v[...] = acc[...].astype(BF16)
    stores.append(begin(sems, 6, ot_v, ot_hbm))
    for pair in range(heads // 2):
        o_ref[:, lanes_of(pair)] = acc[lanes_of(pair), :].T.astype(BF16)
    for store in stores:
        store.wait()


def forward_far(far, other, gain, bias, w, qv_bias, qt, code, state):
    padded, width = far.shape
    half = width // 2
    heads = half // HEAD_DIM
    rows = 2 * (padded - 16)
    specs = [VMEM] * 5 + [HBM] * 4
    kept = (((width, rows), BF16), ((rows, width), BF16), ((half, rows), BF16))
    outs = (((8, rows), F32), ((8, rows), F32), ((rows, half), BF16)) + kept
    scratch = [
        pltpu.SMEM((rows // TILE, rows // TILE), jnp.int32),
        pltpu.VMEM((heads, rows, 128), BF16),
        pltpu.VMEM((heads, 128, rows), BF16),
        pltpu.VMEM((half, rows), BF16),
        pltpu.VMEM((half + 16, rows), F32),
        pltpu.VMEM((8, rows), F32),
        pltpu.VMEM((width, width), BF16),
        pltpu.VMEM((half, rows), BF16),
    ]
    scratch += [pltpu.VMEM(shape, kind) for shape, kind in kept] + [pltpu.SemaphoreType.DMA((7,))]
    run = call(partial(far_kernel, heads=heads), "far_forward", outs, scratch, specs, (VMEM,) * 3 + (HBM,) * 3, hold=(True,) * 6)
    return run(far, other, gain, bias, qv_bias, w, qt, state, code)


def back_tiles(act, kx, qx, kt, dox, delta, qt_ref, kv_ref, do, lse, dq_sum, dk_sum, dv_sum, heads, group):
    half = heads * HEAD_DIM

    def body(at, span):
        for first in range(0, heads, group):
            hs = range(first, first + group)
            scores = {h: mm(kx[h, span, :], qx[h, :, at]) for h in hs}
            dp = {h: mm(kv_ref[span, half + (h // 2) * 128 : half + (h // 2 + 1) * 128], dox[h, :, at]) for h in hs}
            probs = {h: jnp.exp(scores[h] - lse(h, at)) for h in hs}
            rounded = {h: probs[h].astype(BF16) for h in hs}
            ds = {h: (probs[h] * (dp[h] - delta[h : h + 1, at])).astype(BF16) for h in hs}
            dv = {h: mm(do(h, at), rounded[h], NT) for h in hs}
            dk = {h: mm(qt_ref[rows_of(h), at], ds[h], NT) for h in hs}
            dq = {h: mm(kt[rows_of(h), span], ds[h]) for h in hs}
            for h in hs:
                dv_sum[rows_of(h), span] += dv[h]
                dk_sum[rows_of(h), span] += dk[h]
                dq_sum[rows_of(h), at] += dq[h]

    each_tile(act, qx.shape[2], kx.shape[1], body)


def back_ready(act, kx, qx, kt, dox, delta, qt_ref, kv_ref, ot_ref, do, q_code, k_code, heads):
    queries = qt_ref.shape[1]
    note_tiles(q_code, k_code, act)
    load_queries(qt_ref, q_code, qx, heads)
    load_keys(kv_ref, 0, k_code, kx, heads)
    zero = jnp.zeros((HEAD_DIM, queries), BF16)
    for h in range(heads):
        own = slice(0, HEAD_DIM) if h % 2 == 0 else slice(HEAD_DIM, 128)
        rest = slice(HEAD_DIM, 128) if h % 2 == 0 else slice(0, HEAD_DIM)
        grad = do(h, slice(0, queries))
        dox[h, own, :] = grad
        dox[h, rest, :] = zero
        delta[h : h + 1, :] = jnp.sum(grad.astype(F32) * ot_ref[rows_of(h), :].astype(F32), 0, keepdims=True)
    for pair in range(heads // 2):
        kt[lanes_of(pair), :] = turn(kv_ref[:, lanes_of(pair)])


def back_scratch(heads, queries, keys):
    half = heads * HEAD_DIM
    return [
        pltpu.SMEM((queries // TILE, keys // TILE), jnp.int32),
        pltpu.VMEM((heads, keys, 128), BF16),
        pltpu.VMEM((heads, 128, queries), BF16),
        pltpu.VMEM((half, keys), BF16),
        pltpu.VMEM((heads, 128, queries), BF16),
        pltpu.VMEM((8, queries), F32),
        pltpu.VMEM((half, queries), BF16),
        pltpu.VMEM((keys, 2 * half), BF16),
        pltpu.VMEM((half, queries), BF16),
        pltpu.VMEM((half, keys), F32),
        pltpu.VMEM((half, keys), F32),
    ]


def far_back_kernel(
    core_ref,
    flags_ref,
    gain_ref,
    q_code_hbm,
    k_code_hbm,
    lse_hbm,
    part_hbm,
    got_hbm,
    early_hbm,
    middle_hbm,
    cot_mine_hbm,
    cot_other_hbm,
    w_proj_hbm,
    qt_hbm,
    kv_hbm,
    ot_hbm,
    w_hbm,
    dx_ref,
    send_ref,
    sums_hbm,
    small_hbm,
    do_hbm,
    grad_half_hbm,
    grad_middle_hbm,
    dq_hbm,
    out_hbm,
    act,
    kx,
    qx,
    kt,
    dox,
    delta,
    qt_ref,
    kv_ref,
    ot_ref,
    dk_sum,
    dv_sum,
    w_ref,
    dq_sum,
    out_ref,
    middle_v,
    cot_v,
    w_proj_v,
    do_v,
    grad_half_v,
    grad_middle_v,
    sums_v,
    small_v,
    q_code_ref,
    k_code_ref,
    lse_ref,
    part_ref,
    got_ref,
    early_ref,
    sems,
    *,
    heads,
    images,
):
    half = heads * HEAD_DIM
    rows = middle_v.shape[0]
    block = rows // 2
    pairs = (
        (middle_hbm, middle_v),
        (part_hbm, part_ref),
        (got_hbm, got_ref),
        (cot_mine_hbm, cot_v.at[:block, :]),
        (cot_other_hbm, cot_v.at[block:, :]),
        (early_hbm, early_ref),
        (q_code_hbm, q_code_ref),
        (w_proj_hbm.at[pl.ds(pl.multiple_of(core_ref[0] * half, 128), half), :], w_proj_v),
        (qt_hbm, qt_ref),
        (kv_hbm, kv_ref),
        (ot_hbm, ot_ref),
        (k_code_hbm, k_code_ref),
        (lse_hbm, lse_ref),
        (w_hbm.at[:, half:], w_ref),
    )
    loads = [begin(sems, i, source, target) for i, (source, target) in enumerate(pairs)]
    for load in loads[:8]:
        load.wait()
    gain = gain_ref[...].astype(F32)
    total = jnp.zeros((1, 2 * half), F32)
    for at, swapped in row_tiles(rows):
        keep_attn = keep_column(q_code_ref.at[:, at], flags_ref, 0, images)
        unit, scale = centre(middle_v[at, :])
        grad = (part_ref[at, :].astype(F32) + got_ref[swapped, :].astype(F32)) * gain
        grad_middle = cot_v[at, :].astype(F32) + norm_back(unit, scale, grad)
        grad_proj = (keep_attn * grad_middle).astype(BF16)
        grad_half_v[at, :] = jnp.where(core_ref[0] == 0, grad_proj[:, :half], grad_proj[:, half:])
        do_v[:, at] = mm(w_proj_v[...], grad_proj, NT).astype(BF16)
        if at.start < block:
            grad_middle_v[at, :] = grad_middle
            total = total + jnp.sum(grad_proj.astype(F32), 0, keepdims=True)
    small_v[...] = early_ref[...] + jnp.where(lane_of(small_v.shape) == 4, upright(total), 0.0)
    kept = ((do_v, do_hbm), (grad_half_v, grad_half_hbm), (grad_middle_v, grad_middle_hbm), (small_v, small_hbm))
    stores = [begin(sems, 14 + i, source, target) for i, (source, target) in enumerate(kept)]
    for load in loads[8:]:
        load.wait()

    def do(h, at):
        return do_v[rows_of(h), at]

    def lse(h, at):
        return lse_ref[h : h + 1, at]

    q_code, k_code = q_code_ref[0:1, :], k_code_ref[0:1, :]
    back_ready(act, kx, qx, kt, dox, delta, qt_ref, kv_ref, ot_ref, do, q_code, k_code, heads)
    dq_sum[...] = jnp.zeros_like(dq_sum)
    dk_sum[...] = jnp.zeros_like(dk_sum)
    dv_sum[...] = jnp.zeros_like(dv_sum)
    back_tiles(act, kx, qx, kt, dox, delta, qt_ref, kv_ref, do, lse, dq_sum, dk_sum, dv_sum, heads, 3)
    stores.append(begin(sems, 18, dq_sum, dq_hbm))
    out_ref[:half, :] = dk_sum[...].astype(BF16)
    out_ref[half:, :] = dv_sum[...].astype(BF16)
    stores.append(begin(sems, 19, out_ref, out_hbm))
    send_ref[...] = mm(w_ref[...], out_ref[:, block:]).astype(BF16)
    dx_ref[...] = mm(w_ref[...], out_ref[:, :block])
    sums_v[...] = jnp.broadcast_to(jnp.sum(out_ref[...].astype(F32), 1, keepdims=True), sums_v.shape)
    stores.append(begin(sems, 20, sums_v, sums_hbm))
    for store in stores:
        store.wait()


def far_back(after, core, flags, q_code, k_code, lse, part, got, gain, early, held):
    half, queries = held[4].shape
    keys = held[5].shape[0]
    heads = half // HEAD_DIM
    width = 2 * half
    kept = (
        ((half, queries), BF16),
        ((queries, half), BF16),
        ((queries // 2, width), F32),
    )
    column = ((width, 128), F32)
    dq, grad = ((half, queries), F32), ((width, keys), BF16)
    outs = (((width, keys // 2), F32), ((width, keys // 2), BF16), column, column) + kept + (dq, grad)
    scratch = back_scratch(heads, queries, keys) + [
        pltpu.VMEM((width, width), BF16),
        pltpu.VMEM(*dq),
        pltpu.VMEM(*grad),
        pltpu.VMEM((queries, width), F32),
        pltpu.VMEM((queries, width), BF16),
        pltpu.VMEM((half, width), BF16),
        *[pltpu.VMEM(*shape) for shape in kept],
        pltpu.VMEM(*column),
        pltpu.VMEM(*column),
        *[pltpu.VMEM(array.shape, array.dtype) for array in (q_code, k_code, lse, part, got, early)],
        pltpu.SemaphoreType.DMA((21,)),
    ]
    specs = [SMEM, VMEM] + [HBM] * 14
    out_specs = (VMEM,) * 2 + (HBM,) * 7
    kernel = partial(far_back_kernel, heads=heads, images=flags.shape[1])
    run = call(kernel, "far_backward", outs, scratch, specs, out_specs, prefetch=1, after=after)
    return run(core, flags, gain, q_code, k_code, lse, part, got, early, *held)


def near_back_kernel(*refs, first, heads, unit, last):
    bits_ref, code_ref, lse_ref, do_ref, far_sums_ref, gain_ref, bias_ref, early_ref = refs[:8]
    if last:
        q_done_ref, v_done_ref, qt_hbm, kv_hbm, ot_hbm, dq_hbm, w_hbm, near_hbm, far_hbm, grad_hbm, done_hbm = refs[8:19]
        send_ref, send_part, keep_part, dx_hbm = refs[19:23]
        rest = refs[23:]
    else:
        qt_hbm, kv_hbm, ot_hbm, dq_hbm, w_hbm, near_hbm, far_hbm, grad_hbm, got_hbm, grad_half_hbm = refs[8:18]
        send_part, keep_part, small_ref, q_done_ref, v_done_ref, done_hbm = refs[18:24]
        rest = refs[24:]
    act, kx, qx, kt, dox, delta, qt_ref, kv_ref, ot_ref, dk_sum, dv_sum = rest[:11]
    dq_sum, out_ref, near_v, far_v, grad_v, w_ref, sems = rest[11:18]
    part = heads * HEAD_DIM
    half = do_ref.shape[0]
    low = first * HEAD_DIM
    mine = slice(low, low + part)
    block = kv_ref.shape[0] // 2
    pairs = [
        (qt_hbm.at[mine, :], qt_ref),
        (kv_hbm.at[:, mine], kv_ref.at[:, :part]),
        (kv_hbm.at[:, half + low : half + low + part], kv_ref.at[:, part:]),
    ]
    if last:
        done_v, dx_v, small_v = rest[18:]
        pairs += [(ot_hbm.at[mine, :], ot_ref), (dq_hbm.at[mine, :], dq_sum), (done_hbm, done_v)]
        other = part
        own_at = w_ref.shape[1] - 3 * part
        for i in range(3):
            pairs.append((w_hbm.at[:, i * half : i * half + low], w_ref.at[:, i * low : (i + 1) * low]))
    else:
        got_v, grad_half_v, whole_ot = rest[18:]
        pairs += [(ot_hbm, whole_ot), (dq_hbm.at[mine, :], dq_sum), (got_hbm, got_v), (grad_half_hbm, grad_half_v)]
        own_at = 0
        ot_ref = whole_ot
    for i in range(3):
        target = w_ref.at[:, own_at + i * part : own_at + (i + 1) * part]
        pairs.append((w_hbm.at[:, i * half + low : i * half + low + part], target))
    for i in range(2):
        pairs.append((grad_hbm.at[i * half + low : i * half + low + part, :], grad_v.at[i * part : (i + 1) * part, :]))
    pairs += [(near_hbm, near_v), (far_hbm, far_v)]
    loads = [begin(sems, i, source, target) for i, (source, target) in enumerate(pairs)]
    for load in loads[:5]:
        load.wait()

    def do(h, at):
        return do_ref[low + h * HEAD_DIM : low + (h + 1) * HEAD_DIM, at]

    def lse(h, at):
        return lse_ref[first + h : first + h + 1, at]

    code = code_ref[0:1, :]
    back_ready(act, kx, qx, kt, dox, delta, qt_ref, kv_ref, ot_ref, do, code, code, heads)
    dk_sum[...] = jnp.zeros_like(dk_sum)
    dv_sum[...] = jnp.zeros_like(dv_sum)
    back_tiles(act, kx, qx, kt, dox, delta, qt_ref, kv_ref, do, lse, dq_sum, dk_sum, dv_sum, heads, 4 if heads % 4 == 0 else 2)
    out_ref[:part, :] = (dq_sum[...] * attn_scale).astype(BF16)
    out_ref[part : 2 * part, :] = dk_sum[...].astype(BF16)
    out_ref[2 * part :, :] = dv_sum[...].astype(BF16)
    for load in loads[5:]:
        load.wait()
    core = bits_ref[2]
    far_sums = [far_sums_ref[i * half + low : i * half + low + part, :] for i in range(2)]
    sums = jnp.broadcast_to(jnp.sum(out_ref[...].astype(F32), 1, keepdims=True), (3 * part, 128))
    sums = jnp.concatenate([sums[:part], sums[part : 2 * part] + far_sums[0], sums[2 * part :] + far_sums[1]], 0)
    q_column, v_column = sums[:part], sums[2 * part :]
    sums = sums.T[:1]
    if last:
        for start in (block, 0):
            both = mm(w_ref[:, :own_at], done_v[:, start : start + block])
            both = both + mm(w_ref[:, own_at:], out_ref[:, start : start + block])
            if start:
                send_ref[...] = both.astype(BF16)
            else:
                dx_v[...] = both
        stores = [begin(sems, len(pairs), dx_v, dx_hbm)]
        small_v[...] = early_ref[...]
        lane = lane_of((half // 2, 128))
        q_whole = jnp.concatenate([q_done_ref[...], q_column], 0)
        v_whole = jnp.concatenate([v_done_ref[...], v_column], 0)
        for base, column in ((0, q_whole), (half, v_whole)):
            rows = pl.ds(pl.multiple_of(base + core * (half // 2), 8), half // 2)
            for j, piece in enumerate(interleaved(column, unit, 2)):
                small_v[rows, :] += jnp.where(lane == 10 + j, piece, 0.0)
    else:
        stores = [begin(sems, len(pairs), out_ref, done_hbm)]
        q_done_ref[...] = q_column
        v_done_ref[...] = v_column
    gain, bias = gain_ref[...].astype(F32), bias_ref[...].astype(F32)
    for step in range(2 * half // ROW_STEP):
        at = slice(step * ROW_STEP, (step + 1) * ROW_STEP)
        out = mm(near_v[at, :], out_ref[...], NT)
        out = jnp.concatenate([out[:, :part], out[:, part:] + mm(far_v[at, :], grad_v[...], NT)], 1)
        columns = ln_columns(out, w_ref[at, own_at:].astype(F32), sums, gain[:, at], bias[:, at], 0)
        if last:
            deal_part(bits_ref[0], jnp.concatenate([out, small_v[at, :] + columns], 1), send_part, keep_part, step)
            continue
        small_ref[at, :] = early_ref[at, :] + columns

        def join(proj):
            deal_part(bits_ref[1], jnp.concatenate([out, proj], 1), send_part, keep_part, step)

        early, late = grad_half_v[:block, :], grad_half_v[block:, :]

        @pl.when(core == step)
        def _():
            join(mm(whole_ot[:, :block], early) + mm(whole_ot[:, block:], late))

        @pl.when(core != step)
        def _():
            join(mm(got_v[:block, :], late, TN) + mm(got_v[block:, :], early, TN))

    for store in stores:
        store.wait()


def near_back(after, unit, first, last, bits, small, held):
    code, lse, do, far_sums, gain, bias, early = small[:7]
    qt, kv, w = held[0], held[1], held[4]
    half, queries = qt.shape
    keys, width = kv.shape
    heads = half // HEAD_DIM - first if last else 4
    part = heads * HEAD_DIM
    grad = ((3 * part, keys), BF16)
    dx = ((width, keys // 2), F32)
    if last:
        outs = (((width, keys // 2), BF16), *dealt(width, 2 * unit, 3 * part + 128)[0], dx)
        hold = (False, False, False, True)
    else:
        column = ((part, 128), F32)
        outs = (*dealt(width, 4 * unit, 3 * part + half)[0], ((width, 128), F32), column, column, grad)
        hold = (False, False, True, True, True, True)
    scratch = back_scratch(heads, queries, keys) + [
        pltpu.VMEM((part, queries), F32),
        pltpu.VMEM(*grad),
        pltpu.VMEM((width, queries), BF16),
        pltpu.VMEM((width, queries), BF16),
        pltpu.VMEM((2 * part, keys), BF16),
        pltpu.VMEM((width, 3 * half if last else 3 * part), BF16),
        pltpu.SemaphoreType.DMA((17,)),
    ]
    if last:
        scratch += [pltpu.VMEM(held[-1].shape, BF16), pltpu.VMEM(*dx), pltpu.VMEM((width, 128), F32)]
    else:
        scratch += [pltpu.VMEM(held[-2].shape, BF16), pltpu.VMEM(held[-1].shape, BF16), pltpu.VMEM((half, queries), BF16)]
    specs = [VMEM] * len(small) + [HBM] * len(held)
    out_specs = (VMEM,) * (len(outs) - 1) + (HBM,)
    kernel = partial(near_back_kernel, first=first, heads=heads, unit=unit, last=last)
    name = "near_backward_last" if last else "near_backward_first"
    run = call(kernel, name, outs, scratch, specs, out_specs, prefetch=1, after=after, hold=hold)
    return run(bits, *small, *held)


def keep_column(code_ref, flags_ref, branch, images):
    code = jnp.minimum(code_ref[0:1, :], float(PAD_CLASS - 1))
    kept = jnp.zeros_like(code)
    for image in range(images):
        kept = kept + jnp.where(code == image, flags_ref[branch, image].astype(F32), 0.0)
    return jnp.broadcast_to(kept / keep_rate, (128, code.shape[1])).T[:, :1]


def gelu_both(hidden):
    size = jnp.abs(hidden)
    bell = jnp.exp(-0.5 * hidden * hidden)
    t = 1.0 / (1.0 + 0.23164189 * size)
    tail = ((((0.5307027145 * t - 0.7265760135) * t + 0.7107068705) * t - 0.142248368) * t + 0.127414796) * t * bell
    cdf = jnp.where(hidden >= 0, 1.0 - tail, tail)
    return hidden * cdf, cdf + hidden * (bell * 0.3989422804014327)


def row_tiles(rows):
    for start in range(0, rows, TILE):
        other = (start + rows // 2) % rows
        yield slice(start, start + TILE), slice(other, other + TILE)


def mlp_kernel(
    bits_ref,
    flags_ref,
    b_proj_ref,
    gain_ref,
    bias_ref,
    b_up_ref,
    code_hbm,
    own_hbm,
    got_hbm,
    mine_hbm,
    other_hbm,
    cot_mine_hbm,
    cot_other_hbm,
    w_proj_hbm,
    w_up_hbm,
    w_down_hbm,
    part_ref,
    down_other_ref,
    small_ref,
    send_down_hbm,
    keep_down_hbm,
    send_up_hbm,
    keep_up_hbm,
    middle_hbm,
    down_hbm,
    send_down,
    keep_down,
    send_up,
    keep_up,
    x_v,
    cot_v,
    w_proj_v,
    w_up_v,
    w_down_v,
    middle_v,
    normed_v,
    grad_down_v,
    active_v,
    grad_hidden_v,
    down_v,
    up_sums_v,
    code_ref,
    own_ref,
    got_ref,
    sems,
    *,
    images,
    unit,
):
    core = bits_ref[2]
    rows, width = x_v.shape
    block, half, units = rows // 2, width // 2, w_up_v.shape[1]
    mine_at, other_at = pl.multiple_of(core * half, 128), pl.multiple_of((1 - core) * half, 128)
    units_at = pl.multiple_of(core * units, 128)
    pairs = (
        (w_proj_hbm.at[pl.ds(mine_at, half), :], w_proj_v.at[:half, :]),
        (w_proj_hbm.at[pl.ds(other_at, half), :], w_proj_v.at[half:, :]),
        (mine_hbm, x_v.at[:block, :]),
        (other_hbm.at[:block, :], x_v.at[block:, :]),
        (cot_mine_hbm, cot_v.at[:block, :]),
        (cot_other_hbm, cot_v.at[block:, :]),
        (code_hbm, code_ref),
        (own_hbm, own_ref),
        (got_hbm, got_ref),
        (w_up_hbm.at[:, pl.ds(units_at, units)], w_up_v),
        (w_down_hbm.at[pl.ds(units_at, units), :], w_down_v),
    )
    loads = [begin(sems, i, source, target) for i, (source, target) in enumerate(pairs)]
    for load in loads[:9]:
        load.wait()
    gain, bias, b_proj = gain_ref[...].astype(F32), bias_ref[...].astype(F32), b_proj_ref[...].astype(F32)
    down_sums = jnp.zeros((1, width), F32)
    for at, swapped in row_tiles(rows):
        keep_attn = keep_column(code_ref.at[:, at], flags_ref, 0, images)
        keep_mlp = keep_column(code_ref.at[:, at], flags_ref, 1, images)
        branch = mm(own_ref[at, :], w_proj_v[:half, :]) + mm(got_ref[swapped, :], w_proj_v[half:, :]) + b_proj
        middle = x_v[at, :].astype(F32) + keep_attn * branch
        middle_v[at, :] = middle
        normed_v[at, :] = (centre(middle)[0] * gain + bias).astype(BF16)
        grad_down = (keep_mlp * cot_v[at, :].astype(F32)).astype(BF16)
        grad_down_v[at, :] = grad_down
        if at.start < block:
            down_sums = down_sums + jnp.sum(grad_down.astype(F32), 0, keepdims=True)
    stores = [begin(sems, 11, middle_v, middle_hbm)]
    for load in loads[9:]:
        load.wait()
    up_sums_v[...] = jnp.zeros_like(up_sums_v)
    chunk = 512

    def tile(index, carry):
        at = pl.ds(pl.multiple_of(index * TILE, TILE), TILE)
        for start in range(0, units, chunk):
            cols = slice(start, start + chunk)
            hidden = mm(normed_v[at, :], w_up_v[:, cols]) + b_up_ref[:, cols].astype(F32)
            active, slope = gelu_both(hidden)
            active_v[at, cols] = active.astype(BF16)
            grad_hidden = (mm(grad_down_v[at, :], w_down_v[cols, :], NT) * slope).astype(BF16)
            grad_hidden_v[at, cols] = grad_hidden
            up_sums_v[:, cols] += jnp.sum(grad_hidden.astype(F32), 0, keepdims=True)
        return carry

    lax.fori_loop(0, rows // TILE, tile, 0)
    for step in range(units // ROW_STEP):
        at = slice(step * ROW_STEP, (step + 1) * ROW_STEP)
        deal_part(bits_ref[0], mm(active_v[:, at], grad_down_v[...], TN), send_down, keep_down, step)
    stores += [begin(sems, 13, send_down, send_down_hbm), begin(sems, 14, keep_down, keep_down_hbm)]
    for at, _ in row_tiles(rows):
        down = mm(active_v[at, :], w_down_v[...]).astype(BF16)
        if at.start < block:
            down_v[at, :] = down
        else:
            down_other_ref[at.start - block : at.stop - block, :] = down
    stores.append(begin(sems, 12, down_v, down_hbm))
    for step in range(width // ROW_STEP):
        at = slice(step * ROW_STEP, (step + 1) * ROW_STEP)
        out = mm(normed_v[:, at], grad_hidden_v[...], TN)
        deal_part(bits_ref[1], out, send_up, keep_up, step)
        columns = ln_columns(out, w_up_v[at, :].astype(F32), up_sums_v[...], gain[:, at], bias[:, at], 2)
        small_ref[at, :] = columns + jnp.where(lane_of(columns.shape) == 5, upright(down_sums[:, at]), 0.0)
    stores += [begin(sems, 15, send_up, send_up_hbm), begin(sems, 16, keep_up, keep_up_hbm)]
    for at, _ in row_tiles(rows):
        part_ref[at, :] = mm(grad_hidden_v[at, :], w_up_v[...], NT).astype(BF16)
    lane = lane_of((half, 128))
    own = pl.ds(pl.multiple_of(core * half, 8), half)
    for j, column in enumerate(interleaved(upright(up_sums_v[...]), unit, units // half)):
        small_ref[own, :] += jnp.where(lane == 6 + j, column, 0.0)
    for store in stores:
        store.wait()


def mlp(unit, bits, flags, b_proj, gain, bias, b_up, code, own, got, mine, other, cot_mine, cot_other, w_proj, w_up, w_down):
    rows, half = own.shape
    width, units = 2 * half, w_up.shape[1] // 2
    specs = [SMEM] + [VMEM] * 3 + [pl.BlockSpec((1, units), lambda i, b: (0, b[2]))] + [HBM] * 10
    wide, tall = ((rows, width), BF16), ((rows, units), BF16)
    block = ((rows // 2, width), BF16)
    parts = [*dealt(units, 2 * units // (width // unit // 2), width)[0], *dealt(width, 4 * unit, units)[0]]
    outs = (wide, block, ((width, 128), F32), *parts, ((rows, width), F32), block)
    scratch = [pltpu.VMEM(*shape) for shape in parts] + [
        pltpu.VMEM(*wide),
        pltpu.VMEM(*wide),
        pltpu.VMEM((width, width), BF16),
        pltpu.VMEM((width, units), BF16),
        pltpu.VMEM((units, width), BF16),
        pltpu.VMEM((rows, width), F32),
        pltpu.VMEM(*wide),
        pltpu.VMEM(*wide),
        pltpu.VMEM(*tall),
        pltpu.VMEM(*tall),
        pltpu.VMEM(*block),
        pltpu.VMEM((1, units), F32),
        pltpu.VMEM(code.shape, F32),
        pltpu.VMEM((rows, half), BF16),
        pltpu.VMEM((rows, half), BF16),
        pltpu.SemaphoreType.DMA((17,)),
    ]
    out_specs = (VMEM,) * 3 + (HBM,) * 6
    hold = (True,) * 9
    kernel = partial(mlp_kernel, images=flags.shape[1], unit=unit)
    run = call(kernel, "mlp", outs, scratch, specs, out_specs, prefetch=1, hold=hold)
    return run(
        bits, flags, b_proj, gain, bias, b_up, code, own, got, mine, other, cot_mine, cot_other, w_proj, w_up, w_down
    )


def deal(bit, rows, send_ref, keep_ref):
    run = send_ref.shape[1]
    for i in range(send_ref.shape[0]):
        low, high = rows[2 * i * run : (2 * i + 1) * run], rows[(2 * i + 1) * run : (2 * i + 2) * run]
        send_ref[i] = jnp.where(bit == 0, high, low).astype(BF16)
        keep_ref[i] = jnp.where(bit == 0, low, high).astype(BF16)


def deal_part(bit, rows, send_ref, keep_ref, step):
    count = rows.shape[0] // (2 * send_ref.shape[1])
    part = pl.ds(step * count, count)
    deal(bit, rows, send_ref.at[part], keep_ref.at[part])


def dealt(height, run, width):
    shape = (height // (2 * run), run, width)
    count = ROW_STEP // (2 * run)
    return [(shape, BF16)] * 2, [pl.BlockSpec((count, run, width), lambda i, *_: (i, 0, 0))] * 2


def upright(row):
    return jnp.broadcast_to(row, (128, row.shape[1])).T


def lane_of(shape):
    return lax.broadcasted_iota(jnp.int32, shape, 1)


def interleaved(column, unit, parts):
    blocks = column.shape[0] // (unit * parts)
    out = []
    for j in range(parts):
        pieces = [column[(k * parts + j) * unit : (k * parts + j + 1) * unit] for k in range(blocks)]
        out.append(jnp.concatenate(pieces, 0))
    return out


def ln_columns(grad, weight, sums, gain_ref, bias_ref, place):
    first = jnp.sum(weight * grad, 1, keepdims=True)
    second = jnp.sum(weight * sums, 1, keepdims=True)
    lane = lane_of((weight.shape[0], 128))
    scaled = (first - upright(bias_ref) * second) / upright(gain_ref)
    return jnp.where(lane == place, scaled, jnp.where(lane == place + 1, second, 0.0))


def add_kernel(left_ref, right_ref, out_ref):
    out_ref[...] = (left_ref[...].astype(F32) + right_ref[...].astype(F32)).astype(out_ref.dtype)


def add(after, left, right):
    run = call(add_kernel, "add_blocks", ((left.shape, BF16),), [], [VMEM, VMEM], after=after)
    return run(left, right)[0]


def sides(core_ref, kept, other):
    return jnp.where(core_ref[0] == 0, kept, other), jnp.where(core_ref[0] == 0, other, kept)


def join_up_kernel(core_ref, kept_ref, other_ref, down_ref, out_ref, down_out_ref):
    units = kept_ref.shape[1]
    down_out_ref[...] = down_ref[...].astype(F32)
    out_ref[:, :units], out_ref[:, units:] = sides(core_ref, kept_ref[...], other_ref[...])


def join_up(after, core, kept, other, down):
    rows, units = kept.shape
    outs = (((rows, 2 * units), F32), (down.shape, F32))
    return call(join_up_kernel, "join_up", outs, [], [VMEM] * 3, prefetch=1, after=after)(core, kept, other, down)


def join_kernel(core_ref, two_ref, two_other_ref, one_ref, one_other_ref, qkv_ref, proj_ref, *refs):
    rows, half = two_ref.shape[0], proj_ref.shape[1] // 2
    pad = refs[-1]
    big = (two_ref.shape[1] - half) // 3
    small = half - big
    twos = sides(core_ref, two_ref[...], two_other_ref[...])
    ones = sides(core_ref, one_ref[...], one_other_ref[...])
    for core, (two, one) in enumerate(zip(twos, ones)):
        proj_ref[:, core * half : (core + 1) * half] = two[:, 3 * big :]
        for i in range(3):
            at = 2 * i * half + core * half
            qkv_ref[:, at : at + big] = two[:, i * big : (i + 1) * big]
            qkv_ref[:, at + big : at + half] = one[:, i * small : (i + 1) * small]
    pad[...] = jnp.zeros_like(pad)
    pad[:rows, :] = one_ref[:, 3 * small :] + one_other_ref[:, 3 * small :]
    turned = pad[...].T
    lane = 0
    for ref in refs[:-1]:
        count = ref.shape[1] // rows
        ref[...] = jnp.concatenate([turned[lane + i : lane + i + 1, :rows] for i in range(count)], 1)
        lane += count


def join_all(after, core, two, two_other, one, one_other, half):
    rows = two.shape[0]
    outs = [((rows, 6 * half), F32), ((rows, 2 * half), F32)] + [((1, count * rows), F32) for count in (1, 1, 1, 1, 1, 1, 4, 2)]
    scratch = [pltpu.VMEM((128, 128), F32)]
    run = call(join_kernel, "join_all", outs, scratch, [VMEM] * 4, prefetch=1, after=after)
    return run(core, two, two_other, one, one_other)


def finish_kernel(x_ref, dx_ref, beside_ref, across_ref, gain_ref, middle_ref, out_ref):
    unit, scale = centre(x_ref[...].astype(F32))
    grad = (dx_ref[...] + beside_ref[...].astype(F32) + across_ref[...].astype(F32)).T
    out_ref[...] = (middle_ref[...] + norm_back(unit, scale, grad * gain_ref[...].astype(F32))).astype(BF16)


def finish(after, x, dx, beside, across, gain, middle):
    rows, width = x.shape
    tile = pl.BlockSpec((TILE, width), lambda i: (i, 0))
    one = pl.BlockSpec((1, width), lambda i: (0, 0))
    turned = pl.BlockSpec((width, TILE), lambda i: (0, i))
    specs = [tile, turned, turned, turned, one, tile]
    run = call(finish_kernel, "token_gradient", ((x.shape, BF16),), [], specs, (tile,), (rows // TILE,), after=after)
    return run(x, dx, beside, across, gain, middle)[0]


def output_kernel(flags_ref, code_ref, middle_ref, down_ref, got_ref, bias_ref, out_ref, *, images):
    kept = keep_column(code_ref, flags_ref, 1, images)
    branch = down_ref[...].astype(F32) + got_ref[...].astype(F32) + bias_ref[...].astype(F32)
    out_ref[...] = (middle_ref[...] + kept * branch).astype(BF16)


def layer_out(after, flags, code, middle, down, got, bias):
    rows, width = got.shape
    tile = pl.BlockSpec((TILE, width), lambda i: (i, 0))
    one = pl.BlockSpec((1, width), lambda i: (0, 0))
    specs = [SMEM, pl.BlockSpec((8, TILE), lambda i: (0, i)), tile, tile, tile, one]
    kernel = partial(output_kernel, images=flags.shape[1])
    run = call(kernel, "layer_output", ((got.shape, BF16),), [], specs, (tile,), (rows // TILE,), after=after)
    return run(flags, code, middle, down, got, bias)[0]


def swap_halves(rows):
    half = rows.shape[0] // 2
    return jnp.concatenate([rows[half:], rows[:half]], 0)


def pick(array, index, dim):
    return lax.dynamic_index_in_dim(array, index, dim, keepdims=False)


class Links:
    def __init__(self, mesh):
        self.dp, self.blk = mesh.shape["dp"], mesh.shape["blk"]
        self.bits = self.dp.bit_length() - 1

    def core(self, value):
        return lax.ppermute(value, "blk", [(i, i ^ 1) for i in range(self.blk)])

    def side(self, value):
        return lax.ppermute(value, "blk", [(i, i ^ 2) for i in range(self.blk)])

    def cross(self, value, step):
        if step == "x":
            return self.side(value)
        return lax.ppermute(value, "dp", [(i, i ^ (1 << step)) for i in range(self.dp)])

    def bit(self, step):
        if step == "x":
            return lax.axis_index("blk") // 2
        return (lax.axis_index("dp") >> step) & 1

    def swap(self, value):
        top = self.dp // 2
        pairs = []
        for d in range(self.dp):
            for b in range(self.blk):
                high, core = d // top, b % 2
                pairs.append((d * self.blk + b, (d % top + core * top) * self.blk + (b - core + high)))
        return lax.ppermute(value, ("dp", "blk"), pairs)


class Portion:
    def __init__(self, links, send, keep, dims, order, by_core=True):
        self.links, self.order, self.by_core = links, list(order), by_core
        self.dims = [dim for dim in dims if dim != order[0]]
        self.tail = (send.shape[0] * send.shape[1] // 2 ** len(self.dims), send.shape[2])
        self.kept = keep
        self.arrived = links.cross(send, order[0])

    def advance(self, after):
        links = self.links
        self.order.pop(0)
        if not self.order:
            kept, arrived = self.kept.reshape(self.tail), self.arrived.reshape(self.tail)
            if not self.by_core:
                self.total = call(add_kernel, "sum_last", ((self.tail, F32),), [], [VMEM] * 2, after=after)(kept, arrived)[0]
                return self.total
            half = self.tail[0] // 2

            def last_kernel(core_ref, kept_ref, arrived_ref, send_ref, keep_ref):
                total = kept_ref[...].astype(F32) + arrived_ref[...].astype(F32)
                send_ref[...] = jnp.where(core_ref[0] == 0, total[half:], total[:half])
                keep_ref[...] = jnp.where(core_ref[0] == 0, total[:half], total[half:])

            shape = (half, self.tail[1])
            core = (lax.axis_index("blk") % 2).reshape(1).astype(jnp.int32)
            run = call(last_kernel, "sum_last", ((shape, F32), (shape, F32)), [], [VMEM] * 2, prefetch=1, after=after)
            send, self.total = run(core, kept, arrived)
            self.other = links.core(send)
            return self.total
        follow = self.order[0]
        spot = self.dims.index(follow)
        self.dims.pop(spot)
        outer, inner = 2**spot, 2 ** (len(self.dims) - spot)
        shape = (outer, inner) + self.tail
        view = (outer, 2, inner) + self.tail

        def kernel(bit_ref, kept_ref, arrived_ref, send_ref, keep_ref):
            for out_ref, where in ((send_ref, 1 - bit_ref[0]), (keep_ref, bit_ref[0])):
                out_ref[...] = (kept_ref[:, where].astype(F32) + arrived_ref[:, where].astype(F32)).astype(BF16)

        run = call(kernel, "sum_half", ((shape, BF16), (shape, BF16)), [], [VMEM] * 2, prefetch=1, after=after)
        send, keep = run(links.bit(follow).reshape(1).astype(jnp.int32), self.kept.reshape(view), self.arrived.reshape(view))
        self.kept = keep
        self.arrived = links.cross(send, follow)
        return keep


def merged(links, down, up, after):
    count, rb, width = 2 ** len(down.dims), down.tail[0], down.tail[1]
    double, units = up.tail
    high = count // 2
    top = high // 2

    def kernel(bit_ref, down_ref, down_got_ref, up_ref, up_got_ref, send_ref, keep_ref):
        for out_ref, where in ((send_ref, 1 - bit_ref[0]), (keep_ref, bit_ref[0])):
            for i in range(high):
                at = ((i % top) * 2 + where) * 2 + i // top
                out_ref[i, :rb] = (down_ref[at].astype(F32) + down_got_ref[at].astype(F32)).astype(BF16)
                total = (up_ref[2 * i + where].astype(F32) + up_got_ref[2 * i + where].astype(F32)).astype(BF16)
                for part in range(units // width):
                    start = rb + part * double
                    out_ref[i, start : start + double] = total[:, part * width : (part + 1) * width]

    shape = (high, rb + double * (units // width), width)
    bit = links.bit(1).reshape(1).astype(jnp.int32)
    run = call(kernel, "sum_both", ((shape, BF16), (shape, BF16)), [], [VMEM] * 4, prefetch=1, after=after)
    fold = (count, rb, width), (count, double, units)
    return run(
        bit, down.kept.reshape(fold[0]), down.arrived.reshape(fold[0]), up.kept.reshape(fold[1]), up.arrived.reshape(fold[1])
    )


def parted(after, core, kept, arrived, rb, unit, units):
    width = kept.shape[1]

    def kernel(core_ref, kept_ref, arrived_ref, down_ref, send_ref, keep_ref):
        total = kept_ref[...].astype(F32) + arrived_ref[...].astype(F32)
        down_ref[...] = total[:rb].astype(BF16)
        for part in range(units // width):
            start = rb + part * 2 * unit
            low, high = total[start : start + unit], total[start + unit : start + 2 * unit]
            cols = slice(part * width, (part + 1) * width)
            send_ref[:, cols] = jnp.where(core_ref[0] == 0, high, low)
            keep_ref[:, cols] = jnp.where(core_ref[0] == 0, low, high)

    outs = (((rb, width), BF16), ((unit, units), F32), ((unit, units), F32))
    return call(kernel, "part_both", outs, [], [VMEM] * 2, prefetch=1, after=after)(core, kept, arrived)


def local(
    links,
    tokens,
    cotangent,
    segments,
    padding,
    drop_keep,
    ln1_gain,
    ln1_bias,
    qkv_weight,
    qv_bias,
    proj_weight,
    proj_bias,
    ln2_gain,
    ln2_bias,
    fc1_weight,
    fc1_bias,
    fc2_weight,
    fc2_bias,
):
    _, block, width = tokens.shape
    half = width // 2
    units = fc1_weight.shape[1] // 2
    core = lax.axis_index("blk") % 2
    core_arg = core.reshape(1).astype(jnp.int32)
    owners = links.dp * links.blk
    rows = 2 * block

    code = jnp.where(padding == 1, segments, PAD_CLASS).astype(BF16)
    mine = jnp.concatenate([tokens[0], jnp.pad(code, ((0, 15), (0, width - block)))], 0)
    far = links.side(mine)
    other = links.core(mine)
    cot_mine = cotangent[0]
    cot_other = links.core(cot_mine)
    flags = drop_keep[:, 0, :]
    bits = links.bits
    low = [bits - 1 - i for i in range(bits)]
    chip = low + ["x"]
    by_core = low[1:] + ["x", low[0]]
    tail = [s for s in low if s > 1][::-1]
    side_bits = jnp.stack([links.bit("x"), links.bit(0), core, links.bit(1)]).astype(jnp.int32)
    unit = width // owners

    gain_one, bias_one = ln1_gain.reshape(1, -1), ln1_bias.reshape(1, -1)
    gain_two, bias_two = ln2_gain.reshape(1, -1), ln2_bias.reshape(1, -1)
    bias_qv = qv_bias.reshape(1, -1)
    near_code, near_normed, w_qkv, qt, near_kv, state = forward_near(
        core_arg, mine, other, gain_one, bias_one, qkv_weight, bias_qv
    )
    far = lax.dynamic_update_slice(far, near_code[:, :128].astype(BF16), (block + 8, 0))
    far_other = links.core(far)
    bias_v = lax.dynamic_slice(bias_qv, (0, width + core * half), (1, half))
    far_code, lse, own, far_normed, far_kv, ot = forward_far(
        far, far_other, gain_one, bias_one, w_qkv, bias_v, qt, near_code, state
    )
    got = links.core(own)
    part, down_send, small, send_down, keep_down, send_up, keep_up, middle, down = mlp(
        unit,
        side_bits,
        flags,
        proj_bias.reshape(1, -1),
        gain_two,
        bias_two,
        fc1_bias.reshape(1, -1),
        near_code,
        own,
        got,
        tokens[0],
        other,
        cot_mine,
        cot_other,
        proj_weight,
        fc1_weight,
        fc2_weight,
    )
    got_part = links.core(part)
    down_portion = Portion(links, send_down, keep_down, by_core, ["x", 0, 1] + tail, False)
    up_portion = Portion(links, send_up, keep_up, chip, [0, "x", 1] + tail)
    down_other = links.core(down_send)
    held = (middle, cot_mine, cot_other, proj_weight, qt, far_kv, ot, w_qkv)
    far_dx, far_send, far_sums, small, do, grad_half, grad_middle, dq, far_grad = far_back(
        (), core_arg, flags, near_code, far_code, lse, part, got_part, gain_two, small, held
    )
    last = down_portion.advance((far_grad,))
    last = up_portion.advance((last,))
    far_got = links.core(far_send)
    ready = (near_code, lse, do, far_sums, gain_one, bias_one)
    held = (qt, near_kv, ot, dq, w_qkv, near_normed, far_normed, far_grad)
    send, keep, small, q_done, v_done, done = near_back(
        (last,), unit, 0, False, side_bits, ready + (small,), held + (got, grad_half)
    )
    two_portion = Portion(links, send, keep, chip, [0, 1, "x"] + tail)
    far_sum = add((keep,), far_dx, far_got)
    across = links.side(far_sum)
    send, keep = merged(links, down_portion, up_portion, (far_sum,))
    both_portion = Portion(links, send, keep, low[:-1], [1] + tail)
    near_send, send, keep, near_dx = near_back(
        (keep,), unit, 4, True, side_bits, ready + (small, q_done, v_done), held + (done,)
    )
    near_got = links.core(near_send)
    one_portion = Portion(links, send, keep, chip, ["x", 0, 1] + tail)
    last = both_portion.advance((keep,))
    last = two_portion.advance((last, across))
    layer_output = layer_out((last,), flags, near_code, middle, down, down_other, fc2_bias.reshape(1, -1))
    last = one_portion.advance((layer_output,))
    last = two_portion.advance((last,))
    for _ in tail[1:]:
        last = both_portion.advance((last,))
    last = one_portion.advance((last, both_portion.arrived))
    tokens_grad = finish((last,), tokens[0], near_dx, near_got, across, gain_one, grad_middle)
    last = two_portion.advance((tokens_grad,))
    last = one_portion.advance((last,))
    down_total, send, keep = parted(
        (last,),
        core_arg,
        both_portion.kept.reshape(both_portion.tail),
        both_portion.arrived.reshape(both_portion.tail),
        2 * units // owners,
        unit,
        units,
    )
    down_got = links.swap(down_total)
    up_got = links.core(send)
    last = down_total
    while two_portion.order:
        last = two_portion.advance((last,))
    while one_portion.order:
        last = one_portion.advance((last,))
    up_grad, down_grad = join_up((last,), core_arg, keep, up_got, down_got)
    qkv_grad, proj_grad, *vectors = join_all(
        (up_grad,), core_arg, two_portion.total, two_portion.other, one_portion.total, one_portion.other, half
    )
    g1, b1, g2, b2, pb, d2, u1, qvb = (vector.reshape(-1) for vector in vectors)
    shape = tokens.shape
    return (
        layer_output.reshape(shape),
        tokens_grad.reshape(shape),
        g1,
        b1,
        qkv_grad,
        qvb,
        proj_grad,
        pb,
        g2,
        b2,
        up_grad,
        u1,
        down_grad,
        d2,
    )


def solution(mesh):
    both = P(("dp", "blk"))
    rows = P(("dp", "blk"), None)
    token = P("dp", "blk", None)
    placed = (token, token, P("dp", "blk"), P("dp", "blk"), P(None, "dp", None)) + (P(),) * 12
    return jax.shard_map(
        partial(local, Links(mesh)),
        mesh=mesh,
        in_specs=placed,
        out_specs=(token, token, both, both, rows, both, rows, both, both, both, rows, both, rows, both),
        check_vma=False,
    )
```
